32 devices in a mesh: dp: 2 (over x), expert: 16 (over z, y, core).
Axes of the slice: x: 2, y: 2, z: 4, core: 2. Of those that a mesh axis runs over, the one named last changes fastest.
Arguments:
- tokens: bfloat16 [128, 4096], P(('dp', 'expert')), may hold values from -6 to 6
- expert_ids: int32 [128, 8], P(('dp', 'expert')), may hold values from 0 to 15, all different within a row; in each aligned block of 4 rows (0 to 3, 4 to 7, ...) at most 4 rows name the same one
- gate_probs: float32 [128, 8], P(('dp', 'expert')), may hold values from 0.2 to 1
- w_gate: bfloat16 [16, 4096, 2048], P('expert', None, 'dp'), may hold values from -0.09375 to 0.09375
- w_up: bfloat16 [16, 4096, 2048], P('expert', None, 'dp'), may hold values from -0.09375 to 0.09375
- w_down: bfloat16 [16, 2048, 4096], P('expert', None, 'dp'), may hold values from -0.125 to 0.125
Outputs:
- combined: bfloat16 [128, 4096], P(('dp', 'expert'))
The draws below stay inside these ranges and needn't reach their ends.
Inputs may be any that keep to these rules, and one draw needn't show every extreme that they name: `expert_ids`: each row names 8 different experts. In the rows of one device (aligned blocks of 4 rows) no expert is named by more than 4 rows, a bound that some block reaches.
All inputs are finite; a program needn't handle non-finite values.
Results may differ from the reference program's by a relative error of at most 0.0057.
Values may be sent and summed in bfloat16 or wider, within the bound.
No kernel may reach another device: no remote copies, remote signals or barrier semaphores. Data moves between devices by JAX's collectives and lax.ppermute only.
A program may use at most 64 MiB of HBM per device.

```python
import math
import jax
import jax.numpy as jnp
import numpy as np
from jax import lax

D = 4096
HID = 2048
TOP = 8
TOK_DEV = 4
EXPERTS = 16
TOKENS = 128
CAP = 4
SLOTS = 128


def block_scale(rng, extent, cuts, smallest, high):
    loudness = 1.0
    for dim, shards_of in cuts:
        steps = jax.random.uniform(jax.random.fold_in(jax.random.fold_in(rng, 6), dim), (shards_of,), jnp.float32, smallest / len(cuts), high / len(cuts))
        loudness = loudness * jnp.repeat(jnp.exp(steps), extent[dim] // shards_of).reshape((-1,) + (1,) * (len(extent) - 1 - dim))
    return loudness


def shared_out(stream_key, own, number, rows, count, top, limit, skew):
    ranking = jax.random.permutation(stream_key, count)
    heavy_load, ordinary = portions_of(count, rows * top, limit, skew, True), portions_of(count, rows * top, limit, skew, False)
    places = jnp.arange(count)

    def named(sizes, offset_by):
        used = int((sizes > 0).sum())
        fixed = max(1, used // 4)
        passed = fixed + (places - fixed + offset_by * (used - fixed)) % max(1, count - fixed)
        return jnp.zeros((count,), jnp.int32).at[ranking[jnp.where(places < fixed, places, passed)]].set(jnp.asarray(sizes, jnp.int32))

    sizes = jnp.where(number % 4 == 0, named(heavy_load, number // 4), named(ordinary, number - number // 4 - 1))
    mixed = jax.random.permutation(jax.random.fold_in(own, 3), count)
    source_of, taker = mixed[0:count // 2 * 2:2], mixed[1:count // 2 * 2:2]
    room = jnp.minimum(sizes[source_of] - 1, limit - sizes[taker]) // 2
    room = jnp.where((source_of == ranking[0]) | (taker == ranking[0]) | (sizes[taker] == 0), 0, jnp.maximum(room, 0))
    passed = jax.random.randint(jax.random.fold_in(own, 4), (count // 2,), 0, 1 << 20) % (room + 1)
    sizes = sizes.at[source_of].add(-passed).at[taker].add(passed)
    members = jnp.searchsorted(jnp.cumsum(sizes), jnp.arange(rows * top), side="right").astype(jnp.int32)
    grid = members.reshape(top, rows).T
    grid = grid[jax.random.permutation(jax.random.fold_in(own, 1), rows)]
    offset_by = jax.random.randint(jax.random.fold_in(own, 2), (rows, 1), 0, top)
    return jnp.take_along_axis(grid, (jnp.arange(top)[None, :] + offset_by) % top, axis=1)


def portions_of(amount, total, most, slope, full):
    weights = [(1 << 20) // math.isqrt(grade ** slope) + 1 for grade in range(1, amount + 1)]
    largest = most if full else min(most, max(-(-total // amount), total * weights[0] // sum(weights)))
    least = 1 if total - largest >= amount - 1 else 0
    holding, surplus = [largest] + [least] * (amount - 1), total - largest - least * (amount - 1)
    while surplus > 0:
        free = [i for i in range(1, amount) if holding[i] < largest] or [i for i in range(1, amount) if holding[i] < most]
        mass, remaining = sum([weights[i] for i in free]), surplus
        for i in free:
            more = min(most - holding[i], max(1, remaining * weights[i] // mass), surplus)
            holding[i] = holding[i] + more
            surplus = surplus - more
    return np.array(holding)


def scatter_about(key, extent, deviation, most, shards=(), kind=jnp.bfloat16):
    drawn = jax.random.normal(key, extent, jnp.float32) * deviation
    if len(shards) > 0:
        drawn = block_scale(key, extent, shards, -0.22, 0.18) * drawn
    return jnp.clip(drawn, min=-most, max=most).astype(kind)


def setup_inputs(seed: int = 0) -> dict:
    streams_of = jax.random.split(jax.random.key(seed), 7)
    tokens = scatter_about(streams_of[0], (TOKENS, D), 1.0, 6.0, ((0, 32),))
    expert_ids_keys = jax.random.split(jax.random.fold_in(streams_of[1], 1), TOKENS // TOK_DEV)
    expert_ids_turns = jax.random.permutation(jax.random.fold_in(streams_of[1], 3), TOKENS // TOK_DEV)
    expert_ids = jax.vmap(lambda own, number: shared_out(jax.random.fold_in(streams_of[1], 2), own, number, TOK_DEV, EXPERTS, TOP, CAP, 2))(expert_ids_keys, expert_ids_turns).reshape((TOKENS, TOP))
    gate_probs = jnp.clip(0.2 + 0.8 * jax.random.uniform(streams_of[2], (TOKENS, TOP), jnp.float32) ** block_scale(streams_of[2], (TOKENS, TOP), ((0, 32),), -0.2, 0.2), 0.2, 1.0)
    w_gate = scatter_about(streams_of[3], (EXPERTS, D, HID), D ** -0.5, 0.09375, ((0, 16), (2, 2)))
    w_up = scatter_about(streams_of[4], (EXPERTS, D, HID), D ** -0.5, 0.09375, ((0, 16), (2, 2)))
    w_down = scatter_about(streams_of[5], (EXPERTS, HID, D), HID ** -0.5, 0.125, ((0, 16), (2, 2)))
    return {"tokens": tokens, "expert_ids": expert_ids, "gate_probs": gate_probs, "w_gate": w_gate, "w_up": w_up, "w_down": w_down}


def expand_rows(gathered, gate_matrix, up_matrix):
    gate_proj = jnp.dot(gathered, gate_matrix, preferred_element_type=jnp.float32)
    up_proj = jnp.dot(gathered, up_matrix, preferred_element_type=jnp.float32)
    return (jax.nn.silu(gate_proj) * up_proj).astype(jnp.bfloat16)


def reference(tokens, expert_ids, gate_probs, w_gate, w_up, w_down):
    flat_ids = expert_ids.reshape(-1).astype(jnp.int32)
    flat_gates = gate_probs.reshape(-1)
    owners = (jnp.arange(flat_ids.shape[0], dtype=jnp.int32) // TOP).astype(jnp.int32)

    def one_expert(expert_index, running):
        matches = flat_ids == expert_index
        picked = jnp.nonzero(matches, size=SLOTS, fill_value=0)[0].astype(jnp.int32)
        present = jnp.arange(SLOTS, dtype=jnp.int32) < jnp.sum(matches.astype(jnp.int32))
        targets = owners[picked]
        gathered = tokens[targets]
        hidden = expand_rows(gathered, w_gate[expert_index], w_up[expert_index])
        result = jnp.dot(hidden, w_down[expert_index], preferred_element_type=jnp.float32).astype(jnp.bfloat16)
        result = lax.optimization_barrier(result).astype(flat_gates.dtype)
        scales = jnp.where(present, flat_gates[picked], jnp.zeros((), flat_gates.dtype))
        return running.at[targets].add(result * scales[:, None])

    combined = lax.fori_loop(0, EXPERTS, one_expert, jnp.zeros((TOKENS, D), jnp.float32))
    return combined.astype(jnp.bfloat16)
```

```python
import jax
import jax.numpy as jnp
from jax import lax
from jax.sharding import PartitionSpec as P


def swap(value, axis, mask):
    size = lax.axis_size(axis)
    return lax.ppermute(value, axis, [(i, i ^ mask) for i in range(size)])


def spread(value, axis, masks):
    return jnp.concatenate([value[None]] + [swap(value, axis, m)[None] for m in masks])


def gate_table(expert_ids, gate_probs, experts):
    hit = expert_ids[:, :, None] == jnp.arange(experts, dtype=jnp.int32)
    table = jnp.sum(jnp.where(hit, gate_probs[:, :, None], 0.0), axis=1)
    parts = []
    for _ in range(3):
        part = lax.reduce_precision(table, 8, 7)
        parts.append(part.astype(jnp.bfloat16))
        table = table - part
    return jnp.concatenate(parts, axis=1)


def gather_rows(block, high_masks, group_masks):
    rows, width = block.shape
    near = spread(block, "expert", high_masks)
    near = near.reshape(-1, width)
    if group_masks:
        near = spread(near, "dp", group_masks).reshape(-1, width)
    over_x = swap(near, "dp", 1)
    over_y = swap(near, "expert", 2)
    half = near.shape[0] // 2
    corner = jnp.concatenate([swap(over_y[:half], "dp", 1), swap(over_x[half:], "expert", 2)])
    chip = jnp.concatenate([near, over_y, over_x, corner])
    return jnp.concatenate([chip, swap(chip, "expert", 1)])


def local(tokens, expert_ids, gate_probs, w_gate, w_up, w_down):
    token_count, width = tokens.shape
    experts, groups = lax.axis_size("expert"), lax.axis_size("dp")
    me, group = lax.axis_index("expert"), lax.axis_index("dp")
    high_masks = list(range(4, experts, 4))
    group_masks = list(range(2, groups, 2))
    high, wide = len(high_masks) + 1, len(group_masks) + 1

    table = gate_table(expert_ids, gate_probs, experts)
    slots = -(-table.shape[1] // 128) * 128
    block = jnp.concatenate([tokens, jnp.pad(table, ((0, 0), (0, slots - table.shape[1])))], axis=1)
    everything = gather_rows(block, high_masks, group_masks)
    rows = everything[:, :width]
    mine = (jnp.arange(slots) % experts == me) & (jnp.arange(slots) < table.shape[1])
    scale = jnp.sum(jnp.where(mine, everything[:, width:].astype(jnp.float32), 0.0), axis=1)

    gate_proj = jnp.dot(rows, w_gate[0], preferred_element_type=jnp.float32)
    up_proj = jnp.dot(rows, w_up[0], preferred_element_type=jnp.float32)
    hidden = (jax.nn.silu(gate_proj) * up_proj).astype(jnp.bfloat16)

    units = hidden.shape[1]
    shape = (2, 2, 2, wide, high * token_count, units)
    down = w_down[0].reshape(groups, units, -1)
    total = jnp.zeros((rows.shape[0], down.shape[2]), jnp.float32)
    for mask in range(groups):
        part = hidden
        if mask:
            part = swap(hidden, "dp", mask).reshape(shape)
            x_order = [i ^ (mask & 1) for i in range(2)]
            wide_order = [i ^ (mask >> 1) for i in range(wide)]
            part = jnp.stack([part[:, i] for i in x_order], axis=1)
            part = jnp.stack([part[:, :, :, i] for i in wide_order], axis=3)
            part = part.reshape(hidden.shape)
        mine_down = lax.dynamic_index_in_dim(down, group ^ mask, 0, keepdims=False)
        total = total + jnp.dot(part, mine_down, preferred_element_type=jnp.float32)

    total = (total * scale[:, None]).reshape(2, 2, 2, wide, high, token_count, -1)
    send = lambda value, axis, mask: swap(value.astype(jnp.bfloat16), axis, mask).astype(jnp.float32)
    total = total[0] + send(total[1], "expert", 1)
    total = total[:, 0] + send(total[:, 1], "expert", 2)
    kept = total[:, :, 0]
    for slot, mask in enumerate(high_masks, 1):
        kept = kept + send(total[:, :, slot], "expert", mask)
    kept = kept.astype(jnp.bfloat16)
    pieces = []
    for mask in range(groups):
        piece = kept[mask & 1, mask >> 1]
        pieces.append(swap(piece, "dp", mask) if mask else piece)
    pieces = jnp.stack(pieces)
    order = jnp.arange(groups) ^ group
    if groups == 2:
        pieces = jnp.where(group == 0, pieces, pieces[::-1])
    else:
        pieces = jnp.take(pieces, order, axis=0)
    return pieces.transpose(1, 0, 2).reshape(token_count, width)


def solution(mesh):
    placed = (
        P(("dp", "expert"), None),
        P(("dp", "expert"), None),
        P(("dp", "expert"), None),
        P("expert", None, "dp"),
        P("expert", None, "dp"),
        P("expert", None, "dp"),
    )
    return jax.shard_map(
        local, mesh=mesh, in_specs=placed, out_specs=P(("dp", "expert"), None), check_vma=False
    )
```

```python
import jax
import jax.numpy as jnp
from jax import lax
from jax.experimental import pallas as pl
from jax.experimental.pallas import tpu as pltpu
from jax.sharding import PartitionSpec as P


CHUNKS = 2


def swap(value, axis, mask):
    size = lax.axis_size(axis)
    return lax.ppermute(value, axis, [(i, i ^ mask) for i in range(size)])


def spread(value, axis, masks):
    return jnp.concatenate([value[None]] + [swap(value, axis, m)[None] for m in masks])


def fetch(weights, after, cuts, name):
    weights, _ = lax.optimization_barrier((weights, after))
    weights = pltpu.with_memory_space_constraint(weights, pltpu.HBM)

    def body(rows_from, source, *rest):
        pieces, arrived = rest[:-1], rest[-1]
        copies = []
        for i, (_, rows, column, columns) in enumerate(cuts):
            start = pl.multiple_of(rows_from[i], 128)
            part = source.at[pl.ds(start, rows), pl.ds(column, columns)]
            copies.append(pltpu.make_async_copy(part, pieces[i], arrived.at[i]))
        for copy in copies:
            copy.start()
        for copy in copies:
            copy.wait()

    size = sum(rows * columns for _, rows, _, columns in cuts) * weights.dtype.itemsize
    return pl.pallas_call(
        body,
        out_shape=[pltpu.VMEM((rows, columns), weights.dtype) for _, rows, _, columns in cuts],
        in_specs=[
            pl.BlockSpec(memory_space=pltpu.SMEM),
            pl.BlockSpec(memory_space=pltpu.HBM),
        ],
        out_specs=[pl.BlockSpec(memory_space=pltpu.VMEM)] * len(cuts),
        scratch_shapes=[pltpu.SemaphoreType.DMA((len(cuts),))],
        cost_estimate=pl.CostEstimate(flops=0, bytes_accessed=size, transcendentals=0),
        compiler_params=pltpu.CompilerParams(vmem_limit_bytes=1 << 20),
        name=name,
    )(jnp.stack([jnp.asarray(row, jnp.int32) for row, _, _, _ in cuts]), weights)


def gate_table(expert_ids, gate_probs, experts):
    hit = expert_ids[:, :, None] == jnp.arange(experts, dtype=jnp.int32)
    table = jnp.sum(jnp.where(hit, gate_probs[:, :, None], 0.0), axis=1)
    parts = []
    for _ in range(3):
        part = lax.reduce_precision(table, 8, 7)
        parts.append(part.astype(jnp.bfloat16))
        table = table - part
    return jnp.concatenate(parts, axis=1)


def gather_rows(block, high_masks, group_masks, fetches):
    rows, width = block.shape
    near = spread(block, "expert", high_masks)
    near = near.reshape(-1, width)
    if group_masks:
        near = spread(near, "dp", group_masks).reshape(-1, width)
    parts = [fetches[0](block)]
    near, parts[0] = lax.optimization_barrier((near, parts[0]))
    over_x = swap(near, "dp", 1)
    over_y = swap(near, "expert", 2)
    parts.append(fetches[1](near))
    over_x, over_y, parts[1] = lax.optimization_barrier((over_x, over_y, parts[1]))
    half = near.shape[0] // 2
    corner = jnp.concatenate([swap(over_y[:half], "dp", 1), swap(over_x[half:], "expert", 2)])
    parts.append(fetches[2](over_x))
    corner, parts[2] = lax.optimization_barrier((corner, parts[2]))
    chip = jnp.concatenate([near, over_y, over_x, corner])
    return jnp.concatenate([chip, swap(chip, "expert", 1)]), parts


def local(tokens, expert_ids, gate_probs, w_gate, w_up, w_down):
    token_count, width = tokens.shape
    experts, groups = lax.axis_size("expert"), lax.axis_size("dp")
    me, group = lax.axis_index("expert"), lax.axis_index("dp")
    high_masks = list(range(4, experts, 4))
    group_masks = list(range(2, groups, 2))
    high, wide = len(high_masks) + 1, len(group_masks) + 1

    table = gate_table(expert_ids, gate_probs, experts)
    slots = -(-table.shape[1] // 128) * 128
    block = jnp.concatenate([tokens, jnp.pad(table, ((0, 0), (0, slots - table.shape[1])))], axis=1)
    units = w_gate.shape[2]
    chunks = CHUNKS if units % (128 * CHUNKS) == 0 else 1
    step = units // chunks
    columns = [(0, width, i * step, step) for i in range(chunks)]
    down_rows = [
        ((group ^ mask) * units + i * step, step, 0, w_down.shape[2])
        for mask in range(groups)
        for i in range(chunks)
    ]
    fetches = (
        lambda after: fetch(w_gate[0], after, columns, "fetch_gate"),
        lambda after: fetch(w_up[0], after, columns, "fetch_up"),
        lambda after: fetch(w_down[0], after, down_rows, "fetch_down"),
    )
    everything, parts = gather_rows(block, high_masks, group_masks, fetches)
    gate_parts, up_parts, down_parts = parts
    rows = everything[:, :width]
    mine = (jnp.arange(slots) % experts == me) & (jnp.arange(slots) < table.shape[1])
    scale = jnp.sum(jnp.where(mine, everything[:, width:].astype(jnp.float32), 0.0), axis=1)

    shape = (2, 2, 2, wide, high * token_count, step)

    def from_group(value, mask):
        value = swap(value, "dp", mask).reshape(shape)
        value = jnp.stack([value[:, i ^ (mask & 1)] for i in range(2)], axis=1)
        value = jnp.stack([value[:, :, :, i ^ (mask >> 1)] for i in range(wide)], axis=3)
        return value.reshape(-1, step)

    own, others = [], [[] for _ in range(1, groups)]
    for gate_part, up_part in zip(gate_parts, up_parts):
        gate_proj = jnp.dot(rows, gate_part, preferred_element_type=jnp.float32)
        up_proj = jnp.dot(rows, up_part, preferred_element_type=jnp.float32)
        hidden = (jax.nn.silu(gate_proj) * up_proj).astype(jnp.bfloat16)
        own.append(hidden)
        for mask in range(1, groups):
            others[mask - 1].append(from_group(hidden, mask))
    total = jnp.zeros((rows.shape[0], w_down.shape[2]), jnp.float32)
    for part, down_part in zip(sum(others, own), down_parts):
        total = total + jnp.dot(part, down_part, preferred_element_type=jnp.float32)

    total = (total * scale[:, None]).reshape(2, 2, 2, wide, high, token_count, -1)
    send = lambda value, axis, mask: swap(value.astype(jnp.bfloat16), axis, mask).astype(jnp.float32)
    total = total[0] + send(total[1], "expert", 1)
    total = total[:, 0] + send(total[:, 1], "expert", 2)
    kept = total[:, :, 0]
    for slot, mask in enumerate(high_masks, 1):
        kept = kept + send(total[:, :, slot], "expert", mask)
    kept = kept.astype(jnp.bfloat16)
    pieces = []
    for mask in range(groups):
        piece = kept[mask & 1, mask >> 1]
        pieces.append(swap(piece, "dp", mask) if mask else piece)
    pieces = jnp.stack(pieces)
    order = jnp.arange(groups) ^ group
    if groups == 2:
        pieces = jnp.where(group == 0, pieces, pieces[::-1])
    else:
        pieces = jnp.take(pieces, order, axis=0)
    return pieces.transpose(1, 0, 2).reshape(token_count, width)


def solution(mesh):
    placed = (
        P(("dp", "expert"), None),
        P(("dp", "expert"), None),
        P(("dp", "expert"), None),
        P("expert", None, "dp"),
        P("expert", None, "dp"),
        P("expert", None, "dp"),
    )
    return jax.shard_map(
        local, mesh=mesh, in_specs=placed, out_specs=P(("dp", "expert"), None), check_vma=False
    )
```

```python
import jax
import jax.numpy as jnp
from jax import lax
from jax.experimental import pallas as pl
from jax.experimental.pallas import tpu as pltpu
from jax.sharding import Mesh
from jax.sharding import PartitionSpec as P

CHUNKS = 2
TILE = 256
BATCH = 128


def swap(value, axis, offset):
    size = lax.axis_size(axis)
    return lax.ppermute(value, axis, [((i + offset) % size, i) for i in range(size)])


def in_vmem(weights):
    return pltpu.with_memory_space_constraint(weights, pltpu.VMEM)


def row_batches(count, step):
    batch = min(BATCH, count)
    if count == batch:
        step(0, batch)
    else:

        @pl.loop(0, count // batch)
        def _(i):
            step(pl.multiple_of(i * batch, batch), batch)


def expand_rows(rows, w_gate, w_up, start, columns):
    count, depth = rows.shape[0], w_gate.shape[0]

    def body(rows_ref, gate_ref, up_ref, hidden_ref):
        def step(first, batch):
            x = rows_ref[pl.ds(first, batch), :depth]
            tile = min(TILE, columns)
            for i in range(0, columns, tile):
                cut = slice(start + i, start + i + tile)
                gate = jnp.dot(x, gate_ref[:, cut], preferred_element_type=jnp.float32)
                up = jnp.dot(x, up_ref[:, cut], preferred_element_type=jnp.float32)
                value = gate / (1.0 + jnp.exp(-gate)) * up
                hidden_ref[pl.ds(first, batch), i : i + tile] = value.astype(hidden_ref.dtype)

        row_batches(count, step)

    return pl.pallas_call(
        body,
        out_shape=jax.ShapeDtypeStruct((count, columns), rows.dtype),
        in_specs=[pl.BlockSpec(memory_space=pltpu.VMEM)] * 3,
        out_specs=pl.BlockSpec(memory_space=pltpu.VMEM),
        cost_estimate=pl.CostEstimate(flops=0, bytes_accessed=count * columns, transcendentals=0),
        compiler_params=pltpu.CompilerParams(vmem_limit_bytes=24 << 20),
        name="expand_rows",
    )(rows, w_gate, w_up)


def contract_hidden(parts, first_units, w_down, before=None, scale=None):
    count, width = parts[0].shape[0], w_down.shape[1]
    def body(first_ref, down_ref, *refs):
        parts_refs = refs[: len(parts)]

        def step(first, batch):
            here = pl.ds(first, batch)
            tile = min(2 * TILE, width)
            for i in range(0, width, tile):
                cut = slice(i, i + tile)
                total = 0.0 if before is None else refs[len(parts)][here, cut]
                for j, part in enumerate(parts_refs):
                    units = pl.ds(pl.multiple_of(first_ref[j], 128), part.shape[1])
                    total = total + jnp.dot(
                        part[here, :], down_ref[units, cut], preferred_element_type=jnp.float32
                    )
                if scale is not None:
                    total = total.astype(w_down.dtype).astype(jnp.float32)
                    total = total * refs[len(parts) + 1][here, :]
                refs[-1][here, cut] = total

        row_batches(count, step)

    extra = [value for value in (before, scale) if value is not None]
    return pl.pallas_call(
        body,
        out_shape=jax.ShapeDtypeStruct((count, width), jnp.float32),
        in_specs=[pl.BlockSpec(memory_space=pltpu.SMEM)]
        + [pl.BlockSpec(memory_space=pltpu.VMEM)] * (1 + len(parts) + len(extra)),
        out_specs=pl.BlockSpec(memory_space=pltpu.VMEM),
        cost_estimate=pl.CostEstimate(flops=0, bytes_accessed=count * width, transcendentals=0),
        compiler_params=pltpu.CompilerParams(vmem_limit_bytes=24 << 20),
        name="contract_hidden",
    )(jnp.stack(first_units), w_down, *parts, *extra)


def gate_table(expert_ids, gate_probs, experts):
    hit = expert_ids[:, :, None] == jnp.arange(experts, dtype=jnp.int32)
    table = jnp.sum(jnp.where(hit, gate_probs[:, :, None], 0.0), axis=1)
    parts = []
    for _ in range(3):
        part = lax.reduce_precision(table, 8, 7)
        parts.append(part.astype(jnp.bfloat16))
        table = table - part
    table = jnp.concatenate(parts, axis=1)
    return jnp.pad(table, ((0, 0), (0, -table.shape[1] % 128)))


def local(tokens, expert_ids, gate_probs, w_gate, w_up, w_down):
    token_count, width = tokens.shape
    groups, cores = lax.axis_size("dp"), lax.axis_size("core")
    experts = lax.axis_size("far") * cores
    me, group = lax.axis_index(("far", "core")), lax.axis_index("dp")
    w_gate, w_up, w_down = in_vmem(w_gate[0]), in_vmem(w_up[0]), in_vmem(w_down[0])

    table = gate_table(expert_ids, gate_probs, experts)
    block = jnp.concatenate([tokens, table], axis=1)
    rows = lax.all_gather(block, ("dp", "far"), axis=1, tiled=True)
    rows = rows.reshape(token_count, -1, block.shape[1]).transpose(1, 0, 2)
    rows = rows.reshape(-1, block.shape[1])
    rows = jnp.concatenate([rows] + [swap(rows, "core", i) for i in range(1, cores)])
    tables = rows[:, width:]
    slot = jnp.arange(table.shape[1])
    mine = (slot % experts == me) & (slot < 3 * experts)
    scale = jnp.sum(
        jnp.where(mine, tables.astype(jnp.float32), 0.0), axis=1, keepdims=True
    )

    units = w_gate.shape[1]
    chunks = CHUNKS if units % (128 * CHUNKS) == 0 else 1
    step = units // chunks
    total, others, other_units = None, [], []
    for i in range(chunks):
        if total is not None:
            rows, total = lax.optimization_barrier((rows, total))
        hidden = expand_rows(rows, w_gate, w_up, i * step, step)
        for offset in range(1, groups):
            others.append(swap(hidden, "dp", offset))
            other_units.append((group + offset) % groups * units + i * step)
        total = contract_hidden([hidden], [group * units + i * step], w_down, total)
    total = contract_hidden(others, other_units, w_down, total, scale)

    total = total.reshape(cores, -1, w_down.shape[1])
    kept = total[0]
    for i in range(1, cores):
        kept = kept + swap(total[cores - i].astype(jnp.bfloat16), "core", i).astype(jnp.float32)
    blocks = kept.astype(jnp.bfloat16).reshape(-1, token_count, w_down.shape[1])
    blocks = lax.all_to_all(blocks, ("dp", "far"), split_axis=0, concat_axis=0, tiled=True)
    blocks = blocks.reshape(groups, -1, token_count, w_down.shape[1]).astype(jnp.float32)
    combined = jnp.sum(blocks, axis=1).astype(jnp.bfloat16)
    return combined.transpose(1, 0, 2).reshape(token_count, width)


def solution(mesh):
    groups, experts = mesh.devices.shape
    split = Mesh(mesh.devices.reshape(groups, experts // 2, 2), ("dp", "far", "core"))
    row, expert = P(("dp", "far", "core"), None), P(("far", "core"), None, "dp")
    return jax.shard_map(
        local,
        mesh=split,
        in_specs=(row, row, row, expert, expert, expert),
        out_specs=row,
        check_vma=False,
    )
```

```python
import jax
import jax.numpy as jnp
from jax import lax
from jax.experimental import pallas as pl
from jax.experimental.pallas import tpu as pltpu
from jax.sharding import PartitionSpec as P

CHUNKS = 2
TILE = 256
BATCH = 128
COPIES = 8
LANES = 128


def swap(value, group_mask, expert_mask):
    groups, experts = lax.axis_size("dp"), lax.axis_size("expert")
    pairs = [
        (g * experts + e, (g ^ group_mask) * experts + (e ^ expert_mask))
        for g in range(groups)
        for e in range(experts)
    ]
    return lax.ppermute(value, ("dp", "expert"), pairs)


def row_batches(count, step):
    batch = min(BATCH, count)
    if count == batch:
        step(0, batch)
    else:

        @pl.loop(0, count // batch)
        def _(i):
            step(pl.multiple_of(i * batch, batch), batch)


def pack_block(tokens, expert_ids, gate_probs, experts):
    count, width = tokens.shape
    top = expert_ids.shape[1]

    def body(tokens_ref, ids_ref, probs_ref, block_ref):
        block_ref[:, :width] = tokens_ref[...]
        lane = lax.broadcasted_iota(jnp.int32, (count, LANES), 1)
        table = jnp.zeros((count, LANES), jnp.float32)
        for k in range(top):
            hit = ids_ref[:, k : k + 1] == lax.rem(lane, experts)
            table = jnp.where(hit, probs_ref[:, k : k + 1], table)
        packed = jnp.zeros((count, LANES), jnp.float32)
        for i in range(3):
            part = table.astype(jnp.bfloat16).astype(jnp.float32)
            packed = jnp.where(lane // experts == i, part, packed)
            table = table - part
        block_ref[:, width:] = packed.astype(block_ref.dtype)

    return pl.pallas_call(
        body,
        out_shape=jax.ShapeDtypeStruct((count, width + LANES), tokens.dtype),
        in_specs=[pl.BlockSpec(memory_space=pltpu.VMEM)] * 3,
        out_specs=pl.BlockSpec(memory_space=pltpu.VMEM),
        compiler_params=pltpu.CompilerParams(vmem_limit_bytes=1 << 20),
        name="pack_block",
    )(tokens, expert_ids, gate_probs)


def fetch(weights, after, name):
    weights, _ = lax.optimization_barrier((weights, after))
    weights = pltpu.with_memory_space_constraint(weights, pltpu.HBM)
    piece = weights.shape[0] // COPIES

    def body(source, target, arrived):
        copies = []
        for i in range(COPIES):
            part = pl.ds(i * piece, piece)
            copies.append(pltpu.make_async_copy(source.at[part], target.at[part], arrived.at[i]))
        for copy in copies:
            copy.start()
        for copy in copies:
            copy.wait()

    return pl.pallas_call(
        body,
        out_shape=pltpu.VMEM(weights.shape, weights.dtype),
        in_specs=[pl.BlockSpec(memory_space=pltpu.HBM)],
        out_specs=pl.BlockSpec(memory_space=pltpu.VMEM),
        scratch_shapes=[pltpu.SemaphoreType.DMA((COPIES,))],
        cost_estimate=pl.CostEstimate(flops=0, bytes_accessed=weights.nbytes, transcendentals=0),
        compiler_params=pltpu.CompilerParams(vmem_limit_bytes=1 << 20),
        name=name,
    )(weights)


def in_vmem(value):
    return pltpu.with_memory_space_constraint(value, pltpu.VMEM)


def expand_rows(rows, w_gate, w_up, start, columns):
    count, depth = rows.shape[0], w_gate.shape[0]

    def body(rows_ref, gate_ref, up_ref, hidden_ref):
        def step(first, batch):
            x = rows_ref[pl.ds(first, batch), :depth]
            tile = min(TILE, columns)
            for i in range(0, columns, tile):
                cut = slice(start + i, start + i + tile)
                gate = jnp.dot(x, gate_ref[:, cut], preferred_element_type=jnp.float32)
                up = jnp.dot(x, up_ref[:, cut], preferred_element_type=jnp.float32)
                value = gate / (1.0 + jnp.exp(-gate)) * up
                hidden_ref[pl.ds(first, batch), i : i + tile] = value.astype(hidden_ref.dtype)

        row_batches(count, step)

    return pl.pallas_call(
        body,
        out_shape=jax.ShapeDtypeStruct((count, columns), rows.dtype),
        in_specs=[pl.BlockSpec(memory_space=pltpu.VMEM)] * 3,
        out_specs=pl.BlockSpec(memory_space=pltpu.VMEM),
        cost_estimate=pl.CostEstimate(flops=0, bytes_accessed=count * columns, transcendentals=0),
        compiler_params=pltpu.CompilerParams(vmem_limit_bytes=rows.nbytes + (6 << 20)),
        name="expand_rows",
    )(rows, in_vmem(w_gate), in_vmem(w_up))


def contract_hidden(parts, first_units, w_down, before=None, scale=None):
    count, width = parts[0].shape[0], w_down.shape[1]

    def body(first_ref, down_ref, *refs):
        parts_refs = refs[: len(parts)]

        def step(first, batch):
            here = pl.ds(first, batch)
            tile = min(2 * TILE, width)
            for i in range(0, width, tile):
                cut = slice(i, i + tile)
                total = 0.0 if before is None else refs[len(parts)][here, cut]
                for j, part in enumerate(parts_refs):
                    units = pl.ds(pl.multiple_of(first_ref[j], 128), part.shape[1])
                    total = total + jnp.dot(
                        part[here, :], down_ref[units, cut], preferred_element_type=jnp.float32
                    )
                if scale is not None:
                    total = total.astype(w_down.dtype).astype(jnp.float32)
                    total = total * refs[len(parts) + 1][here, :]
                refs[-1][here, cut] = total

        row_batches(count, step)

    extra = [value for value in (before, scale) if value is not None]
    return pl.pallas_call(
        body,
        out_shape=jax.ShapeDtypeStruct((count, width), jnp.float32),
        in_specs=[pl.BlockSpec(memory_space=pltpu.SMEM)]
        + [pl.BlockSpec(memory_space=pltpu.VMEM)] * (1 + len(parts) + len(extra)),
        out_specs=pl.BlockSpec(memory_space=pltpu.VMEM),
        cost_estimate=pl.CostEstimate(flops=0, bytes_accessed=count * width, transcendentals=0),
        compiler_params=pltpu.CompilerParams(vmem_limit_bytes=8 * count * width + (6 << 20)),
        name="contract_hidden",
    )(jnp.stack(first_units), in_vmem(w_down), *parts, *extra)


def local(tokens, expert_ids, gate_probs, w_gate, w_up, w_down):
    token_count, width = tokens.shape
    groups, experts = lax.axis_size("dp"), lax.axis_size("expert")
    group, me = lax.axis_index("dp"), lax.axis_index("expert")
    wide, high = groups // 2, experts // 4

    block = pack_block(tokens, expert_ids, gate_probs, experts)
    near = jnp.stack([block] + [swap(block, 0, 4 * i) for i in range(1, high)])
    near = near.reshape(-1, block.shape[1])
    gate_weights = fetch(w_gate[0], block, "fetch_gate")
    near, gate_weights = lax.optimization_barrier((near, gate_weights))
    if wide > 1:
        near = jnp.concatenate([near] + [swap(near, 2 * i, 0) for i in range(1, wide)])
    chip = [near, swap(near, 0, 2), swap(near, 1, 0), swap(near, 1, 2)]
    up_weights = fetch(w_up[0], near, "fetch_up")
    down_weights = fetch(w_down[0], near, "fetch_down")
    chip[3], up_weights, down_weights = lax.optimization_barrier(
        (chip[3], up_weights, down_weights)
    )
    chip = jnp.concatenate(chip)
    rows = jnp.concatenate([chip, swap(chip, 0, 1)])
    lane = jnp.arange(LANES)
    mine = (lane % experts == me) & (lane < 3 * experts)
    scale = jnp.where(mine, rows[:, width:].astype(jnp.float32), 0.0)
    scale = jnp.sum(scale, axis=1, keepdims=True)

    units = gate_weights.shape[1]
    chunks = CHUNKS if units % (LANES * CHUNKS) == 0 else 1
    step = units // chunks

    def from_group(value, mask):
        value = swap(value, mask, 0).reshape(2, 2, 2, wide, high * token_count, step)
        if mask & 1:
            value = jnp.concatenate([value[:, 1:], value[:, :1]], axis=1)
        if mask > 1:
            value = jnp.stack([value[:, :, :, i ^ (mask >> 1)] for i in range(wide)], axis=3)
        return value.reshape(-1, step)

    total, others, other_units = None, [], []
    for i in range(chunks):
        if total is not None:
            rows, total = lax.optimization_barrier((rows, total))
        hidden = expand_rows(rows, gate_weights, up_weights, i * step, step)
        for mask in range(1, groups):
            others.append(from_group(hidden, mask))
            other_units.append((group ^ mask) * units + i * step)
        total = contract_hidden([hidden], [group * units + i * step], down_weights, total)
    total = contract_hidden(others, other_units, down_weights, total, scale)

    columns = total.shape[1]
    send = lambda value, g, e: swap(value.astype(jnp.bfloat16), g, e).astype(jnp.float32)
    total = total.reshape(2, -1, columns)
    total = total[0] + send(total[1], 0, 1)
    part = total.shape[0] // 4
    near, over_y, over_x, corner = (total[i * part : (i + 1) * part] for i in range(4))
    total = jnp.concatenate(
        [near + send(over_y, 0, 2), send(over_x, 1, 0) + send(corner, 1, 2)], axis=1
    )
    part = part // wide
    total = jnp.concatenate(
        [total[:part]]
        + [send(total[i * part : (i + 1) * part], 2 * i, 0) for i in range(1, wide)],
        axis=1,
    )
    combined = total[:token_count]
    for i in range(1, high):
        combined = combined + send(total[i * token_count : (i + 1) * token_count], 0, 4 * i)
    combined = combined.astype(jnp.bfloat16)
    if groups == 2:
        swapped = jnp.concatenate([combined[:, columns:], combined[:, :columns]], axis=1)
        return jnp.where(group == 0, combined, swapped)
    combined = combined.reshape(token_count, groups, columns)
    combined = jnp.take(combined, jnp.arange(groups) ^ group, axis=1)
    return combined.reshape(token_count, width)


def solution(mesh):
    row, expert = P(("dp", "expert"), None), P("expert", None, "dp")
    return jax.shard_map(
        local,
        mesh=mesh,
        in_specs=(row, row, row, expert, expert, expert),
        out_specs=row,
        check_vma=False,
    )
```

```python
import jax
import jax.numpy as jnp
from jax import lax
from jax.experimental import pallas as pl
from jax.experimental.pallas import tpu as pltpu
from jax.sharding import PartitionSpec as P

CHUNKS = 2
TILE = 256
BATCH = 128
COPIES = 8
LANES = 128


def swap(value, group_mask, expert_mask):
    groups, experts = lax.axis_size("dp"), lax.axis_size("expert")
    pairs = [
        (g * experts + e, (g ^ group_mask) * experts + (e ^ expert_mask))
        for g in range(groups)
        for e in range(experts)
    ]
    return lax.ppermute(value, ("dp", "expert"), pairs)


def in_vmem(value):
    return pltpu.with_memory_space_constraint(value, pltpu.VMEM)


def in_hbm(value):
    return pltpu.with_memory_space_constraint(value, pltpu.HBM)


def row_batches(count, step):
    batch = min(BATCH, count)
    if count == batch:
        step(0, batch)
    else:

        @pl.loop(0, count // batch)
        def _(i):
            step(pl.multiple_of(i * batch, batch), batch)


def pack_block(tokens, expert_ids, gate_probs, experts):
    count, width = tokens.shape
    top = expert_ids.shape[1]

    def body(tokens_ref, ids_ref, probs_ref, block_ref):
        block_ref[:, :width] = tokens_ref[...]
        lane = lax.broadcasted_iota(jnp.int32, (count, LANES), 1)
        table = jnp.zeros((count, LANES), jnp.float32)
        for k in range(top):
            hit = ids_ref[:, k : k + 1] == lax.rem(lane, experts)
            table = jnp.where(hit, probs_ref[:, k : k + 1], table)
        packed = jnp.zeros((count, LANES), jnp.float32)
        for i in range(3):
            part = table.astype(jnp.bfloat16).astype(jnp.float32)
            packed = jnp.where(lane // experts == i, part, packed)
            table = table - part
        block_ref[:, width:] = packed.astype(block_ref.dtype)

    return pl.pallas_call(
        body,
        out_shape=jax.ShapeDtypeStruct((count, width + LANES), tokens.dtype),
        in_specs=[pl.BlockSpec(memory_space=pltpu.VMEM)] * 3,
        out_specs=pl.BlockSpec(memory_space=pltpu.VMEM),
        compiler_params=pltpu.CompilerParams(vmem_limit_bytes=1 << 20),
        name="pack_block",
    )(in_hbm(tokens), in_hbm(expert_ids), in_hbm(gate_probs))


def stack_blocks(blocks):
    count, width = blocks[0].shape

    def body(*refs):
        values = [ref[...].astype(jnp.float32) for ref in refs[:-1]]
        refs[-1][...] = jnp.concatenate(values).astype(refs[-1].dtype)

    return pl.pallas_call(
        body,
        out_shape=jax.ShapeDtypeStruct((len(blocks) * count, width), blocks[0].dtype),
        in_specs=[pl.BlockSpec(memory_space=pltpu.VMEM)] * len(blocks),
        out_specs=pl.BlockSpec(memory_space=pltpu.VMEM),
        compiler_params=pltpu.CompilerParams(vmem_limit_bytes=4 << 20),
        name="stack_blocks",
    )(*blocks)


def fetch(weights, after, name, rows=None, part=None):
    weights, _ = lax.optimization_barrier((weights, after))
    rows = rows or weights.shape[0]
    piece = rows // COPIES
    size = rows * weights.shape[1] * weights.dtype.itemsize

    def body(source, target, arrived):
        first = 0 if part is None else (lax.axis_index("dp") ^ part) * rows
        copies = []
        for i in range(COPIES):
            here = pl.ds(pl.multiple_of(first + i * piece, piece), piece)
            copies.append(
                pltpu.make_async_copy(
                    source.at[here], target.at[pl.ds(i * piece, piece)], arrived.at[i]
                )
            )
        for copy in copies:
            copy.start()
        for copy in copies:
            copy.wait()

    return pl.pallas_call(
        body,
        out_shape=pltpu.VMEM((rows, weights.shape[1]), weights.dtype),
        in_specs=[pl.BlockSpec(memory_space=pltpu.HBM)],
        out_specs=pl.BlockSpec(memory_space=pltpu.VMEM),
        scratch_shapes=[pltpu.SemaphoreType.DMA((COPIES,))],
        cost_estimate=pl.CostEstimate(flops=0, bytes_accessed=size, transcendentals=0),
        compiler_params=pltpu.CompilerParams(vmem_limit_bytes=1 << 20),
        name=name,
    )(in_hbm(weights))


def expand_rows(rows, w_gate, w_up, start, columns):
    count, depth = rows.shape[0], w_gate.shape[0]

    def body(rows_ref, gate_ref, up_ref, hidden_ref):
        def step(first, batch):
            x = rows_ref[pl.ds(first, batch), :depth]
            tile = min(TILE, columns)
            for i in range(0, columns, tile):
                cut = slice(start + i, start + i + tile)
                gate = jnp.dot(x, gate_ref[:, cut], preferred_element_type=jnp.float32)
                up = jnp.dot(x, up_ref[:, cut], preferred_element_type=jnp.float32)
                value = gate / (1.0 + jnp.exp(-gate)) * up
                hidden_ref[pl.ds(first, batch), i : i + tile] = value.astype(hidden_ref.dtype)

        row_batches(count, step)

    return pl.pallas_call(
        body,
        out_shape=jax.ShapeDtypeStruct((count, columns), rows.dtype),
        in_specs=[pl.BlockSpec(memory_space=pltpu.VMEM)] * 3,
        out_specs=pl.BlockSpec(memory_space=pltpu.VMEM),
        cost_estimate=pl.CostEstimate(flops=0, bytes_accessed=count * columns, transcendentals=0),
        compiler_params=pltpu.CompilerParams(vmem_limit_bytes=rows.nbytes + (6 << 20)),
        name="expand_rows",
    )(rows, in_vmem(w_gate), in_vmem(w_up))


def contract_hidden(parts, downs, before=None, rows=None, half=None):
    count, width = parts[0][0].shape[0], downs[0].shape[1]
    experts = lax.axis_size("expert")
    operands = [part for part, _, _ in parts] + [in_vmem(down) for down in downs]
    operands += [value for value in (before, rows) if value is not None]

    def body(*refs):
        part_refs, down_refs = refs[: len(parts)], refs[len(parts) : len(parts) + len(downs)]
        rest = list(refs[len(parts) + len(downs) : -1])
        before_ref = rest.pop(0) if before is not None else None
        rows_ref = rest.pop(0) if rows is not None else None
        me = lax.axis_index("expert")

        def step(first, batch):
            here = pl.ds(first, batch)
            lefts = [ref[here, :] for ref in part_refs]
            if half is not None:
                order = [i ^ 1 for i in range(count // half)]
                lefts = [
                    jnp.concatenate([left[i * half : (i + 1) * half] for i in order])
                    for left in lefts
                ]
            if rows is not None:
                table = rows_ref[here, rows.shape[1] - LANES :].astype(jnp.float32)
                lane = lax.broadcasted_iota(jnp.int32, table.shape, 1)
                mine = (lax.rem(lane, experts) == me) & (lane < 3 * experts)
                scale = jnp.sum(jnp.where(mine, table, 0.0), axis=1, keepdims=True)
            tile = min(2 * TILE, width)
            for i in range(0, width, tile):
                cut = slice(i, i + tile)
                total = 0.0 if before is None else before_ref[here, cut]
                for left, (_, j, unit) in zip(lefts, parts):
                    right = down_refs[j][unit : unit + left.shape[1], cut]
                    total = total + jnp.dot(left, right, preferred_element_type=jnp.float32)
                if rows is not None:
                    total = total.astype(jnp.bfloat16).astype(jnp.float32) * scale
                refs[-1][here, cut] = total

        row_batches(count, step)

    return pl.pallas_call(
        body,
        out_shape=jax.ShapeDtypeStruct((count, width), jnp.float32),
        in_specs=[pl.BlockSpec(memory_space=pltpu.VMEM)] * len(operands),
        out_specs=pl.BlockSpec(memory_space=pltpu.VMEM),
        cost_estimate=pl.CostEstimate(flops=0, bytes_accessed=count * width, transcendentals=0),
        compiler_params=pltpu.CompilerParams(
            vmem_limit_bytes=8 * count * width
            + (6 << 20)
            + (0 if rows is None else rows.nbytes)
        ),
        name="contract_hidden",
    )(*operands)


def local(tokens, expert_ids, gate_probs, w_gate, w_up, w_down):
    token_count, width = tokens.shape
    groups, experts = lax.axis_size("dp"), lax.axis_size("expert")
    wide, high = groups // 2, experts // 4

    block = pack_block(tokens, expert_ids, gate_probs, experts)
    near = stack_blocks([block] + [swap(block, 0, 4 * i) for i in range(1, high)])
    gate_weights = fetch(w_gate[0], block, "fetch_gate")
    near, gate_weights = lax.optimization_barrier((near, gate_weights))
    if wide > 1:
        near = jnp.concatenate([near] + [swap(near, 2 * i, 0) for i in range(1, wide)])
    chip = [near, swap(near, 0, 2), swap(near, 1, 0), swap(near, 1, 2)]
    up_weights = fetch(w_up[0], near, "fetch_up")
    units = up_weights.shape[1]
    own_down = fetch(w_down[0], near, "fetch_down", units, 0)
    chip[3], up_weights, own_down = lax.optimization_barrier((chip[3], up_weights, own_down))
    chip = jnp.concatenate(chip)
    rows = jnp.concatenate([chip, swap(chip, 0, 1)])

    chunks = CHUNKS if units % (LANES * CHUNKS) == 0 else 1
    step = units // chunks
    half = rows.shape[0] // 4 if groups == 2 and rows.shape[0] <= BATCH else None

    def from_group(value, mask):
        value = swap(value, mask, 0)
        if half is not None:
            return value
        value = value.reshape(2, 2, 2, wide, high * token_count, step)
        value = jnp.stack([value[:, i ^ (mask & 1)] for i in range(2)], axis=1)
        value = jnp.stack([value[:, :, :, i ^ (mask >> 1)] for i in range(wide)], axis=3)
        return value.reshape(-1, step)

    total, others = None, [[] for _ in range(chunks)]
    for i in range(chunks):
        if total is not None:
            rows, total = lax.optimization_barrier((rows, total))
        hidden = expand_rows(rows, gate_weights, up_weights, i * step, step)
        for mask in range(1, groups):
            others[i].append((from_group(hidden, mask), mask - 1, i * step))
        total = contract_hidden([(hidden, 0, i * step)], [own_down], total)
    downs = [
        fetch(w_down[0], hidden, "fetch_down", units, mask) for mask in range(1, groups)
    ]
    for i in range(chunks):
        weigh = rows if i == chunks - 1 else None
        total = contract_hidden(others[i], downs, total, weigh, half)

    columns = w_down.shape[2]
    send = lambda value, g, e: swap(value.astype(jnp.bfloat16), g, e).astype(jnp.float32)
    total = total.reshape(2, -1, columns)
    total = total[0] + send(total[1], 0, 1)
    part = total.shape[0] // 4
    near, over_y, over_x, corner = (total[i * part : (i + 1) * part] for i in range(4))
    total = jnp.concatenate(
        [near + send(over_y, 0, 2), send(over_x, 1, 0) + send(corner, 1, 2)], axis=1
    )
    part = part // wide
    total = jnp.concatenate(
        [total[:part]]
        + [send(total[i * part : (i + 1) * part], 2 * i, 0) for i in range(1, wide)],
        axis=1,
    )
    combined = total[:token_count]
    for i in range(1, high):
        combined = combined + send(total[i * token_count : (i + 1) * token_count], 0, 4 * i)
    combined = combined.astype(jnp.bfloat16)
    group = lax.axis_index("dp")
    if groups == 2:
        swapped = jnp.concatenate([combined[:, columns:], combined[:, :columns]], axis=1)
        return jnp.where(group == 0, combined, swapped)
    combined = combined.reshape(token_count, groups, columns)
    combined = jnp.take(combined, jnp.arange(groups) ^ group, axis=1)
    return combined.reshape(token_count, width)


def solution(mesh):
    row, expert = P(("dp", "expert"), None), P("expert", None, "dp")
    return jax.shard_map(
        local,
        mesh=mesh,
        in_specs=(row, row, row, expert, expert, expert),
        out_specs=row,
        check_vma=False,
    )
```

```python
import jax
import jax.numpy as jnp
from jax import lax
from jax.experimental import pallas as pl
from jax.experimental.pallas import tpu as pltpu
from jax.sharding import Mesh
from jax.sharding import PartitionSpec as P

CHUNKS = 2
TILE = 256
BATCH = 128
COPY_BYTES = 1 << 20
LANES = 128
EXPERT = ("far", "core")


def swap(value, group_mask, expert_mask):
    groups, experts = lax.axis_size("dp"), lax.axis_size(EXPERT)
    pairs = [
        (g * experts + e, (g ^ group_mask) * experts + (e ^ expert_mask))
        for g in range(groups)
        for e in range(experts)
    ]
    return lax.ppermute(value, ("dp",) + EXPERT, pairs)


def in_vmem(value):
    return pltpu.with_memory_space_constraint(value, pltpu.VMEM)


def in_hbm(value):
    return pltpu.with_memory_space_constraint(value, pltpu.HBM)


def row_batches(count, step):
    batch = min(BATCH, count)
    if count == batch:
        step(0, batch)
    else:

        @pl.loop(0, count // batch)
        def _(i):
            step(pl.multiple_of(i * batch, batch), batch)


def pack_block(tokens, expert_ids, gate_probs, experts):
    count, width = tokens.shape
    top = expert_ids.shape[1]

    def body(tokens_ref, ids_ref, probs_ref, block_ref):
        block_ref[:, :width] = tokens_ref[...]
        lane = lax.broadcasted_iota(jnp.int32, (count, LANES), 1)
        table = jnp.zeros((count, LANES), jnp.float32)
        for k in range(top):
            hit = ids_ref[:, k : k + 1] == lax.rem(lane, experts)
            table = jnp.where(hit, probs_ref[:, k : k + 1], table)
        packed = jnp.zeros((count, LANES), jnp.float32)
        for i in range(3):
            part = table.astype(jnp.bfloat16).astype(jnp.float32)
            packed = jnp.where(lane // experts == i, part, packed)
            table = table - part
        block_ref[:, width:] = packed.astype(block_ref.dtype)

    return pl.pallas_call(
        body,
        out_shape=jax.ShapeDtypeStruct((count, width + LANES), tokens.dtype),
        in_specs=[pl.BlockSpec(memory_space=pltpu.VMEM)] * 3,
        out_specs=pl.BlockSpec(memory_space=pltpu.VMEM),
        compiler_params=pltpu.CompilerParams(vmem_limit_bytes=1 << 20),
        name="pack_block",
    )(in_hbm(tokens), in_hbm(expert_ids), in_hbm(gate_probs))


def stack_blocks(blocks):
    count, width = blocks[0].shape

    def body(*refs):
        values = [ref[...].astype(jnp.float32) for ref in refs[:-1]]
        refs[-1][...] = jnp.concatenate(values).astype(refs[-1].dtype)

    return pl.pallas_call(
        body,
        out_shape=jax.ShapeDtypeStruct((len(blocks) * count, width), blocks[0].dtype),
        in_specs=[pl.BlockSpec(memory_space=pltpu.VMEM)] * len(blocks),
        out_specs=pl.BlockSpec(memory_space=pltpu.VMEM),
        compiler_params=pltpu.CompilerParams(vmem_limit_bytes=4 << 20),
        name="stack_blocks",
    )(*blocks)


def fetch(pieces, after, units, name):
    shapes = [(w.shape[0] if mask is None else units, w.shape[1]) for w, mask in pieces]
    parts = []
    for i, (rows, columns) in enumerate(shapes):
        step = max(16, min(rows, COPY_BYTES // (2 * columns)))
        parts += [(i, first, step) for first in range(0, rows, step)]
    operands, _ = lax.optimization_barrier(([w for w, _ in pieces], after))

    def body(*refs):
        sources, targets = refs[: len(pieces)], refs[len(pieces) : -1]
        group = lax.axis_index("dp")
        copies = []
        for j, (i, first, step) in enumerate(parts):
            mask = pieces[i][1]
            start = first if mask is None else pl.multiple_of((group ^ mask) * units + first, 16)
            source = sources[i].at[pl.ds(start, step)]
            target = targets[i].at[pl.ds(first, step)]
            copies.append(pltpu.make_async_copy(source, target, refs[-1].at[j]))
        for copy in copies:
            copy.start()
        for copy in copies:
            copy.wait()

    return pl.pallas_call(
        body,
        out_shape=[pltpu.VMEM(shape, w.dtype) for shape, (w, _) in zip(shapes, pieces)],
        in_specs=[pl.BlockSpec(memory_space=pltpu.HBM)] * len(pieces),
        out_specs=[pl.BlockSpec(memory_space=pltpu.VMEM)] * len(pieces),
        scratch_shapes=[pltpu.SemaphoreType.DMA((len(parts),))],
        cost_estimate=pl.CostEstimate(
            flops=0, bytes_accessed=sum(2 * r * c for r, c in shapes), transcendentals=0
        ),
        compiler_params=pltpu.CompilerParams(vmem_limit_bytes=1 << 20),
        name=name,
    )(*[in_hbm(w) for w in operands])


def expand_rows(rows, w_gate, w_up, start, columns):
    count, depth = rows.shape[0], w_gate.shape[0]

    def body(rows_ref, gate_ref, up_ref, hidden_ref):
        def step(first, batch):
            x = rows_ref[pl.ds(first, batch), :depth]
            tile = min(TILE, columns)
            for i in range(0, columns, tile):
                cut = slice(start + i, start + i + tile)
                gate = jnp.dot(x, gate_ref[:, cut], preferred_element_type=jnp.float32)
                up = jnp.dot(x, up_ref[:, cut], preferred_element_type=jnp.float32)
                value = gate / (1.0 + jnp.exp(-gate)) * up
                hidden_ref[pl.ds(first, batch), i : i + tile] = value.astype(hidden_ref.dtype)

        row_batches(count, step)

    return pl.pallas_call(
        body,
        out_shape=jax.ShapeDtypeStruct((count, columns), rows.dtype),
        in_specs=[pl.BlockSpec(memory_space=pltpu.VMEM)] * 3,
        out_specs=pl.BlockSpec(memory_space=pltpu.VMEM),
        cost_estimate=pl.CostEstimate(flops=0, bytes_accessed=count * columns, transcendentals=0),
        compiler_params=pltpu.CompilerParams(vmem_limit_bytes=rows.nbytes + (6 << 20)),
        name="expand_rows",
    )(rows, in_vmem(w_gate), in_vmem(w_up))


def contract_hidden(parts, downs, before=None, rows=None, half=None):
    count, width = parts[0][0].shape[0], downs[0].shape[1]
    experts = lax.axis_size(EXPERT)
    operands = [part for part, _, _ in parts] + [in_vmem(down) for down in downs]
    operands += [value for value in (before, rows) if value is not None]

    def body(*refs):
        part_refs, down_refs = refs[: len(parts)], refs[len(parts) : len(parts) + len(downs)]
        rest = list(refs[len(parts) + len(downs) : -1])
        before_ref = rest.pop(0) if before is not None else None
        rows_ref = rest.pop(0) if rows is not None else None
        me = lax.axis_index(EXPERT)

        def step(first, batch):
            here = pl.ds(first, batch)
            lefts = [ref[here, :] for ref in part_refs]
            if half is not None:
                order = [i ^ 1 for i in range(count // half)]
                lefts = [
                    jnp.concatenate([left[i * half : (i + 1) * half] for i in order])
                    for left in lefts
                ]
            if rows is not None:
                table = rows_ref[here, rows.shape[1] - LANES :].astype(jnp.float32)
                lane = lax.broadcasted_iota(jnp.int32, table.shape, 1)
                mine = (lax.rem(lane, experts) == me) & (lane < 3 * experts)
                scale = jnp.sum(jnp.where(mine, table, 0.0), axis=1, keepdims=True)
            tile = min(2 * TILE, width)
            for i in range(0, width, tile):
                cut = slice(i, i + tile)
                total = 0.0 if before is None else before_ref[here, cut]
                for left, (_, j, unit) in zip(lefts, parts):
                    right = down_refs[j][unit : unit + left.shape[1], cut]
                    total = total + jnp.dot(left, right, preferred_element_type=jnp.float32)
                if rows is not None:
                    total = total.astype(jnp.bfloat16).astype(jnp.float32) * scale
                refs[-1][here, cut] = total

        row_batches(count, step)

    return pl.pallas_call(
        body,
        out_shape=jax.ShapeDtypeStruct((count, width), jnp.float32),
        in_specs=[pl.BlockSpec(memory_space=pltpu.VMEM)] * len(operands),
        out_specs=pl.BlockSpec(memory_space=pltpu.VMEM),
        cost_estimate=pl.CostEstimate(flops=0, bytes_accessed=count * width, transcendentals=0),
        compiler_params=pltpu.CompilerParams(
            vmem_limit_bytes=8 * count * width
            + (6 << 20)
            + (0 if rows is None else rows.nbytes)
        ),
        name="contract_hidden",
    )(*operands)


def add_and_order(total, received, wide, high):
    count, width = received.shape
    blocks = 4 * wide * high
    tokens, far_size = count // blocks, 2 * high

    def body(total_ref, received_ref, out_ref):
        group, far = lax.axis_index("dp"), lax.axis_index("far")
        for i in range(blocks):
            x, y, w, h = i // (blocks // 2), i // (wide * high) % 2, i // high % wide, i % high
            slot = (group ^ (x + 2 * w)) * far_size + (far ^ (y + 2 * h))
            here = slice(i * tokens, (i + 1) * tokens)
            value = total_ref[here, :] + received_ref[here, :].astype(jnp.float32)
            out_ref[slot] = value.astype(out_ref.dtype)

    return pl.pallas_call(
        body,
        out_shape=jax.ShapeDtypeStruct((blocks, tokens, width), received.dtype),
        in_specs=[pl.BlockSpec(memory_space=pltpu.VMEM)] * 2,
        out_specs=pl.BlockSpec(memory_space=pltpu.VMEM),
        compiler_params=pltpu.CompilerParams(vmem_limit_bytes=12 * total.size + (6 << 20)),
        name="add_and_order",
    )(total, received)


def local(tokens, expert_ids, gate_probs, w_gate, w_up, w_down):
    token_count, width = tokens.shape
    groups, experts = lax.axis_size("dp"), lax.axis_size(EXPERT)
    wide, high = groups // 2, experts // 4

    block = pack_block(tokens, expert_ids, gate_probs, experts)
    near = stack_blocks([block] + [swap(block, 0, 4 * i) for i in range(1, high)])
    units = w_up.shape[2]
    (gate_weights,) = fetch([(w_gate[0], None)], block, units, "fetch_gate")
    near, gate_weights = lax.optimization_barrier((near, gate_weights))
    if wide > 1:
        near = jnp.concatenate([near] + [swap(near, 2 * i, 0) for i in range(1, wide)])
    chip = [near, swap(near, 0, 2), swap(near, 1, 0), swap(near, 1, 2)]
    up_weights, own_down = fetch([(w_up[0], None), (w_down[0], 0)], near, units, "fetch_up")
    chip[3], up_weights, own_down = lax.optimization_barrier((chip[3], up_weights, own_down))
    chip = jnp.concatenate(chip)
    rows = jnp.concatenate([chip, swap(chip, 0, 1)])

    chunks = CHUNKS if units % (LANES * CHUNKS) == 0 else 1
    step = units // chunks
    half = rows.shape[0] // 4 if groups == 2 and rows.shape[0] <= BATCH else None

    def from_group(value, mask):
        value = swap(value, mask, 0)
        if half is not None:
            return value
        value = value.reshape(2, 2, 2, wide, high * token_count, step)
        value = jnp.stack([value[:, i ^ (mask & 1)] for i in range(2)], axis=1)
        value = jnp.stack([value[:, :, :, i ^ (mask >> 1)] for i in range(wide)], axis=3)
        return value.reshape(-1, step)

    total, others = None, [[] for _ in range(chunks)]
    for i in range(chunks):
        if total is not None:
            rows, total = lax.optimization_barrier((rows, total))
        hidden = expand_rows(rows, gate_weights, up_weights, i * step, step)
        for mask in range(1, groups):
            others[i].append((from_group(hidden, mask), mask - 1, i * step))
        total = contract_hidden([(hidden, 0, i * step)], [own_down], total)
    pieces = [(w_down[0], mask) for mask in range(1, groups)]
    downs = fetch(pieces, hidden, units, "fetch_down")
    for i in range(chunks):
        weigh = rows if i == chunks - 1 else None
        total = contract_hidden(others[i], downs, total, weigh, half)

    count, columns = rows.shape[0] // 2, w_down.shape[2]
    received = swap(total[count:].astype(jnp.bfloat16), 0, 1)
    blocks = add_and_order(total, received, wide, high)
    blocks = lax.all_to_all(blocks, ("dp", "far"), split_axis=0, concat_axis=0, tiled=True)
    blocks = blocks.reshape(groups, -1, token_count, columns).astype(jnp.float32)
    combined = jnp.sum(blocks, axis=1).astype(jnp.bfloat16)
    return combined.transpose(1, 0, 2).reshape(token_count, width)


def solution(mesh):
    groups, experts = mesh.devices.shape
    split = Mesh(mesh.devices.reshape(groups, experts // 2, 2), ("dp", "far", "core"))
    row, expert = P(("dp", "far", "core"), None), P(EXPERT, None, "dp")
    return jax.shard_map(
        local,
        mesh=split,
        in_specs=(row, row, row, expert, expert, expert),
        out_specs=row,
        check_vma=False,
    )
```

```python
import jax
import jax.numpy as jnp
from jax import lax
from jax.experimental import pallas as pl
from jax.experimental.pallas import tpu as pltpu
from jax.sharding import Mesh
from jax.sharding import PartitionSpec as P

CHUNKS = 2
TILE = 256
BATCH = 128
LANES = 128
EXPERT = ("far", "core")


def swap(value, group_mask, expert_mask):
    groups, experts = lax.axis_size("dp"), lax.axis_size(EXPERT)
    pairs = [
        (g * experts + e, (g ^ group_mask) * experts + (e ^ expert_mask))
        for g in range(groups)
        for e in range(experts)
    ]
    return lax.ppermute(value, ("dp",) + EXPERT, pairs)


def in_vmem(value):
    return pltpu.with_memory_space_constraint(value, pltpu.VMEM)


def in_hbm(value):
    return pltpu.with_memory_space_constraint(value, pltpu.HBM)


def row_batches(count, step):
    batch = min(BATCH, count)
    if count == batch:
        step(0, batch)
    else:

        @pl.loop(0, count // batch)
        def _(i):
            step(pl.multiple_of(i * batch, batch), batch)


def pack_block(tokens, expert_ids, gate_probs, experts):
    count, width = tokens.shape
    top = expert_ids.shape[1]

    def body(tokens_ref, ids_ref, probs_ref, block_ref):
        block_ref[:, :width] = tokens_ref[...]
        lane = lax.broadcasted_iota(jnp.int32, (count, LANES), 1)
        table = jnp.zeros((count, LANES), jnp.float32)
        for k in range(top):
            hit = ids_ref[:, k : k + 1] == lax.rem(lane, experts)
            table = jnp.where(hit, probs_ref[:, k : k + 1], table)
        packed = jnp.zeros((count, LANES), jnp.float32)
        for i in range(3):
            part = table.astype(jnp.bfloat16).astype(jnp.float32)
            packed = jnp.where(lane // experts == i, part, packed)
            table = table - part
        block_ref[:, width:] = packed.astype(block_ref.dtype)

    return pl.pallas_call(
        body,
        out_shape=jax.ShapeDtypeStruct((count, width + LANES), tokens.dtype),
        in_specs=[pl.BlockSpec(memory_space=pltpu.VMEM)] * 3,
        out_specs=pl.BlockSpec(memory_space=pltpu.VMEM),
        cost_estimate=pl.CostEstimate(flops=20 * 10**9, bytes_accessed=0, transcendentals=0),
        compiler_params=pltpu.CompilerParams(vmem_limit_bytes=1 << 20),
        name="pack_block",
    )(in_hbm(tokens), in_hbm(expert_ids), in_hbm(gate_probs))


def stack_blocks(blocks):
    count, width = blocks[0].shape

    def body(*refs):
        values = [ref[...].astype(jnp.float32) for ref in refs[:-1]]
        refs[-1][...] = jnp.concatenate(values).astype(refs[-1].dtype)

    return pl.pallas_call(
        body,
        out_shape=jax.ShapeDtypeStruct((len(blocks) * count, width), blocks[0].dtype),
        in_specs=[pl.BlockSpec(memory_space=pltpu.VMEM)] * len(blocks),
        out_specs=pl.BlockSpec(memory_space=pltpu.VMEM),
        compiler_params=pltpu.CompilerParams(vmem_limit_bytes=4 << 20),
        name="stack_blocks",
    )(*blocks)


def expand_rows(rows, w_gate, w_up, start, columns):
    count, depth = rows.shape[0], w_gate.shape[0]

    def body(rows_ref, gate_ref, up_ref, hidden_ref):
        def step(first, batch):
            x = rows_ref[pl.ds(first, batch), :depth]
            tile = min(TILE, columns)
            for i in range(0, columns, tile):
                cut = slice(start + i, start + i + tile)
                gate = jnp.dot(x, gate_ref[:, cut], preferred_element_type=jnp.float32)
                up = jnp.dot(x, up_ref[:, cut], preferred_element_type=jnp.float32)
                value = gate / (1.0 + jnp.exp(-gate)) * up
                hidden_ref[pl.ds(first, batch), i : i + tile] = value.astype(hidden_ref.dtype)

        row_batches(count, step)

    return pl.pallas_call(
        body,
        out_shape=jax.ShapeDtypeStruct((count, columns), rows.dtype),
        in_specs=[pl.BlockSpec(memory_space=pltpu.VMEM)] * 3,
        out_specs=pl.BlockSpec(memory_space=pltpu.VMEM),
        cost_estimate=pl.CostEstimate(flops=0, bytes_accessed=count * columns, transcendentals=0),
        compiler_params=pltpu.CompilerParams(vmem_limit_bytes=rows.nbytes + (6 << 20)),
        name="expand_rows",
    )(rows, in_vmem(w_gate), in_vmem(w_up))


def contract_hidden(parts, w_down, units, before=None, rows=None, half=None):
    count, width = parts[0][0].shape[0], w_down.shape[1]
    experts = lax.axis_size(EXPERT)
    operands = [part for part, _, _ in parts] + [in_vmem(w_down)]
    operands += [value for value in (before, rows) if value is not None]

    def body(*refs):
        part_refs, down_ref = refs[: len(parts)], refs[len(parts)]
        rest = list(refs[len(parts) + 1 : -1])
        before_ref = rest.pop(0) if before is not None else None
        rows_ref = rest.pop(0) if rows is not None else None
        me, group = lax.axis_index(EXPERT), lax.axis_index("dp")

        def step(first, batch):
            here = pl.ds(first, batch)
            lefts = [ref[here, :] for ref in part_refs]
            if half is not None:
                order = [i ^ 1 for i in range(count // half)]
                lefts = [
                    jnp.concatenate([left[i * half : (i + 1) * half] for i in order])
                    for left in lefts
                ]
            if rows is not None:
                table = rows_ref[here, rows.shape[1] - LANES :].astype(jnp.float32)
                lane = lax.broadcasted_iota(jnp.int32, table.shape, 1)
                mine = (lax.rem(lane, experts) == me) & (lane < 3 * experts)
                scale = jnp.sum(jnp.where(mine, table, 0.0), axis=1, keepdims=True)
            tile = min(2 * TILE, width)
            for i in range(0, width, tile):
                cut = slice(i, i + tile)
                total = 0.0 if before is None else before_ref[here, cut]
                for left, (_, mask, unit) in zip(lefts, parts):
                    start = pl.multiple_of((group ^ mask) * units + unit, LANES)
                    right = down_ref[pl.ds(start, left.shape[1]), cut]
                    total = total + jnp.dot(left, right, preferred_element_type=jnp.float32)
                if rows is not None:
                    total = total.astype(jnp.bfloat16).astype(jnp.float32) * scale
                refs[-1][here, cut] = total

        row_batches(count, step)

    return pl.pallas_call(
        body,
        out_shape=jax.ShapeDtypeStruct((count, width), jnp.float32),
        in_specs=[pl.BlockSpec(memory_space=pltpu.VMEM)] * len(operands),
        out_specs=pl.BlockSpec(memory_space=pltpu.VMEM),
        cost_estimate=pl.CostEstimate(flops=0, bytes_accessed=count * width, transcendentals=0),
        compiler_params=pltpu.CompilerParams(
            vmem_limit_bytes=8 * count * width
            + (6 << 20)
            + (0 if rows is None else rows.nbytes)
        ),
        name="contract_hidden",
    )(*operands)


def add_and_order(total, received, wide, high):
    count, width = received.shape
    blocks = 4 * wide * high
    tokens, far_size = count // blocks, 2 * high

    def body(total_ref, received_ref, out_ref):
        group, far = lax.axis_index("dp"), lax.axis_index("far")
        for i in range(blocks):
            x, y, w, h = i // (blocks // 2), i // (wide * high) % 2, i // high % wide, i % high
            slot = (group ^ (x + 2 * w)) * far_size + (far ^ (y + 2 * h))
            here = slice(i * tokens, (i + 1) * tokens)
            value = total_ref[here, :] + received_ref[here, :].astype(jnp.float32)
            out_ref[slot] = value.astype(out_ref.dtype)

    return pl.pallas_call(
        body,
        out_shape=jax.ShapeDtypeStruct((blocks, tokens, width), received.dtype),
        in_specs=[pl.BlockSpec(memory_space=pltpu.VMEM)] * 2,
        out_specs=pl.BlockSpec(memory_space=pltpu.VMEM),
        compiler_params=pltpu.CompilerParams(vmem_limit_bytes=12 * total.size + (6 << 20)),
        name="add_and_order",
    )(total, received)


def local(tokens, expert_ids, gate_probs, w_gate, w_up, w_down):
    token_count, width = tokens.shape
    groups, experts = lax.axis_size("dp"), lax.axis_size(EXPERT)
    wide, high = groups // 2, experts // 4

    block = pack_block(tokens, expert_ids, gate_probs, experts)
    units = w_up.shape[2]
    weights = lax.optimization_barrier((block, w_gate[0], w_up[0], w_down[0]))
    block, gate_weights, up_weights, down_weights = weights
    near = stack_blocks([block] + [swap(block, 0, 4 * i) for i in range(1, high)])
    if wide > 1:
        near = jnp.concatenate([near] + [swap(near, 2 * i, 0) for i in range(1, wide)])
    chip = [near, swap(near, 0, 2), swap(near, 1, 0), swap(near, 1, 2)]
    chip = jnp.concatenate(chip)
    rows = jnp.concatenate([chip, swap(chip, 0, 1)])

    chunks = CHUNKS if units % (LANES * CHUNKS) == 0 else 1
    step = units // chunks
    half = rows.shape[0] // 4 if groups == 2 and rows.shape[0] <= BATCH else None

    def from_group(value, mask):
        value = swap(value, mask, 0)
        if half is not None:
            return value
        value = value.reshape(2, 2, 2, wide, high * token_count, step)
        value = jnp.stack([value[:, i ^ (mask & 1)] for i in range(2)], axis=1)
        value = jnp.stack([value[:, :, :, i ^ (mask >> 1)] for i in range(wide)], axis=3)
        return value.reshape(-1, step)

    total, others = None, [[] for _ in range(chunks)]
    for i in range(chunks):
        if total is not None:
            rows, total = lax.optimization_barrier((rows, total))
        hidden = expand_rows(rows, gate_weights, up_weights, i * step, step)
        for mask in range(1, groups):
            others[i].append((from_group(hidden, mask), mask, i * step))
        total = contract_hidden([(hidden, 0, i * step)], down_weights, units, total)
    for i in range(chunks):
        weigh = rows if i == chunks - 1 else None
        total = contract_hidden(others[i], down_weights, units, total, weigh, half)

    count, columns = rows.shape[0] // 2, w_down.shape[2]
    received = swap(total[count:].astype(jnp.bfloat16), 0, 1)
    blocks = add_and_order(total, received, wide, high)
    blocks = lax.all_to_all(blocks, ("dp", "far"), split_axis=0, concat_axis=0, tiled=True)
    blocks = blocks.reshape(groups, -1, token_count, columns).astype(jnp.float32)
    combined = jnp.sum(blocks, axis=1).astype(jnp.bfloat16)
    return combined.transpose(1, 0, 2).reshape(token_count, width)


def solution(mesh):
    groups, experts = mesh.devices.shape
    split = Mesh(mesh.devices.reshape(groups, experts // 2, 2), ("dp", "far", "core"))
    row, expert = P(("dp", "far", "core"), None), P(EXPERT, None, "dp")
    return jax.shard_map(
        local,
        mesh=split,
        in_specs=(row, row, row, expert, expert, expert),
        out_specs=row,
        check_vma=False,
    )
```

```python
import jax
import jax.numpy as jnp
from jax import lax
from jax.experimental import pallas as pl
from jax.experimental.pallas import tpu as pltpu
from jax.sharding import Mesh
from jax.sharding import PartitionSpec as P

TILE = 256
BATCH = 128
LANES = 128
EXPERT = ("far", "core")


def swap(value, group_mask, expert_mask):
    groups, experts = lax.axis_size("dp"), lax.axis_size(EXPERT)
    pairs = [
        (g * experts + e, (g ^ group_mask) * experts + (e ^ expert_mask))
        for g in range(groups)
        for e in range(experts)
    ]
    return lax.ppermute(value, ("dp",) + EXPERT, pairs)


def in_vmem(value):
    return pltpu.with_memory_space_constraint(value, pltpu.VMEM)


def in_hbm(value):
    return pltpu.with_memory_space_constraint(value, pltpu.HBM)


def row_batches(count, step):
    batch = min(BATCH, count)
    if count == batch:
        step(0, batch)
    else:

        @pl.loop(0, count // batch)
        def _(i):
            step(pl.multiple_of(i * batch, batch), batch)


def pack_block(tokens, expert_ids, gate_probs, experts):
    count, width = tokens.shape
    top = expert_ids.shape[1]

    def body(tokens_ref, ids_ref, probs_ref, block_ref):
        block_ref[:, :width] = tokens_ref[...]
        lane = lax.broadcasted_iota(jnp.int32, (count, LANES), 1)
        table = jnp.zeros((count, LANES), jnp.float32)
        for k in range(top):
            hit = ids_ref[:, k : k + 1] == lax.rem(lane, experts)
            table = jnp.where(hit, probs_ref[:, k : k + 1], table)
        packed = jnp.zeros((count, LANES), jnp.float32)
        for i in range(3):
            part = table.astype(jnp.bfloat16).astype(jnp.float32)
            packed = jnp.where(lane // experts == i, part, packed)
            table = table - part
        block_ref[:, width:] = packed.astype(block_ref.dtype)

    return pl.pallas_call(
        body,
        out_shape=jax.ShapeDtypeStruct((count, width + LANES), tokens.dtype),
        in_specs=[pl.BlockSpec(memory_space=pltpu.VMEM)] * 3,
        out_specs=pl.BlockSpec(memory_space=pltpu.VMEM),
        cost_estimate=pl.CostEstimate(flops=20 * 10**9, bytes_accessed=0, transcendentals=0),
        compiler_params=pltpu.CompilerParams(vmem_limit_bytes=1 << 20),
        name="pack_block",
    )(in_hbm(tokens), in_hbm(expert_ids), in_hbm(gate_probs))


def stack_blocks(blocks):
    count, width = blocks[0].shape

    def body(*refs):
        values = [ref[...].astype(jnp.float32) for ref in refs[:-1]]
        refs[-1][...] = jnp.concatenate(values).astype(refs[-1].dtype)

    return pl.pallas_call(
        body,
        out_shape=jax.ShapeDtypeStruct((len(blocks) * count, width), blocks[0].dtype),
        in_specs=[pl.BlockSpec(memory_space=pltpu.VMEM)] * len(blocks),
        out_specs=pl.BlockSpec(memory_space=pltpu.VMEM),
        compiler_params=pltpu.CompilerParams(vmem_limit_bytes=4 << 20),
        name="stack_blocks",
    )(*blocks)


def expand_rows(rows, w_gate, w_up):
    count, depth, units = rows.shape[0], w_gate.shape[0], w_gate.shape[1]

    def body(rows_ref, gate_ref, up_ref, hidden_ref):
        def step(first, batch):
            x = rows_ref[pl.ds(first, batch), :depth]
            tile = min(TILE, units)
            for i in range(0, units, tile):
                cut = slice(i, i + tile)
                gate = jnp.dot(x, gate_ref[:, cut], preferred_element_type=jnp.float32)
                up = jnp.dot(x, up_ref[:, cut], preferred_element_type=jnp.float32)
                value = gate / (1.0 + jnp.exp(-gate)) * up
                hidden_ref[pl.ds(first, batch), cut] = value.astype(hidden_ref.dtype)

        row_batches(count, step)

    return pl.pallas_call(
        body,
        out_shape=jax.ShapeDtypeStruct((count, units), rows.dtype),
        in_specs=[pl.BlockSpec(memory_space=pltpu.VMEM)] * 3,
        out_specs=pl.BlockSpec(memory_space=pltpu.VMEM),
        cost_estimate=pl.CostEstimate(flops=0, bytes_accessed=count * units, transcendentals=0),
        compiler_params=pltpu.CompilerParams(vmem_limit_bytes=rows.nbytes + (6 << 20)),
        name="expand_rows",
    )(rows, in_vmem(w_gate), in_vmem(w_up))


def contract_own(halves, w_down):
    count, units = halves[0].shape
    width = w_down.shape[1]

    def body(first_ref, second_ref, down_ref, total_ref):
        start = pl.multiple_of(lax.axis_index("dp") * units, LANES)

        def step(first, batch):
            here = pl.ds(first, batch)
            left = jnp.concatenate([first_ref[here, :], second_ref[here, :]])
            tile = min(2 * TILE, width)
            for i in range(0, width, tile):
                cut = slice(i, i + tile)
                right = down_ref[pl.ds(start, units), cut]
                total = jnp.dot(left, right, preferred_element_type=jnp.float32)
                total_ref[0, here, cut] = total[:batch]
                total_ref[1, here, cut] = total[batch:]

        row_batches(count, step)

    return pl.pallas_call(
        body,
        out_shape=jax.ShapeDtypeStruct((2, count, width), jnp.float32),
        in_specs=[pl.BlockSpec(memory_space=pltpu.VMEM)] * 3,
        out_specs=pl.BlockSpec(memory_space=pltpu.VMEM),
        cost_estimate=pl.CostEstimate(flops=0, bytes_accessed=count * width, transcendentals=0),
        compiler_params=pltpu.CompilerParams(vmem_limit_bytes=12 * count * width + (6 << 20)),
        name="contract_own",
    )(*halves, in_vmem(w_down))


def contract_others(parts, w_down, own, index, rows, kind, swapped):
    count, units = parts[0].shape
    width = w_down.shape[1]
    experts = lax.axis_size(EXPERT)

    def body(down_ref, own_ref, rows_ref, *refs):
        me, group = lax.axis_index(EXPERT), lax.axis_index("dp")

        def step(first, batch):
            here = pl.ds(first, batch)
            lefts = [ref[here, :] for ref in refs[:-1]]
            if swapped:
                half = count // 2
                lefts = [jnp.concatenate([left[half:], left[:half]]) for left in lefts]
            table = rows_ref[here, rows.shape[1] - LANES :].astype(jnp.float32)
            lane = lax.broadcasted_iota(jnp.int32, table.shape, 1)
            mine = (lax.rem(lane, experts) == me) & (lane < 3 * experts)
            scale = jnp.sum(jnp.where(mine, table, 0.0), axis=1, keepdims=True)
            tile = min(2 * TILE, width)
            for i in range(0, width, tile):
                cut = slice(i, i + tile)
                total = own_ref[index, here, cut]
                for mask, left in enumerate(lefts, 1):
                    start = pl.multiple_of((group ^ mask) * units, LANES)
                    right = down_ref[pl.ds(start, units), cut]
                    total = total + jnp.dot(left, right, preferred_element_type=jnp.float32)
                total = total.astype(jnp.bfloat16).astype(jnp.float32) * scale
                refs[-1][here, cut] = total.astype(kind)

        row_batches(count, step)

    return pl.pallas_call(
        body,
        out_shape=jax.ShapeDtypeStruct((count, width), kind),
        in_specs=[pl.BlockSpec(memory_space=pltpu.VMEM)] * (3 + len(parts)),
        out_specs=pl.BlockSpec(memory_space=pltpu.VMEM),
        cost_estimate=pl.CostEstimate(flops=0, bytes_accessed=count * width, transcendentals=0),
        compiler_params=pltpu.CompilerParams(
            vmem_limit_bytes=16 * count * width + (6 << 20) + rows.nbytes
        ),
        name="contract_others",
    )(in_vmem(w_down), own, rows, *parts)


def add_and_order(total, received, wide, high):
    count, width = received.shape
    blocks = 4 * wide * high
    tokens, far_size = count // blocks, 2 * high

    def body(total_ref, received_ref, out_ref):
        group, far = lax.axis_index("dp"), lax.axis_index("far")
        for i in range(blocks):
            x, y, w, h = i // (blocks // 2), i // (wide * high) % 2, i // high % wide, i % high
            slot = (group ^ (x + 2 * w)) * far_size + (far ^ (y + 2 * h))
            here = slice(i * tokens, (i + 1) * tokens)
            value = total_ref[here, :] + received_ref[here, :].astype(jnp.float32)
            out_ref[slot] = value.astype(out_ref.dtype)

    return pl.pallas_call(
        body,
        out_shape=jax.ShapeDtypeStruct((blocks, tokens, width), received.dtype),
        in_specs=[pl.BlockSpec(memory_space=pltpu.VMEM)] * 2,
        out_specs=pl.BlockSpec(memory_space=pltpu.VMEM),
        compiler_params=pltpu.CompilerParams(vmem_limit_bytes=12 * total.size + (6 << 20)),
        name="add_and_order",
    )(total, received)


def local(tokens, expert_ids, gate_probs, w_gate, w_up, w_down):
    token_count, width = tokens.shape
    groups, experts = lax.axis_size("dp"), lax.axis_size(EXPERT)
    wide, high = groups // 2, experts // 4

    block = pack_block(tokens, expert_ids, gate_probs, experts)
    units = w_up.shape[2]
    weights = lax.optimization_barrier((block, w_gate[0], w_up[0], w_down[0]))
    block, gate_weights, up_weights, down_weights = weights
    near = stack_blocks([block] + [swap(block, 0, 4 * i) for i in range(1, high)])
    if wide > 1:
        near = jnp.concatenate([near] + [swap(near, 2 * i, 0) for i in range(1, wide)])
    chip = [near, swap(near, 0, 2), swap(near, 1, 0), swap(near, 1, 2)]
    chip = jnp.concatenate(chip)

    swapped = groups == 2 and chip.shape[0] <= BATCH

    def from_group(value, mask, as_sent):
        value = swap(value, mask, 0)
        if as_sent:
            return value
        value = value.reshape(2, 2, wide, high * token_count, units)
        value = jnp.stack([value[i ^ (mask & 1)] for i in range(2)])
        value = jnp.stack([value[:, :, i ^ (mask >> 1)] for i in range(wide)], axis=2)
        return value.reshape(-1, units)

    halves = [chip, swap(chip, 0, 1)]
    first = expand_rows(halves[0], gate_weights, up_weights)
    first, halves[1] = lax.optimization_barrier((first, halves[1]))
    hidden = [first, expand_rows(halves[1], gate_weights, up_weights)]
    others = [
        [from_group(value, mask, swapped and i == 1) for mask in range(1, groups)]
        for i, value in enumerate(hidden)
    ]
    others = lax.optimization_barrier(others)
    own = contract_own(hidden, down_weights)
    kept, sent = (
        contract_others(
            others[i], down_weights, own, i, halves[i], kind, swapped and i == 1
        )
        for i, kind in enumerate((jnp.float32, jnp.bfloat16))
    )

    columns = w_down.shape[2]
    blocks = add_and_order(kept, swap(sent, 0, 1), wide, high)
    blocks = lax.all_to_all(blocks, ("dp", "far"), split_axis=0, concat_axis=0, tiled=True)
    blocks = blocks.reshape(groups, -1, token_count, columns).astype(jnp.float32)
    combined = jnp.sum(blocks, axis=1).astype(jnp.bfloat16)
    return combined.transpose(1, 0, 2).reshape(token_count, width)


def solution(mesh):
    groups, experts = mesh.devices.shape
    split = Mesh(mesh.devices.reshape(groups, experts // 2, 2), ("dp", "far", "core"))
    row, expert = P(("dp", "far", "core"), None), P(EXPERT, None, "dp")
    return jax.shard_map(
        local,
        mesh=split,
        in_specs=(row, row, row, expert, expert, expert),
        out_specs=row,
        check_vma=False,
    )
```

```python
import jax
import jax.numpy as jnp
from jax import lax
from jax.experimental import pallas as pl
from jax.experimental.pallas import tpu as pltpu
from jax.sharding import Mesh
from jax.sharding import PartitionSpec as P

CHUNKS = 2
TILE = 256
BATCH = 128
LANES = 128
EXPERT = ("far", "core")


def swap(value, group_mask, expert_mask):
    groups, experts = lax.axis_size("dp"), lax.axis_size(EXPERT)
    pairs = [
        (g * experts + e, (g ^ group_mask) * experts + (e ^ expert_mask))
        for g in range(groups)
        for e in range(experts)
    ]
    return lax.ppermute(value, ("dp",) + EXPERT, pairs)


def in_vmem(value):
    return pltpu.with_memory_space_constraint(value, pltpu.VMEM)


def in_hbm(value):
    return pltpu.with_memory_space_constraint(value, pltpu.HBM)


def row_batches(count, step):
    batch = min(BATCH, count)
    if count == batch:
        step(0, batch)
    else:

        @pl.loop(0, count // batch)
        def _(i):
            step(pl.multiple_of(i * batch, batch), batch)


def pack_block(tokens, expert_ids, gate_probs, experts):
    count, width = tokens.shape
    top = expert_ids.shape[1]

    def body(tokens_ref, ids_ref, probs_ref, block_ref):
        block_ref[:, :width] = tokens_ref[...]
        lane = lax.broadcasted_iota(jnp.int32, (count, LANES), 1)
        table = jnp.zeros((count, LANES), jnp.float32)
        for k in range(top):
            hit = ids_ref[:, k : k + 1] == lax.rem(lane, experts)
            table = jnp.where(hit, probs_ref[:, k : k + 1], table)
        packed = jnp.zeros((count, LANES), jnp.float32)
        for i in range(3):
            part = table.astype(jnp.bfloat16).astype(jnp.float32)
            packed = jnp.where(lane // experts == i, part, packed)
            table = table - part
        block_ref[:, width:] = packed.astype(block_ref.dtype)

    return pl.pallas_call(
        body,
        out_shape=jax.ShapeDtypeStruct((count, width + LANES), tokens.dtype),
        in_specs=[pl.BlockSpec(memory_space=pltpu.VMEM)] * 3,
        out_specs=pl.BlockSpec(memory_space=pltpu.VMEM),
        cost_estimate=pl.CostEstimate(flops=60 * 10**9, bytes_accessed=0, transcendentals=0),
        compiler_params=pltpu.CompilerParams(vmem_limit_bytes=1 << 20),
        name="pack_block",
    )(in_hbm(tokens), in_hbm(expert_ids), in_hbm(gate_probs))


def stack_blocks(blocks):
    def body(*refs):
        for i, ref in enumerate(refs[:-2]):
            refs[-2][i] = ref[...]
            if i:
                refs[-1][i - 1] = ref[...]

    count, shape, dtype = len(blocks), blocks[0].shape, blocks[0].dtype
    return pl.pallas_call(
        body,
        out_shape=[jax.ShapeDtypeStruct((n,) + shape, dtype) for n in (count, count - 1)],
        in_specs=[pl.BlockSpec(memory_space=pltpu.VMEM)] * count,
        out_specs=[pl.BlockSpec(memory_space=pltpu.VMEM)] * 2,
        compiler_params=pltpu.CompilerParams(vmem_limit_bytes=4 << 20),
        name="stack_blocks",
    )(*blocks)


def join_rows(stacks):
    _, tokens, width = stacks[0].shape
    total = sum(1 if stack.ndim == 2 else stack.shape[0] for stack in stacks)
    batch = max(1, 16 // tokens)

    def body(*refs):
        group, start = [], 0
        for ref, stack in zip(refs, stacks):
            for i in range(1 if stack.ndim == 2 else stack.shape[0]):
                value = ref[...] if stack.ndim == 2 else ref[i]
                group.append(value.astype(jnp.float32))
                if len(group) == batch:
                    rows = jnp.concatenate(group).astype(refs[-1].dtype)
                    refs[-1][start : start + batch * tokens, :] = rows
                    group, start = [], start + batch * tokens

    return pl.pallas_call(
        body,
        out_shape=jax.ShapeDtypeStruct((total * tokens, width), stacks[0].dtype),
        in_specs=[pl.BlockSpec(memory_space=pltpu.VMEM)] * len(stacks),
        out_specs=pl.BlockSpec(memory_space=pltpu.VMEM),
        compiler_params=pltpu.CompilerParams(
            vmem_limit_bytes=5 * total * tokens * width + (4 << 20)
        ),
        name="join_rows",
    )(*stacks)


def expand_rows(rows, w_gate, w_up, start, columns):
    count, depth = rows.shape[0], w_gate.shape[0]

    def body(rows_ref, gate_ref, up_ref, hidden_ref):
        def step(first, batch):
            x = rows_ref[pl.ds(first, batch), :depth]
            tile = min(TILE, columns)
            for i in range(0, columns, tile):
                cut = slice(start + i, start + i + tile)
                gate = jnp.dot(x, gate_ref[:, cut], preferred_element_type=jnp.float32)
                up = jnp.dot(x, up_ref[:, cut], preferred_element_type=jnp.float32)
                value = gate / (1.0 + jnp.exp(-gate)) * up
                hidden_ref[pl.ds(first, batch), i : i + tile] = value.astype(hidden_ref.dtype)

        row_batches(count, step)

    return pl.pallas_call(
        body,
        out_shape=jax.ShapeDtypeStruct((count, columns), rows.dtype),
        in_specs=[pl.BlockSpec(memory_space=pltpu.VMEM)] * 3,
        out_specs=pl.BlockSpec(memory_space=pltpu.VMEM),
        cost_estimate=pl.CostEstimate(flops=0, bytes_accessed=count * columns, transcendentals=0),
        compiler_params=pltpu.CompilerParams(vmem_limit_bytes=rows.nbytes + (6 << 20)),
        name="expand_rows",
    )(rows, in_vmem(w_gate), in_vmem(w_up))


def contract_hidden(
    parts, w_down, units, before=None, rows=None, half=None, index=None, kind=jnp.float32
):
    total_count, width = parts[0][0].shape[0], w_down.shape[1]
    count = total_count if index is None else total_count // 2
    offset = 0 if index is None else index * count
    experts = lax.axis_size(EXPERT)
    operands = [part for part, _, _ in parts] + [in_vmem(w_down)]
    operands += [value for value in (before, rows) if value is not None]

    def body(*refs):
        part_refs, down_ref = refs[: len(parts)], refs[len(parts)]
        rest = list(refs[len(parts) + 1 : -1])
        before_ref = rest.pop(0) if before is not None else None
        rows_ref = rest.pop(0) if rows is not None else None
        me, group = lax.axis_index(EXPERT), lax.axis_index("dp")

        def step(first, batch):
            here = pl.ds(offset + first, batch)
            lefts = [ref[here, :] for ref in part_refs]
            if half is not None:
                order = [i ^ 1 for i in range(count // half)]
                lefts = [
                    jnp.concatenate([left[i * half : (i + 1) * half] for i in order])
                    for left in lefts
                ]
            if rows is not None:
                table = rows_ref[here, rows.shape[1] - LANES :].astype(jnp.float32)
                lane = lax.broadcasted_iota(jnp.int32, table.shape, 1)
                mine = (lax.rem(lane, experts) == me) & (lane < 3 * experts)
                scale = jnp.sum(jnp.where(mine, table, 0.0), axis=1, keepdims=True)
            tile = min(2 * TILE, width)
            for i in range(0, width, tile):
                cut = slice(i, i + tile)
                total = 0.0 if before is None else before_ref[here, cut]
                for left, (_, mask, unit) in zip(lefts, parts):
                    start = pl.multiple_of((group ^ mask) * units + unit, LANES)
                    right = down_ref[pl.ds(start, left.shape[1]), cut]
                    total = total + jnp.dot(left, right, preferred_element_type=jnp.float32)
                if rows is not None:
                    total = total.astype(jnp.bfloat16).astype(jnp.float32) * scale
                refs[-1][pl.ds(first, batch), cut] = total.astype(kind)

        row_batches(count, step)

    return pl.pallas_call(
        body,
        out_shape=jax.ShapeDtypeStruct((count, width), kind),
        in_specs=[pl.BlockSpec(memory_space=pltpu.VMEM)] * len(operands),
        out_specs=pl.BlockSpec(memory_space=pltpu.VMEM),
        cost_estimate=pl.CostEstimate(flops=0, bytes_accessed=count * width, transcendentals=0),
        compiler_params=pltpu.CompilerParams(
            vmem_limit_bytes=8 * total_count * width
            + (6 << 20)
            + (0 if rows is None else rows.nbytes)
        ),
        name="contract_hidden",
    )(*operands)


def add_and_order(total, received, wide, high):
    count, width = received.shape
    blocks = 4 * wide * high
    tokens, far_size = count // blocks, 2 * high

    def body(total_ref, received_ref, out_ref):
        group, far = lax.axis_index("dp"), lax.axis_index("far")
        for i in range(blocks):
            x, y, w, h = i // (blocks // 2), i // (wide * high) % 2, i // high % wide, i % high
            slot = (group ^ (x + 2 * w)) * far_size + (far ^ (y + 2 * h))
            here = slice(i * tokens, (i + 1) * tokens)
            value = total_ref[here, :] + received_ref[here, :].astype(jnp.float32)
            out_ref[slot] = value.astype(out_ref.dtype)

    return pl.pallas_call(
        body,
        out_shape=jax.ShapeDtypeStruct((blocks, tokens, width), received.dtype),
        in_specs=[pl.BlockSpec(memory_space=pltpu.VMEM)] * 2,
        out_specs=pl.BlockSpec(memory_space=pltpu.VMEM),
        compiler_params=pltpu.CompilerParams(vmem_limit_bytes=12 * total.size + (6 << 20)),
        name="add_and_order",
    )(total, received)


def local(tokens, expert_ids, gate_probs, w_gate, w_up, w_down):
    token_count, width = tokens.shape
    groups, experts = lax.axis_size("dp"), lax.axis_size(EXPERT)
    wide, high = groups // 2, experts // 4

    block = pack_block(tokens, expert_ids, gate_probs, experts)
    units = w_up.shape[2]
    weights = lax.optimization_barrier((block, w_gate[0], w_up[0], w_down[0]))
    block, gate_weights, up_weights, down_weights = weights
    near = [block] + [swap(block, 0, 4 * i) for i in range(1, high)]
    early = swap(block, 1, 2)
    near[-1], early = lax.optimization_barrier((near[-1], early))
    near, rest = stack_blocks(near)
    if wide > 1:
        near = jnp.concatenate([near] + [swap(near, 2 * i, 0) for i in range(1, wide)])
        rest = near[1:]
    chip = join_rows([near, swap(near, 0, 2), swap(near, 1, 0), early, swap(rest, 1, 2)])
    rows = jnp.concatenate([chip, swap(chip, 0, 1)])

    chunks = CHUNKS if units % (LANES * CHUNKS) == 0 else 1
    step = units // chunks
    half = rows.shape[0] // 4 if groups == 2 and rows.shape[0] <= BATCH else None

    def from_group(value, mask):
        value = swap(value, mask, 0)
        if half is not None:
            return value
        value = value.reshape(2, 2, 2, wide, high * token_count, step)
        value = jnp.stack([value[:, i ^ (mask & 1)] for i in range(2)], axis=1)
        value = jnp.stack([value[:, :, :, i ^ (mask >> 1)] for i in range(wide)], axis=3)
        return value.reshape(-1, step)

    hidden, others = [], []
    for i in range(chunks):
        if hidden:
            rows, hidden[-1] = lax.optimization_barrier((rows, hidden[-1]))
        hidden.append(expand_rows(rows, gate_weights, up_weights, i * step, step))
        others.append(
            [(from_group(hidden[-1], mask), mask, i * step) for mask in range(1, groups)]
        )
    parts = [(value, 0, i * step) for i, value in enumerate(hidden)]
    total = contract_hidden(parts, down_weights, units)
    for i in range(chunks - 1):
        total = contract_hidden(others[i], down_weights, units, total, half=half)
    last = lambda index, kind: contract_hidden(
        others[-1], down_weights, units, total, rows, half, index, kind
    )
    sent, kept = last(1, jnp.bfloat16), last(0, jnp.float32)

    columns = w_down.shape[2]
    blocks = add_and_order(kept, swap(sent, 0, 1), wide, high)
    blocks = lax.all_to_all(blocks, ("dp", "far"), split_axis=0, concat_axis=0, tiled=True)
    blocks = blocks.reshape(groups, -1, token_count, columns).astype(jnp.float32)
    combined = jnp.sum(blocks, axis=1).astype(jnp.bfloat16)
    return combined.transpose(1, 0, 2).reshape(token_count, width)


def solution(mesh):
    groups, experts = mesh.devices.shape
    split = Mesh(mesh.devices.reshape(groups, experts // 2, 2), ("dp", "far", "core"))
    row, expert = P(("dp", "far", "core"), None), P(EXPERT, None, "dp")
    return jax.shard_map(
        local,
        mesh=split,
        in_specs=(row, row, row, expert, expert, expert),
        out_specs=row,
        check_vma=False,
    )
```

```python
import jax
import jax.numpy as jnp
from jax import lax
from jax.experimental import pallas as pl
from jax.experimental.pallas import tpu as pltpu
from jax.sharding import Mesh
from jax.sharding import PartitionSpec as P

CHUNKS = 2
TILE = 256
BATCH = 128
LANES = 128
EXPERT = ("far", "core")


def swap(value, group_mask, expert_mask):
    groups, experts = lax.axis_size("dp"), lax.axis_size(EXPERT)
    pairs = [
        (g * experts + e, (g ^ group_mask) * experts + (e ^ expert_mask))
        for g in range(groups)
        for e in range(experts)
    ]
    return lax.ppermute(value, ("dp",) + EXPERT, pairs)


def in_vmem(value):
    return pltpu.with_memory_space_constraint(value, pltpu.VMEM)


def in_hbm(value):
    return pltpu.with_memory_space_constraint(value, pltpu.HBM)


def row_batches(count, step):
    batch = min(BATCH, count)
    if count == batch:
        step(0, batch)
    else:

        @pl.loop(0, count // batch)
        def _(i):
            step(pl.multiple_of(i * batch, batch), batch)


def pack_block(tokens, expert_ids, gate_probs, experts):
    count, width = tokens.shape
    top = expert_ids.shape[1]

    def body(tokens_ref, ids_ref, probs_ref, block_ref):
        block_ref[:, :width] = tokens_ref[...]
        lane = lax.broadcasted_iota(jnp.int32, (count, LANES), 1)
        table = jnp.zeros((count, LANES), jnp.float32)
        for k in range(top):
            hit = ids_ref[:, k : k + 1] == lax.rem(lane, experts)
            table = jnp.where(hit, probs_ref[:, k : k + 1], table)
        packed = jnp.zeros((count, LANES), jnp.float32)
        for i in range(3):
            part = table.astype(jnp.bfloat16).astype(jnp.float32)
            packed = jnp.where(lane // experts == i, part, packed)
            table = table - part
        block_ref[:, width:] = packed.astype(block_ref.dtype)

    return pl.pallas_call(
        body,
        out_shape=jax.ShapeDtypeStruct((count, width + LANES), tokens.dtype),
        in_specs=[pl.BlockSpec(memory_space=pltpu.VMEM)] * 3,
        out_specs=pl.BlockSpec(memory_space=pltpu.VMEM),
        cost_estimate=pl.CostEstimate(flops=60 * 10**9, bytes_accessed=0, transcendentals=0),
        compiler_params=pltpu.CompilerParams(vmem_limit_bytes=1 << 20),
        name="pack_block",
    )(in_hbm(tokens), in_hbm(expert_ids), in_hbm(gate_probs))


def stack_blocks(blocks):
    def body(*refs):
        for i, ref in enumerate(refs[:-1]):
            refs[-1][i] = ref[...]

    return pl.pallas_call(
        body,
        out_shape=jax.ShapeDtypeStruct((len(blocks),) + blocks[0].shape, blocks[0].dtype),
        in_specs=[pl.BlockSpec(memory_space=pltpu.VMEM)] * len(blocks),
        out_specs=pl.BlockSpec(memory_space=pltpu.VMEM),
        compiler_params=pltpu.CompilerParams(vmem_limit_bytes=4 << 20),
        name="stack_blocks",
    )(*blocks)


def join_rows(stacks):
    blocks, tokens, width = stacks[0].shape
    total = len(stacks) * blocks
    batch = max(1, 16 // tokens)

    def body(*refs):
        for i in range(0, total, batch):
            group = [refs[j // blocks][j % blocks] for j in range(i, i + batch)]
            rows = jnp.concatenate([value.astype(jnp.float32) for value in group])
            refs[-1][i * tokens : (i + batch) * tokens, :] = rows.astype(refs[-1].dtype)

    return pl.pallas_call(
        body,
        out_shape=jax.ShapeDtypeStruct((total * tokens, width), stacks[0].dtype),
        in_specs=[pl.BlockSpec(memory_space=pltpu.VMEM)] * len(stacks),
        out_specs=pl.BlockSpec(memory_space=pltpu.VMEM),
        compiler_params=pltpu.CompilerParams(
            vmem_limit_bytes=5 * total * tokens * width + (4 << 20)
        ),
        name="join_rows",
    )(*stacks)


def expand_rows(rows, w_gate, w_up, start, columns):
    count, depth = rows.shape[0], w_gate.shape[0]

    def body(rows_ref, gate_ref, up_ref, hidden_ref):
        def step(first, batch):
            x = rows_ref[pl.ds(first, batch), :depth]
            tile = min(TILE, columns)
            for i in range(0, columns, tile):
                cut = slice(start + i, start + i + tile)
                gate = jnp.dot(x, gate_ref[:, cut], preferred_element_type=jnp.float32)
                up = jnp.dot(x, up_ref[:, cut], preferred_element_type=jnp.float32)
                value = gate / (1.0 + jnp.exp(-gate)) * up
                hidden_ref[pl.ds(first, batch), i : i + tile] = value.astype(hidden_ref.dtype)

        row_batches(count, step)

    return pl.pallas_call(
        body,
        out_shape=jax.ShapeDtypeStruct((count, columns), rows.dtype),
        in_specs=[pl.BlockSpec(memory_space=pltpu.VMEM)] * 3,
        out_specs=pl.BlockSpec(memory_space=pltpu.VMEM),
        cost_estimate=pl.CostEstimate(flops=0, bytes_accessed=count * columns, transcendentals=0),
        compiler_params=pltpu.CompilerParams(vmem_limit_bytes=rows.nbytes + (6 << 20)),
        name="expand_rows",
    )(rows, in_vmem(w_gate), in_vmem(w_up))


def contract_hidden(
    parts, w_down, units, before=None, rows=None, half=None, index=None, kind=jnp.float32
):
    total_count, width = parts[0][0].shape[0], w_down.shape[1]
    count = total_count if index is None else total_count // 2
    offset = 0 if index is None else index * count
    experts = lax.axis_size(EXPERT)
    operands = [part for part, _, _ in parts] + [in_vmem(w_down)]
    operands += [value for value in (before, rows) if value is not None]

    def body(*refs):
        part_refs, down_ref = refs[: len(parts)], refs[len(parts)]
        rest = list(refs[len(parts) + 1 : -1])
        before_ref = rest.pop(0) if before is not None else None
        rows_ref = rest.pop(0) if rows is not None else None
        me, group = lax.axis_index(EXPERT), lax.axis_index("dp")

        def step(first, batch):
            here = pl.ds(offset + first, batch)
            lefts = [ref[here, :] for ref in part_refs]
            if half is not None:
                order = [i ^ 1 for i in range(count // half)]
                lefts = [
                    jnp.concatenate([left[i * half : (i + 1) * half] for i in order])
                    for left in lefts
                ]
            if rows is not None:
                table = rows_ref[here, rows.shape[1] - LANES :].astype(jnp.float32)
                lane = lax.broadcasted_iota(jnp.int32, table.shape, 1)
                mine = (lax.rem(lane, experts) == me) & (lane < 3 * experts)
                scale = jnp.sum(jnp.where(mine, table, 0.0), axis=1, keepdims=True)
            tile = min(2 * TILE, width)
            for i in range(0, width, tile):
                cut = slice(i, i + tile)
                total = 0.0 if before is None else before_ref[here, cut]
                for left, (_, mask, unit) in zip(lefts, parts):
                    start = pl.multiple_of((group ^ mask) * units + unit, LANES)
                    right = down_ref[pl.ds(start, left.shape[1]), cut]
                    total = total + jnp.dot(left, right, preferred_element_type=jnp.float32)
                if rows is not None:
                    total = total.astype(jnp.bfloat16).astype(jnp.float32) * scale
                refs[-1][pl.ds(first, batch), cut] = total.astype(kind)

        row_batches(count, step)

    return pl.pallas_call(
        body,
        out_shape=jax.ShapeDtypeStruct((count, width), kind),
        in_specs=[pl.BlockSpec(memory_space=pltpu.VMEM)] * len(operands),
        out_specs=pl.BlockSpec(memory_space=pltpu.VMEM),
        cost_estimate=pl.CostEstimate(flops=0, bytes_accessed=count * width, transcendentals=0),
        compiler_params=pltpu.CompilerParams(
            vmem_limit_bytes=8 * total_count * width
            + (6 << 20)
            + (0 if rows is None else rows.nbytes)
        ),
        name="contract_hidden",
    )(*operands)


def sum_stage(inputs, plan, shape, dtype):
    def body(*refs):
        sources, targets = refs[: len(inputs)], refs[len(inputs) :]
        for target, blocks in zip(targets, plan):
            for i, block in enumerate(blocks):
                total = 0.0
                for ref in sources:
                    if len(ref.shape) == 2:
                        value = ref[block * shape[0] : (block + 1) * shape[0], :]
                    else:
                        value = ref[block]
                    total = total + value.astype(jnp.float32)
                target[i] = total.astype(target.dtype)

    return pl.pallas_call(
        body,
        out_shape=[
            jax.ShapeDtypeStruct((len(blocks),) + shape, dtype if i else jnp.float32)
            for i, blocks in enumerate(plan)
        ],
        in_specs=[pl.BlockSpec(memory_space=pltpu.VMEM)] * len(inputs),
        out_specs=[pl.BlockSpec(memory_space=pltpu.VMEM)] * len(plan),
        compiler_params=pltpu.CompilerParams(
            vmem_limit_bytes=sum(value.nbytes for value in inputs) * 2 + (6 << 20)
        ),
        name="sum_stage",
    )(*inputs)


def finish(sums, groups, dtype):
    tokens, columns = sums[0][0].shape[1:]
    flat = [value for parts in sums for value in parts]

    def body(*refs):
        group = lax.axis_index("dp")
        refs, out_ref = list(refs[:-1]), refs[-1]
        for i, parts in enumerate(sums):
            total = sum(refs.pop(0)[0].astype(jnp.float32) for _ in parts)
            start = pl.multiple_of((group ^ i) * columns, LANES)
            out_ref[:, pl.ds(start, columns)] = total.astype(dtype)

    return pl.pallas_call(
        body,
        out_shape=jax.ShapeDtypeStruct((tokens, groups * columns), dtype),
        in_specs=[pl.BlockSpec(memory_space=pltpu.VMEM)] * len(flat),
        out_specs=pl.BlockSpec(memory_space=pltpu.VMEM),
        compiler_params=pltpu.CompilerParams(vmem_limit_bytes=4 << 20),
        name="finish",
    )(*flat)


def local(tokens, expert_ids, gate_probs, w_gate, w_up, w_down):
    token_count, width = tokens.shape
    groups, experts = lax.axis_size("dp"), lax.axis_size(EXPERT)
    wide, high = groups // 2, experts // 4

    block = pack_block(tokens, expert_ids, gate_probs, experts)
    units = w_up.shape[2]
    weights = lax.optimization_barrier((block, w_gate[0], w_up[0], w_down[0]))
    block, gate_weights, up_weights, down_weights = weights
    near = stack_blocks([block] + [swap(block, 0, 4 * i) for i in range(1, high)])
    if wide > 1:
        near = jnp.concatenate([near] + [swap(near, 2 * i, 0) for i in range(1, wide)])
    chip = join_rows([near, swap(near, 0, 2), swap(near, 1, 0), swap(near, 1, 2)])
    rows = jnp.concatenate([chip, swap(chip, 0, 1)])

    chunks = CHUNKS if units % (LANES * CHUNKS) == 0 else 1
    step = units // chunks
    half = rows.shape[0] // 4 if groups == 2 and rows.shape[0] <= BATCH else None

    def from_group(value, mask):
        value = swap(value, mask, 0)
        if half is not None:
            return value
        value = value.reshape(2, 2, 2, wide, high * token_count, step)
        value = jnp.stack([value[:, i ^ (mask & 1)] for i in range(2)], axis=1)
        value = jnp.stack([value[:, :, :, i ^ (mask >> 1)] for i in range(wide)], axis=3)
        return value.reshape(-1, step)

    hidden, others = [], []
    for i in range(chunks):
        if hidden:
            rows, hidden[-1] = lax.optimization_barrier((rows, hidden[-1]))
        hidden.append(expand_rows(rows, gate_weights, up_weights, i * step, step))
        others.append(
            [(from_group(hidden[-1], mask), mask, i * step) for mask in range(1, groups)]
        )
    parts = [(value, 0, i * step) for i, value in enumerate(hidden)]
    total = contract_hidden(parts, down_weights, units)
    for i in range(chunks - 1):
        total = contract_hidden(others[i], down_weights, units, total, half=half)
    last = lambda index, kind: contract_hidden(
        others[-1], down_weights, units, total, rows, half, index, kind
    )
    sent, kept = last(1, jnp.bfloat16), last(0, jnp.float32)

    shape = (token_count, w_down.shape[2])
    rest = [(g, h) for g in range(groups) for h in range(0, high, 2)]
    slot = lambda g, y, h: (((g & 1) * 2 + y) * wide + (g >> 1)) * high + h
    plan = [[slot(g, y, h + z) for g, h in rest] for y, z in ((0, 0), (1, 0), (0, 1), (1, 1))]
    mine, *away = sum_stage([kept, swap(sent, 0, 1)], plan, shape, jnp.bfloat16)
    inputs = [mine] + [swap(value, 0, mask) for value, mask in zip(away, (2, 4, 6))]
    mine, *away = sum_stage(inputs, [[i] for i in range(len(rest))], shape, jnp.bfloat16)
    sums = [[] for _ in range(groups)]
    sums[0].append(mine)
    for value, (g, h) in zip(away, rest[1:]):
        sums[g].append(swap(value, g, 4 * h))
    return finish(sums, groups, tokens.dtype)


def solution(mesh):
    groups, experts = mesh.devices.shape
    split = Mesh(mesh.devices.reshape(groups, experts // 2, 2), ("dp", "far", "core"))
    row, expert = P(("dp", "far", "core"), None), P(EXPERT, None, "dp")
    return jax.shard_map(
        local,
        mesh=split,
        in_specs=(row, row, row, expert, expert, expert),
        out_specs=row,
        check_vma=False,
    )
```

```python
import jax
import jax.numpy as jnp
from jax import lax
from jax.experimental import pallas as pl
from jax.experimental.pallas import tpu as pltpu
from jax.sharding import Mesh
from jax.sharding import PartitionSpec as P

CHUNKS = 2
TILE = 256
BATCH = 128
LANES = 128
EXPERT = ("far", "near", "core")


def swap(value, group_mask, expert_mask):
    groups, experts = lax.axis_size("dp"), lax.axis_size(EXPERT)
    pairs = [
        (g * experts + e, (g ^ group_mask) * experts + (e ^ expert_mask))
        for g in range(groups)
        for e in range(experts)
    ]
    return lax.ppermute(value, ("dp",) + EXPERT, pairs)


def in_vmem(value):
    return pltpu.with_memory_space_constraint(value, pltpu.VMEM)


def in_hbm(value):
    return pltpu.with_memory_space_constraint(value, pltpu.HBM)


def row_batches(count, step):
    batch = min(BATCH, count)
    if count == batch:
        step(0, batch)
    else:

        @pl.loop(0, count // batch)
        def _(i):
            step(pl.multiple_of(i * batch, batch), batch)


def pack_block(tokens, expert_ids, gate_probs, experts):
    count, width = tokens.shape
    top = expert_ids.shape[1]

    def body(tokens_ref, ids_ref, probs_ref, block_ref):
        block_ref[:, :width] = tokens_ref[...]
        lane = lax.broadcasted_iota(jnp.int32, (count, LANES), 1)
        table = jnp.zeros((count, LANES), jnp.float32)
        for k in range(top):
            hit = ids_ref[:, k : k + 1] == lax.rem(lane, experts)
            table = jnp.where(hit, probs_ref[:, k : k + 1], table)
        packed = jnp.zeros((count, LANES), jnp.float32)
        for i in range(3):
            part = table.astype(jnp.bfloat16).astype(jnp.float32)
            packed = jnp.where(lane // experts == i, part, packed)
            table = table - part
        block_ref[:, width:] = packed.astype(block_ref.dtype)

    return pl.pallas_call(
        body,
        out_shape=jax.ShapeDtypeStruct((count, width + LANES), tokens.dtype),
        in_specs=[pl.BlockSpec(memory_space=pltpu.VMEM)] * 3,
        out_specs=pl.BlockSpec(memory_space=pltpu.VMEM),
        cost_estimate=pl.CostEstimate(flops=60 * 10**9, bytes_accessed=0, transcendentals=0),
        compiler_params=pltpu.CompilerParams(vmem_limit_bytes=1 << 20),
        name="pack_block",
    )(in_hbm(tokens), in_hbm(expert_ids), in_hbm(gate_probs))


def stack_blocks(blocks):
    def body(*refs):
        for i, ref in enumerate(refs[:-1]):
            refs[-1][i] = ref[...]

    return pl.pallas_call(
        body,
        out_shape=jax.ShapeDtypeStruct((len(blocks),) + blocks[0].shape, blocks[0].dtype),
        in_specs=[pl.BlockSpec(memory_space=pltpu.VMEM)] * len(blocks),
        out_specs=pl.BlockSpec(memory_space=pltpu.VMEM),
        compiler_params=pltpu.CompilerParams(vmem_limit_bytes=4 << 20),
        name="stack_blocks",
    )(*blocks)


def join_rows(stacks):
    blocks, tokens, width = stacks[0].shape
    total = len(stacks) * blocks
    batch = max(1, 16 // tokens)

    def body(*refs):
        for i in range(0, total, batch):
            group = [refs[j // blocks][j % blocks] for j in range(i, i + batch)]
            rows = jnp.concatenate([value.astype(jnp.float32) for value in group])
            refs[-1][i * tokens : (i + batch) * tokens, :] = rows.astype(refs[-1].dtype)

    return pl.pallas_call(
        body,
        out_shape=jax.ShapeDtypeStruct((total * tokens, width), stacks[0].dtype),
        in_specs=[pl.BlockSpec(memory_space=pltpu.VMEM)] * len(stacks),
        out_specs=pl.BlockSpec(memory_space=pltpu.VMEM),
        compiler_params=pltpu.CompilerParams(
            vmem_limit_bytes=5 * total * tokens * width + (4 << 20)
        ),
        name="join_rows",
    )(*stacks)


def expand_rows(rows, w_gate, w_up, start, columns):
    count, depth = rows.shape[0], w_gate.shape[0]

    def body(rows_ref, gate_ref, up_ref, hidden_ref):
        def step(first, batch):
            x = rows_ref[pl.ds(first, batch), :depth]
            tile = min(TILE, columns)
            for i in range(0, columns, tile):
                cut = slice(start + i, start + i + tile)
                gate = jnp.dot(x, gate_ref[:, cut], preferred_element_type=jnp.float32)
                up = jnp.dot(x, up_ref[:, cut], preferred_element_type=jnp.float32)
                value = gate / (1.0 + jnp.exp(-gate)) * up
                hidden_ref[pl.ds(first, batch), i : i + tile] = value.astype(hidden_ref.dtype)

        row_batches(count, step)

    return pl.pallas_call(
        body,
        out_shape=jax.ShapeDtypeStruct((count, columns), rows.dtype),
        in_specs=[pl.BlockSpec(memory_space=pltpu.VMEM)] * 3,
        out_specs=pl.BlockSpec(memory_space=pltpu.VMEM),
        cost_estimate=pl.CostEstimate(flops=0, bytes_accessed=count * columns, transcendentals=0),
        compiler_params=pltpu.CompilerParams(vmem_limit_bytes=rows.nbytes + (6 << 20)),
        name="expand_rows",
    )(rows, in_vmem(w_gate), in_vmem(w_up))


def contract_hidden(
    parts, w_down, units, before=None, rows=None, half=None, index=None, kind=jnp.float32
):
    total_count, width = parts[0][0].shape[0], w_down.shape[1]
    count = total_count if index is None else total_count // 2
    offset = 0 if index is None else index * count
    experts = lax.axis_size(EXPERT)
    operands = [part for part, _, _ in parts] + [in_vmem(w_down)]
    operands += [value for value in (before, rows) if value is not None]

    def body(*refs):
        part_refs, down_ref = refs[: len(parts)], refs[len(parts)]
        rest = list(refs[len(parts) + 1 : -1])
        before_ref = rest.pop(0) if before is not None else None
        rows_ref = rest.pop(0) if rows is not None else None
        me, group = lax.axis_index(EXPERT), lax.axis_index("dp")

        def step(first, batch):
            here = pl.ds(offset + first, batch)
            lefts = [ref[here, :] for ref in part_refs]
            if half is not None:
                order = [i ^ 1 for i in range(count // half)]
                lefts = [
                    jnp.concatenate([left[i * half : (i + 1) * half] for i in order])
                    for left in lefts
                ]
            if rows is not None:
                table = rows_ref[here, rows.shape[1] - LANES :].astype(jnp.float32)
                lane = lax.broadcasted_iota(jnp.int32, table.shape, 1)
                mine = (lax.rem(lane, experts) == me) & (lane < 3 * experts)
                scale = jnp.sum(jnp.where(mine, table, 0.0), axis=1, keepdims=True)
            tile = min(2 * TILE, width)
            for i in range(0, width, tile):
                cut = slice(i, i + tile)
                total = 0.0 if before is None else before_ref[here, cut]
                for left, (_, mask, unit) in zip(lefts, parts):
                    start = pl.multiple_of((group ^ mask) * units + unit, LANES)
                    right = down_ref[pl.ds(start, left.shape[1]), cut]
                    total = total + jnp.dot(left, right, preferred_element_type=jnp.float32)
                if rows is not None:
                    total = total.astype(jnp.bfloat16).astype(jnp.float32) * scale
                refs[-1][pl.ds(first, batch), cut] = total.astype(kind)

        row_batches(count, step)

    return pl.pallas_call(
        body,
        out_shape=jax.ShapeDtypeStruct((count, width), kind),
        in_specs=[pl.BlockSpec(memory_space=pltpu.VMEM)] * len(operands),
        out_specs=pl.BlockSpec(memory_space=pltpu.VMEM),
        cost_estimate=pl.CostEstimate(flops=0, bytes_accessed=count * width, transcendentals=0),
        compiler_params=pltpu.CompilerParams(
            vmem_limit_bytes=8 * total_count * width
            + (6 << 20)
            + (0 if rows is None else rows.nbytes)
        ),
        name="contract_hidden",
    )(*operands)


def add_blocks(inputs, plan, shape, dtype, ordered):
    def body(*refs):
        group, far = lax.axis_index("dp"), lax.axis_index("far")
        far_size = lax.axis_size("far")
        sources, targets = refs[: len(inputs)], refs[len(inputs) :]
        for target, blocks in zip(targets, plan):
            for i, block in enumerate(blocks):
                total = 0.0
                for ref in sources:
                    if len(ref.shape) == 2:
                        value = ref[block * shape[0] : (block + 1) * shape[0], :]
                    else:
                        value = ref[block]
                    total = total + value.astype(jnp.float32)
                if ordered:
                    i = (group ^ (i // far_size)) * far_size + (far ^ (i % far_size))
                target[i] = total.astype(target.dtype)

    kinds = [dtype if i or ordered else jnp.float32 for i in range(len(plan))]
    return pl.pallas_call(
        body,
        out_shape=[
            jax.ShapeDtypeStruct((len(blocks),) + shape, kind)
            for kind, blocks in zip(kinds, plan)
        ],
        in_specs=[pl.BlockSpec(memory_space=pltpu.VMEM)] * len(inputs),
        out_specs=[pl.BlockSpec(memory_space=pltpu.VMEM)] * len(plan),
        compiler_params=pltpu.CompilerParams(
            vmem_limit_bytes=sum(value.nbytes for value in inputs) * 2 + (6 << 20)
        ),
        name="add_blocks",
    )(*inputs)


def finish(blocks, groups):
    count, tokens, columns = blocks.shape
    parts = count // groups

    def body(blocks_ref, out_ref):
        for g in range(groups):
            total = blocks_ref[g * parts].astype(jnp.float32)
            for i in range(1, parts):
                total = total + blocks_ref[g * parts + i].astype(jnp.float32)
            out_ref[:, g * columns : (g + 1) * columns] = total.astype(out_ref.dtype)

    return pl.pallas_call(
        body,
        out_shape=jax.ShapeDtypeStruct((tokens, groups * columns), blocks.dtype),
        in_specs=[pl.BlockSpec(memory_space=pltpu.VMEM)],
        out_specs=pl.BlockSpec(memory_space=pltpu.VMEM),
        compiler_params=pltpu.CompilerParams(vmem_limit_bytes=blocks.nbytes + (4 << 20)),
        name="finish",
    )(blocks)


def local(tokens, expert_ids, gate_probs, w_gate, w_up, w_down):
    token_count, width = tokens.shape
    groups, experts = lax.axis_size("dp"), lax.axis_size(EXPERT)
    wide, high = groups // 2, experts // 4

    block = pack_block(tokens, expert_ids, gate_probs, experts)
    units = w_up.shape[2]
    weights = lax.optimization_barrier((block, w_gate[0], w_up[0], w_down[0]))
    block, gate_weights, up_weights, down_weights = weights
    near = stack_blocks([block] + [swap(block, 0, 4 * i) for i in range(1, high)])
    if wide > 1:
        near = jnp.concatenate([near] + [swap(near, 2 * i, 0) for i in range(1, wide)])
    chip = join_rows([near, swap(near, 0, 2), swap(near, 1, 0), swap(near, 1, 2)])
    rows = jnp.concatenate([chip, swap(chip, 0, 1)])

    chunks = CHUNKS if units % (LANES * CHUNKS) == 0 else 1
    step = units // chunks
    half = rows.shape[0] // 4 if groups == 2 and rows.shape[0] <= BATCH else None

    def from_group(value, mask):
        value = swap(value, mask, 0)
        if half is not None:
            return value
        value = value.reshape(2, 2, 2, wide, high * token_count, step)
        value = jnp.stack([value[:, i ^ (mask & 1)] for i in range(2)], axis=1)
        value = jnp.stack([value[:, :, :, i ^ (mask >> 1)] for i in range(wide)], axis=3)
        return value.reshape(-1, step)

    hidden, others = [], []
    for i in range(chunks):
        if hidden:
            rows, hidden[-1] = lax.optimization_barrier((rows, hidden[-1]))
        hidden.append(expand_rows(rows, gate_weights, up_weights, i * step, step))
        others.append(
            [(from_group(hidden[-1], mask), mask, i * step) for mask in range(1, groups)]
        )
    parts = [(value, 0, i * step) for i, value in enumerate(hidden)]
    total = contract_hidden(parts, down_weights, units)
    for i in range(chunks - 1):
        total = contract_hidden(others[i], down_weights, units, total, half=half)
    last = lambda index, kind: contract_hidden(
        others[-1], down_weights, units, total, rows, half, index, kind
    )
    sent, kept = last(1, jnp.bfloat16), last(0, jnp.float32)

    shape = (token_count, w_down.shape[2])
    rest = [(g, h) for g in range(groups) for h in range(0, high, 2)]
    slot = lambda g, y, h: (((g & 1) * 2 + y) * wide + (g >> 1)) * high + h
    plan = [[slot(g, y, h + z) for g, h in rest] for y, z in ((0, 0), (1, 1), (0, 1), (1, 0))]
    mine, *away = add_blocks([kept, swap(sent, 0, 1)], plan, shape, jnp.bfloat16, False)
    inputs = [mine] + [swap(value, 0, mask) for value, mask in zip(away, (6, 4, 2))]
    (blocks,) = add_blocks(inputs, [range(len(rest))], shape, jnp.bfloat16, True)
    blocks = lax.all_to_all(blocks, ("dp", "far"), split_axis=0, concat_axis=0, tiled=True)
    return finish(blocks, groups)


def solution(mesh):
    groups, experts = mesh.devices.shape
    split = Mesh(mesh.devices.reshape(groups, experts // 8, 4, 2), ("dp",) + EXPERT)
    row, expert = P(("dp",) + EXPERT, None), P(EXPERT, None, "dp")
    return jax.shard_map(
        local,
        mesh=split,
        in_specs=(row, row, row, expert, expert, expert),
        out_specs=row,
        check_vma=False,
    )
```

```python
import jax
import jax.numpy as jnp
from jax import lax
from jax.experimental import pallas as pl
from jax.experimental.pallas import tpu as pltpu
from jax.sharding import Mesh
from jax.sharding import PartitionSpec as P

CHUNKS = 2
TILE = 256
BATCH = 128
LANES = 128
X, Y = (1, 1), (0, 3)
EXPERT = ("far", "core")


def far(i):
    return (0, 4 * i + bin(i).count("1") % 2)


def both(a, b):
    return (a[0] ^ b[0], a[1] ^ b[1])


def swap(value, masks):
    group_mask, expert_mask = masks
    groups, experts = lax.axis_size("dp"), lax.axis_size(EXPERT)
    pairs = [
        (g * experts + e, (g ^ group_mask) * experts + (e ^ expert_mask))
        for g in range(groups)
        for e in range(experts)
    ]
    return lax.ppermute(value, ("dp",) + EXPERT, pairs)


def in_vmem(value):
    return pltpu.with_memory_space_constraint(value, pltpu.VMEM)


def in_hbm(value):
    return pltpu.with_memory_space_constraint(value, pltpu.HBM)


def row_batches(count, step):
    batch = min(BATCH, count)
    if count == batch:
        step(0, batch)
    else:

        @pl.loop(0, count // batch)
        def _(i):
            step(pl.multiple_of(i * batch, batch), batch)


def pack_block(tokens, expert_ids, gate_probs, experts):
    count, width = tokens.shape
    top = expert_ids.shape[1]

    def body(tokens_ref, ids_ref, probs_ref, block_ref):
        block_ref[:, :width] = tokens_ref[...]
        lane = lax.broadcasted_iota(jnp.int32, (count, LANES), 1)
        table = jnp.zeros((count, LANES), jnp.float32)
        for k in range(top):
            hit = ids_ref[:, k : k + 1] == lax.rem(lane, experts)
            table = jnp.where(hit, probs_ref[:, k : k + 1], table)
        packed = jnp.zeros((count, LANES), jnp.float32)
        for i in range(3):
            part = table.astype(jnp.bfloat16).astype(jnp.float32)
            packed = jnp.where(lane // experts == i, part, packed)
            table = table - part
        block_ref[:, width:] = packed.astype(block_ref.dtype)

    return pl.pallas_call(
        body,
        out_shape=jax.ShapeDtypeStruct((count, width + LANES), tokens.dtype),
        in_specs=[pl.BlockSpec(memory_space=pltpu.VMEM)] * 3,
        out_specs=pl.BlockSpec(memory_space=pltpu.VMEM),
        cost_estimate=pl.CostEstimate(flops=60 * 10**9, bytes_accessed=0, transcendentals=0),
        compiler_params=pltpu.CompilerParams(vmem_limit_bytes=1 << 20),
        name="pack_block",
    )(in_hbm(tokens), in_hbm(expert_ids), in_hbm(gate_probs))


def stack_blocks(blocks):
    def body(*refs):
        for i, ref in enumerate(refs[:-1]):
            refs[-1][i] = ref[...]

    return pl.pallas_call(
        body,
        out_shape=jax.ShapeDtypeStruct((len(blocks),) + blocks[0].shape, blocks[0].dtype),
        in_specs=[pl.BlockSpec(memory_space=pltpu.VMEM)] * len(blocks),
        out_specs=pl.BlockSpec(memory_space=pltpu.VMEM),
        compiler_params=pltpu.CompilerParams(vmem_limit_bytes=4 << 20),
        name="stack_blocks",
    )(*blocks)


def join_rows(stacks):
    blocks, tokens, width = stacks[0].shape
    total = len(stacks) * blocks
    batch = max(1, 16 // tokens)

    def body(*refs):
        for i in range(0, total, batch):
            group = [refs[j // blocks][j % blocks] for j in range(i, i + batch)]
            rows = jnp.concatenate([value.astype(jnp.float32) for value in group])
            refs[-1][i * tokens : (i + batch) * tokens, :] = rows.astype(refs[-1].dtype)

    return pl.pallas_call(
        body,
        out_shape=jax.ShapeDtypeStruct((total * tokens, width), stacks[0].dtype),
        in_specs=[pl.BlockSpec(memory_space=pltpu.VMEM)] * len(stacks),
        out_specs=pl.BlockSpec(memory_space=pltpu.VMEM),
        compiler_params=pltpu.CompilerParams(
            vmem_limit_bytes=5 * total * tokens * width + (4 << 20)
        ),
        name="join_rows",
    )(*stacks)


def expand_rows(rows, w_gate, w_up, start, columns):
    count, depth = rows.shape[0], w_gate.shape[0]

    def body(rows_ref, gate_ref, up_ref, hidden_ref):
        def step(first, batch):
            x = rows_ref[pl.ds(first, batch), :depth]
            tile = min(TILE, columns)
            for i in range(0, columns, tile):
                cut = slice(start + i, start + i + tile)
                gate = jnp.dot(x, gate_ref[:, cut], preferred_element_type=jnp.float32)
                up = jnp.dot(x, up_ref[:, cut], preferred_element_type=jnp.float32)
                value = gate / (1.0 + jnp.exp(-gate)) * up
                hidden_ref[pl.ds(first, batch), i : i + tile] = value.astype(hidden_ref.dtype)

        row_batches(count, step)

    return pl.pallas_call(
        body,
        out_shape=jax.ShapeDtypeStruct((count, columns), rows.dtype),
        in_specs=[pl.BlockSpec(memory_space=pltpu.VMEM)] * 3,
        out_specs=pl.BlockSpec(memory_space=pltpu.VMEM),
        cost_estimate=pl.CostEstimate(flops=0, bytes_accessed=count * columns, transcendentals=0),
        compiler_params=pltpu.CompilerParams(vmem_limit_bytes=rows.nbytes + (6 << 20)),
        name="expand_rows",
    )(rows, in_vmem(w_gate), in_vmem(w_up))


def contract_hidden(
    parts, w_down, units, before=None, rows=None, half=None, index=None, kind=jnp.float32
):
    total_count, width = parts[0][0].shape[0], w_down.shape[1]
    count = total_count if index is None else total_count // 2
    offset = 0 if index is None else index * count
    experts = lax.axis_size(EXPERT)
    operands = [part for part, _, _ in parts] + [in_vmem(w_down)]
    operands += [value for value in (before, rows) if value is not None]

    def body(*refs):
        part_refs, down_ref = refs[: len(parts)], refs[len(parts)]
        rest = list(refs[len(parts) + 1 : -1])
        before_ref = rest.pop(0) if before is not None else None
        rows_ref = rest.pop(0) if rows is not None else None
        me, group = lax.axis_index(EXPERT), lax.axis_index("dp")

        def step(first, batch):
            here = pl.ds(offset + first, batch)
            if half is None:
                lefts = [ref[here, :] for ref in part_refs]
            else:
                order = [i ^ 3 for i in range(offset // half, (offset + count) // half)]
                lefts = [
                    jnp.concatenate([ref[i * half : (i + 1) * half, :] for i in order])
                    for ref in part_refs
                ]
            if rows is not None:
                table = rows_ref[here, rows.shape[1] - LANES :].astype(jnp.float32)
                lane = lax.broadcasted_iota(jnp.int32, table.shape, 1)
                mine = (lax.rem(lane, experts) == me) & (lane < 3 * experts)
                scale = jnp.sum(jnp.where(mine, table, 0.0), axis=1, keepdims=True)
            tile = min(2 * TILE, width)
            for i in range(0, width, tile):
                cut = slice(i, i + tile)
                total = 0.0 if before is None else before_ref[here, cut]
                for left, (_, mask, unit) in zip(lefts, parts):
                    start = pl.multiple_of((group ^ mask) * units + unit, LANES)
                    right = down_ref[pl.ds(start, left.shape[1]), cut]
                    total = total + jnp.dot(left, right, preferred_element_type=jnp.float32)
                if rows is not None:
                    total = total.astype(jnp.bfloat16).astype(jnp.float32) * scale
                refs[-1][pl.ds(first, batch), cut] = total.astype(kind)

        row_batches(count, step)

    return pl.pallas_call(
        body,
        out_shape=jax.ShapeDtypeStruct((count, width), kind),
        in_specs=[pl.BlockSpec(memory_space=pltpu.VMEM)] * len(operands),
        out_specs=pl.BlockSpec(memory_space=pltpu.VMEM),
        cost_estimate=pl.CostEstimate(flops=0, bytes_accessed=count * width, transcendentals=0),
        compiler_params=pltpu.CompilerParams(
            vmem_limit_bytes=8 * total_count * width
            + (6 << 20)
            + (0 if rows is None else rows.nbytes)
        ),
        name="contract_hidden",
    )(*operands)


def sum_stage(inputs, plan, shape, dtype):
    def body(*refs):
        sources, targets = refs[: len(inputs)], refs[len(inputs) :]
        for target, blocks in zip(targets, plan):
            for i, block in enumerate(blocks):
                total = 0.0
                for ref in sources:
                    if len(ref.shape) == 2:
                        value = ref[block * shape[0] : (block + 1) * shape[0], :]
                    else:
                        value = ref[block]
                    total = total + value.astype(jnp.float32)
                target[i] = total.astype(target.dtype)

    return pl.pallas_call(
        body,
        out_shape=[
            jax.ShapeDtypeStruct((len(blocks),) + shape, dtype if i else jnp.float32)
            for i, blocks in enumerate(plan)
        ],
        in_specs=[pl.BlockSpec(memory_space=pltpu.VMEM)] * len(inputs),
        out_specs=[pl.BlockSpec(memory_space=pltpu.VMEM)] * len(plan),
        compiler_params=pltpu.CompilerParams(
            vmem_limit_bytes=sum(value.nbytes for value in inputs) * 2 + (6 << 20)
        ),
        name="sum_stage",
    )(*inputs)


def finish(sums, groups, dtype):
    tokens, columns = sums[0][0].shape[1:]
    flat = [value for parts in sums for value in parts]

    def body(*refs):
        group = lax.axis_index("dp")
        refs, out_ref = list(refs[:-1]), refs[-1]
        for i, parts in enumerate(sums):
            total = sum(refs.pop(0)[0].astype(jnp.float32) for _ in parts)
            start = pl.multiple_of((group ^ i) * columns, LANES)
            out_ref[:, pl.ds(start, columns)] = total.astype(dtype)

    return pl.pallas_call(
        body,
        out_shape=jax.ShapeDtypeStruct((tokens, groups * columns), dtype),
        in_specs=[pl.BlockSpec(memory_space=pltpu.VMEM)] * len(flat),
        out_specs=pl.BlockSpec(memory_space=pltpu.VMEM),
        compiler_params=pltpu.CompilerParams(vmem_limit_bytes=4 << 20),
        name="finish",
    )(*flat)


def local(tokens, expert_ids, gate_probs, w_gate, w_up, w_down):
    token_count, width = tokens.shape
    groups, experts = lax.axis_size("dp"), lax.axis_size(EXPERT)
    wide, high = groups // 2, experts // 4

    block = pack_block(tokens, expert_ids, gate_probs, experts)
    units = w_up.shape[2]
    weights = lax.optimization_barrier((block, w_gate[0], w_up[0], w_down[0]))
    block, gate_weights, up_weights, down_weights = weights
    near = stack_blocks([block] + [swap(block, far(i)) for i in range(1, high)])
    if wide > 1:
        near = jnp.concatenate([near] + [swap(near, (2 * i, 0)) for i in range(1, wide)])
    chip = join_rows([near, swap(near, Y), swap(near, X), swap(near, both(X, Y))])
    rows = jnp.concatenate([chip, swap(chip, (0, 1))])

    chunks = CHUNKS if units % (LANES * CHUNKS) == 0 else 1
    step = units // chunks
    half = rows.shape[0] // 4 if groups == 2 and rows.shape[0] <= BATCH else None

    def from_group(value, mask):
        value = swap(value, (mask, 0))
        if half is not None:
            return value
        value = value.reshape(2, 2, 2, wide, high * token_count, step)
        for axis in range(2):
            order = [i ^ (mask & 1) for i in range(2)]
            value = jnp.stack([lax.index_in_dim(value, i, axis, False) for i in order], axis)
        value = jnp.stack([value[:, :, :, i ^ (mask >> 1)] for i in range(wide)], axis=3)
        return value.reshape(-1, step)

    hidden, others = [], []
    for i in range(chunks):
        if hidden:
            rows, hidden[-1] = lax.optimization_barrier((rows, hidden[-1]))
        hidden.append(expand_rows(rows, gate_weights, up_weights, i * step, step))
        others.append(
            [(from_group(hidden[-1], mask), mask, i * step) for mask in range(1, groups)]
        )
    parts = [(value, 0, i * step) for i, value in enumerate(hidden)]
    total = contract_hidden(parts, down_weights, units)
    for i in range(chunks - 1):
        total = contract_hidden(others[i], down_weights, units, total, half=half)
    last = lambda index, kind: contract_hidden(
        others[-1], down_weights, units, total, rows, half, index, kind
    )
    sent, kept = last(1, jnp.bfloat16), last(0, jnp.float32)

    shape = (token_count, w_down.shape[2])
    rest = [(g, h) for g in range(groups) for h in range(0, high, 2)]
    slot = lambda g, y, h: (((g & 1) * 2 + y) * wide + (g >> 1)) * high + h
    plan = [[slot(g, y, h + z) for g, h in rest] for y, z in ((0, 0), (1, 1), (0, 1), (1, 0))]
    mine, *away = sum_stage([kept, swap(sent, (0, 1))], plan, shape, jnp.bfloat16)
    masks = (both(Y, far(1)), far(1), Y)
    inputs = [mine] + [swap(value, mask) for value, mask in zip(away, masks)]
    order = [0] + list(range(len(rest) - 1, 0, -1))
    mine, *away = sum_stage(inputs, [[i] for i in order], shape, jnp.bfloat16)
    sums = [[] for _ in range(groups)]
    sums[0].append(mine)
    for value, (g, h) in zip(away, [rest[i] for i in order[1:]]):
        mask = both((g - g % 2, 0), far(h))
        sums[g].append(swap(value, both(mask, X) if g % 2 else mask))
    return finish(sums, groups, tokens.dtype)


def solution(mesh):
    groups, experts = mesh.devices.shape
    split = Mesh(mesh.devices.reshape(groups, experts // 2, 2), ("dp", "far", "core"))
    row, expert = P(("dp", "far", "core"), None), P(EXPERT, None, "dp")
    return jax.shard_map(
        local,
        mesh=split,
        in_specs=(row, row, row, expert, expert, expert),
        out_specs=row,
        check_vma=False,
    )
```

```python
import jax
import jax.numpy as jnp
from jax import lax
from jax.experimental import pallas as pl
from jax.experimental.pallas import tpu as pltpu
from jax.sharding import Mesh
from jax.sharding import PartitionSpec as P

CHUNKS = 2
TILE = 256
BATCH = 128
LANES = 128
X, Y = (1, 0), (0, 2)
EXPERT = ("far", "core")


def far(i):
    return (0, 4 * i + bin(i).count("1") % 2)


def both(a, b):
    return (a[0] ^ b[0], a[1] ^ b[1])


def swap(value, masks):
    group_mask, expert_mask = masks
    groups, experts = lax.axis_size("dp"), lax.axis_size(EXPERT)
    pairs = [
        (g * experts + e, (g ^ group_mask) * experts + (e ^ expert_mask))
        for g in range(groups)
        for e in range(experts)
    ]
    return lax.ppermute(value, ("dp",) + EXPERT, pairs)


def in_vmem(value):
    return pltpu.with_memory_space_constraint(value, pltpu.VMEM)


def in_hbm(value):
    return pltpu.with_memory_space_constraint(value, pltpu.HBM)


def row_batches(count, step):
    batch = min(BATCH, count)
    if count == batch:
        step(0, batch)
    else:

        @pl.loop(0, count // batch)
        def _(i):
            step(pl.multiple_of(i * batch, batch), batch)


def pack_block(tokens, expert_ids, gate_probs, experts):
    count, width = tokens.shape
    top = expert_ids.shape[1]

    def body(tokens_ref, ids_ref, probs_ref, block_ref):
        block_ref[:, :width] = tokens_ref[...]
        lane = lax.broadcasted_iota(jnp.int32, (count, LANES), 1)
        table = jnp.zeros((count, LANES), jnp.float32)
        for k in range(top):
            hit = ids_ref[:, k : k + 1] == lax.rem(lane, experts)
            table = jnp.where(hit, probs_ref[:, k : k + 1], table)
        packed = jnp.zeros((count, LANES), jnp.float32)
        for i in range(3):
            part = table.astype(jnp.bfloat16).astype(jnp.float32)
            packed = jnp.where(lane // experts == i, part, packed)
            table = table - part
        block_ref[:, width:] = packed.astype(block_ref.dtype)

    return pl.pallas_call(
        body,
        out_shape=jax.ShapeDtypeStruct((count, width + LANES), tokens.dtype),
        in_specs=[pl.BlockSpec(memory_space=pltpu.VMEM)] * 3,
        out_specs=pl.BlockSpec(memory_space=pltpu.VMEM),
        cost_estimate=pl.CostEstimate(flops=60 * 10**9, bytes_accessed=0, transcendentals=0),
        compiler_params=pltpu.CompilerParams(vmem_limit_bytes=1 << 20),
        name="pack_block",
    )(in_hbm(tokens), in_hbm(expert_ids), in_hbm(gate_probs))


def stack_blocks(blocks):
    def body(*refs):
        for i, ref in enumerate(refs[:-1]):
            refs[-1][i] = ref[...]

    return pl.pallas_call(
        body,
        out_shape=jax.ShapeDtypeStruct((len(blocks),) + blocks[0].shape, blocks[0].dtype),
        in_specs=[pl.BlockSpec(memory_space=pltpu.VMEM)] * len(blocks),
        out_specs=pl.BlockSpec(memory_space=pltpu.VMEM),
        compiler_params=pltpu.CompilerParams(vmem_limit_bytes=4 << 20),
        name="stack_blocks",
    )(*blocks)


def join_rows(stacks):
    blocks, tokens, width = stacks[0].shape
    total = len(stacks) * blocks
    batch = max(1, 16 // tokens)

    def body(*refs):
        for i in range(0, total, batch):
            group = [refs[j // blocks][j % blocks] for j in range(i, i + batch)]
            rows = jnp.concatenate([value.astype(jnp.float32) for value in group])
            refs[-1][i * tokens : (i + batch) * tokens, :] = rows.astype(refs[-1].dtype)

    return pl.pallas_call(
        body,
        out_shape=jax.ShapeDtypeStruct((total * tokens, width), stacks[0].dtype),
        in_specs=[pl.BlockSpec(memory_space=pltpu.VMEM)] * len(stacks),
        out_specs=pl.BlockSpec(memory_space=pltpu.VMEM),
        compiler_params=pltpu.CompilerParams(
            vmem_limit_bytes=5 * total * tokens * width + (4 << 20)
        ),
        name="join_rows",
    )(*stacks)


def expand_rows(rows, w_gate, w_up, start, columns):
    count, depth = rows.shape[0], w_gate.shape[0]

    def body(rows_ref, gate_ref, up_ref, hidden_ref):
        def step(first, batch):
            x = rows_ref[pl.ds(first, batch), :depth]
            tile = min(TILE, columns)
            for i in range(0, columns, tile):
                cut = slice(start + i, start + i + tile)
                gate = jnp.dot(x, gate_ref[:, cut], preferred_element_type=jnp.float32)
                up = jnp.dot(x, up_ref[:, cut], preferred_element_type=jnp.float32)
                value = gate / (1.0 + jnp.exp(-gate)) * up
                hidden_ref[pl.ds(first, batch), i : i + tile] = value.astype(hidden_ref.dtype)

        row_batches(count, step)

    return pl.pallas_call(
        body,
        out_shape=jax.ShapeDtypeStruct((count, columns), rows.dtype),
        in_specs=[pl.BlockSpec(memory_space=pltpu.VMEM)] * 3,
        out_specs=pl.BlockSpec(memory_space=pltpu.VMEM),
        cost_estimate=pl.CostEstimate(flops=0, bytes_accessed=count * columns, transcendentals=0),
        compiler_params=pltpu.CompilerParams(vmem_limit_bytes=rows.nbytes + (6 << 20)),
        name="expand_rows",
    )(rows, in_vmem(w_gate), in_vmem(w_up))


def contract_hidden(
    parts, w_down, units, before=None, rows=None, half=None, index=None, kind=jnp.float32
):
    total_count, width = parts[0][0].shape[0], w_down.shape[1]
    count = total_count if index is None else total_count // 2
    offset = 0 if index is None else index * count
    experts = lax.axis_size(EXPERT)
    operands = [part for part, _, _ in parts] + [in_vmem(w_down)]
    operands += [value for value in (before, rows) if value is not None]

    def body(*refs):
        part_refs, down_ref = refs[: len(parts)], refs[len(parts)]
        rest = list(refs[len(parts) + 1 : -1])
        before_ref = rest.pop(0) if before is not None else None
        rows_ref = rest.pop(0) if rows is not None else None
        me, group = lax.axis_index(EXPERT), lax.axis_index("dp")

        def step(first, batch):
            here = pl.ds(offset + first, batch)
            if half is None:
                lefts = [ref[here, :] for ref in part_refs]
            else:
                order = [i ^ 1 for i in range(offset // half, (offset + count) // half)]
                lefts = [
                    jnp.concatenate([ref[i * half : (i + 1) * half, :] for i in order])
                    for ref in part_refs
                ]
            if rows is not None:
                table = rows_ref[here, rows.shape[1] - LANES :].astype(jnp.float32)
                lane = lax.broadcasted_iota(jnp.int32, table.shape, 1)
                mine = (lax.rem(lane, experts) == me) & (lane < 3 * experts)
                scale = jnp.sum(jnp.where(mine, table, 0.0), axis=1, keepdims=True)
            tile = min(2 * TILE, width)
            for i in range(0, width, tile):
                cut = slice(i, i + tile)
                total = 0.0 if before is None else before_ref[here, cut]
                for left, (_, mask, unit) in zip(lefts, parts):
                    start = pl.multiple_of((group ^ mask) * units + unit, LANES)
                    right = down_ref[pl.ds(start, left.shape[1]), cut]
                    total = total + jnp.dot(left, right, preferred_element_type=jnp.float32)
                if rows is not None:
                    total = total.astype(jnp.bfloat16).astype(jnp.float32) * scale
                refs[-1][pl.ds(first, batch), cut] = total.astype(kind)

        row_batches(count, step)

    return pl.pallas_call(
        body,
        out_shape=jax.ShapeDtypeStruct((count, width), kind),
        in_specs=[pl.BlockSpec(memory_space=pltpu.VMEM)] * len(operands),
        out_specs=pl.BlockSpec(memory_space=pltpu.VMEM),
        cost_estimate=pl.CostEstimate(flops=0, bytes_accessed=count * width, transcendentals=0),
        compiler_params=pltpu.CompilerParams(
            vmem_limit_bytes=8 * total_count * width
            + (6 << 20)
            + (0 if rows is None else rows.nbytes)
        ),
        name="contract_hidden",
    )(*operands)


def sum_stage(inputs, plan, shape, dtype):
    def body(*refs):
        sources, targets = refs[: len(inputs)], refs[len(inputs) :]
        for target, blocks in zip(targets, plan):
            for i, block in enumerate(blocks):
                total = 0.0
                for ref in sources:
                    if len(ref.shape) == 2:
                        value = ref[block * shape[0] : (block + 1) * shape[0], :]
                    else:
                        value = ref[block]
                    total = total + value.astype(jnp.float32)
                target[i] = total.astype(target.dtype)

    return pl.pallas_call(
        body,
        out_shape=[
            jax.ShapeDtypeStruct((len(blocks),) + shape, dtype if i else jnp.float32)
            for i, blocks in enumerate(plan)
        ],
        in_specs=[pl.BlockSpec(memory_space=pltpu.VMEM)] * len(inputs),
        out_specs=[pl.BlockSpec(memory_space=pltpu.VMEM)] * len(plan),
        compiler_params=pltpu.CompilerParams(
            vmem_limit_bytes=sum(value.nbytes for value in inputs) * 2 + (6 << 20)
        ),
        name="sum_stage",
    )(*inputs)


def finish(sums, groups, dtype):
    tokens, columns = sums[0][0].shape[1:]
    flat = [value for parts in sums for value in parts]

    def body(*refs):
        group = lax.axis_index("dp")
        refs, out_ref = list(refs[:-1]), refs[-1]
        for i, parts in enumerate(sums):
            total = sum(refs.pop(0)[0].astype(jnp.float32) for _ in parts)
            start = pl.multiple_of((group ^ i) * columns, LANES)
            out_ref[:, pl.ds(start, columns)] = total.astype(dtype)

    return pl.pallas_call(
        body,
        out_shape=jax.ShapeDtypeStruct((tokens, groups * columns), dtype),
        in_specs=[pl.BlockSpec(memory_space=pltpu.VMEM)] * len(flat),
        out_specs=pl.BlockSpec(memory_space=pltpu.VMEM),
        compiler_params=pltpu.CompilerParams(vmem_limit_bytes=4 << 20),
        name="finish",
    )(*flat)


def local(tokens, expert_ids, gate_probs, w_gate, w_up, w_down):
    token_count, width = tokens.shape
    groups, experts = lax.axis_size("dp"), lax.axis_size(EXPERT)
    wide, high = groups // 2, experts // 4

    block = pack_block(tokens, expert_ids, gate_probs, experts)
    units = w_up.shape[2]
    weights = lax.optimization_barrier((block, w_gate[0], w_up[0], w_down[0]))
    block, gate_weights, up_weights, down_weights = weights
    near = stack_blocks([block] + [swap(block, far(i)) for i in range(1, high)])
    if wide > 1:
        near = jnp.concatenate([near] + [swap(near, (2 * i, 0)) for i in range(1, wide)])
    chip = join_rows([near, swap(near, Y), swap(near, X), swap(near, both(X, Y))])
    rows = jnp.concatenate([chip, swap(chip, (0, 1))])

    chunks = CHUNKS if units % (LANES * CHUNKS) == 0 else 1
    step = units // chunks
    half = rows.shape[0] // 4 if groups == 2 and rows.shape[0] <= BATCH else None

    def from_group(value, mask):
        value = swap(value, (mask, 0))
        if half is not None:
            return value
        value = value.reshape(2, 2, 2, wide, high * token_count, step)
        value = jnp.stack([value[:, i ^ (mask & 1)] for i in range(2)], axis=1)
        value = jnp.stack([value[:, :, :, i ^ (mask >> 1)] for i in range(wide)], axis=3)
        return value.reshape(-1, step)

    hidden, others = [], []
    for i in range(chunks):
        if hidden:
            rows, hidden[-1] = lax.optimization_barrier((rows, hidden[-1]))
        hidden.append(expand_rows(rows, gate_weights, up_weights, i * step, step))
        others.append(
            [(from_group(hidden[-1], mask), mask, i * step) for mask in range(1, groups)]
        )
    parts = [(value, 0, i * step) for i, value in enumerate(hidden)]
    total = contract_hidden(parts, down_weights, units)
    for i in range(chunks - 1):
        total = contract_hidden(others[i], down_weights, units, total, half=half)
    last = lambda index, kind: contract_hidden(
        others[-1], down_weights, units, total, rows, half, index, kind
    )
    sent, kept = last(1, jnp.bfloat16), last(0, jnp.float32)

    shape = (token_count, w_down.shape[2])
    rest = [(g, h) for g in range(groups) for h in range(0, high, 2)]
    slot = lambda g, y, h: (((g & 1) * 2 + y) * wide + (g >> 1)) * high + h
    plan = [[slot(g, y, h + z) for g, h in rest] for y, z in ((0, 0), (1, 1), (0, 1), (1, 0))]
    mine, *away = sum_stage([kept, swap(sent, (0, 1))], plan, shape, jnp.bfloat16)
    masks = (both(Y, far(1)), far(1), Y)
    inputs = [mine] + [swap(value, mask) for value, mask in zip(away, masks)]
    order = [0] + list(range(len(rest) - 1, 0, -1))
    mine, *away = sum_stage(inputs, [[i] for i in order], shape, jnp.bfloat16)
    sums = [[] for _ in range(groups)]
    sums[0].append(mine)
    for value, (g, h) in zip(away, [rest[i] for i in order[1:]]):
        mask = both((g - g % 2, 0), far(h))
        sums[g].append(swap(value, both(mask, X) if g % 2 else mask))
    return finish(sums, groups, tokens.dtype)


def solution(mesh):
    groups, experts = mesh.devices.shape
    split = Mesh(mesh.devices.reshape(groups, experts // 2, 2), ("dp", "far", "core"))
    row, expert = P(("dp", "far", "core"), None), P(EXPERT, None, "dp")
    return jax.shard_map(
        local,
        mesh=split,
        in_specs=(row, row, row, expert, expert, expert),
        out_specs=row,
        check_vma=False,
    )
```

```python
import jax
import jax.numpy as jnp
from jax import lax
from jax.experimental import pallas as pl
from jax.experimental.pallas import tpu as pltpu
from jax.sharding import Mesh
from jax.sharding import PartitionSpec as P

CHUNKS = 2
TILE = 256
BATCH = 128
LANES = 128
EXPERT = ("far", "core")


def swap(value, group_mask, expert_mask):
    groups, experts = lax.axis_size("dp"), lax.axis_size(EXPERT)
    pairs = [
        (g * experts + e, (g ^ group_mask) * experts + (e ^ expert_mask))
        for g in range(groups)
        for e in range(experts)
    ]
    return lax.ppermute(value, ("dp",) + EXPERT, pairs)


def in_vmem(value):
    return pltpu.with_memory_space_constraint(value, pltpu.VMEM)


def in_hbm(value):
    return pltpu.with_memory_space_constraint(value, pltpu.HBM)


def row_batches(count, step):
    batch = min(BATCH, count)
    if count == batch:
        step(0, batch)
    else:

        @pl.loop(0, count // batch)
        def _(i):
            step(pl.multiple_of(i * batch, batch), batch)


def pack_block(tokens, expert_ids, gate_probs, experts):
    count, width = tokens.shape
    top = expert_ids.shape[1]

    def body(tokens_ref, ids_ref, probs_ref, block_ref):
        block_ref[:, :width] = tokens_ref[...]
        lane = lax.broadcasted_iota(jnp.int32, (count, LANES), 1)
        table = jnp.zeros((count, LANES), jnp.float32)
        for k in range(top):
            hit = ids_ref[:, k : k + 1] == lax.rem(lane, experts)
            table = jnp.where(hit, probs_ref[:, k : k + 1], table)
        packed = jnp.zeros((count, LANES), jnp.float32)
        for i in range(3):
            part = table.astype(jnp.bfloat16).astype(jnp.float32)
            packed = jnp.where(lane // experts == i, part, packed)
            table = table - part
        block_ref[:, width:] = packed.astype(block_ref.dtype)

    return pl.pallas_call(
        body,
        out_shape=jax.ShapeDtypeStruct((count, width + LANES), tokens.dtype),
        in_specs=[pl.BlockSpec(memory_space=pltpu.VMEM)] * 3,
        out_specs=pl.BlockSpec(memory_space=pltpu.VMEM),
        cost_estimate=pl.CostEstimate(flops=60 * 10**9, bytes_accessed=0, transcendentals=0),
        compiler_params=pltpu.CompilerParams(vmem_limit_bytes=1 << 20),
        name="pack_block",
    )(in_hbm(tokens), in_hbm(expert_ids), in_hbm(gate_probs))


def stack_blocks(blocks):
    def body(*refs):
        for i, ref in enumerate(refs[:-1]):
            refs[-1][i] = ref[...]

    return pl.pallas_call(
        body,
        out_shape=jax.ShapeDtypeStruct((len(blocks),) + blocks[0].shape, blocks[0].dtype),
        in_specs=[pl.BlockSpec(memory_space=pltpu.VMEM)] * len(blocks),
        out_specs=pl.BlockSpec(memory_space=pltpu.VMEM),
        compiler_params=pltpu.CompilerParams(vmem_limit_bytes=4 << 20),
        name="stack_blocks",
    )(*blocks)


def join_rows(stacks):
    blocks, tokens, width = stacks[0].shape
    total = len(stacks) * blocks
    batch = max(1, 16 // tokens)

    def body(*refs):
        for i in range(0, total, batch):
            group = [refs[j // blocks][j % blocks] for j in range(i, i + batch)]
            rows = jnp.concatenate([value.astype(jnp.float32) for value in group])
            refs[-1][i * tokens : (i + batch) * tokens, :] = rows.astype(refs[-1].dtype)

    return pl.pallas_call(
        body,
        out_shape=jax.ShapeDtypeStruct((total * tokens, width), stacks[0].dtype),
        in_specs=[pl.BlockSpec(memory_space=pltpu.VMEM)] * len(stacks),
        out_specs=pl.BlockSpec(memory_space=pltpu.VMEM),
        compiler_params=pltpu.CompilerParams(
            vmem_limit_bytes=5 * total * tokens * width + (4 << 20)
        ),
        name="join_rows",
    )(*stacks)


def expand_rows(rows, w_gate, w_up, start, columns):
    count, depth = rows.shape[0], w_gate.shape[0]

    def body(rows_ref, gate_ref, up_ref, hidden_ref):
        def step(first, batch):
            x = rows_ref[pl.ds(first, batch), :depth]
            tile = min(TILE, columns)
            for i in range(0, columns, tile):
                cut = slice(start + i, start + i + tile)
                gate = jnp.dot(x, gate_ref[:, cut], preferred_element_type=jnp.float32)
                up = jnp.dot(x, up_ref[:, cut], preferred_element_type=jnp.float32)
                value = gate / (1.0 + jnp.exp(-gate)) * up
                hidden_ref[pl.ds(first, batch), i : i + tile] = value.astype(hidden_ref.dtype)

        row_batches(count, step)

    return pl.pallas_call(
        body,
        out_shape=jax.ShapeDtypeStruct((count, columns), rows.dtype),
        in_specs=[pl.BlockSpec(memory_space=pltpu.VMEM)] * 3,
        out_specs=pl.BlockSpec(memory_space=pltpu.VMEM),
        cost_estimate=pl.CostEstimate(flops=0, bytes_accessed=count * columns, transcendentals=0),
        compiler_params=pltpu.CompilerParams(vmem_limit_bytes=rows.nbytes + (6 << 20)),
        name="expand_rows",
    )(rows, in_vmem(w_gate), in_vmem(w_up))


def contract_hidden(
    parts, w_down, units, before=None, rows=None, half=None, index=None, kind=jnp.float32
):
    total_count, width = parts[0][0].shape[0], w_down.shape[1]
    count = total_count if index is None else total_count // 2
    offset = 0 if index is None else index * count
    experts = lax.axis_size(EXPERT)
    operands = [part for part, _, _ in parts] + [in_vmem(w_down)]
    operands += [value for value in (before, rows) if value is not None]

    def body(*refs):
        part_refs, down_ref = refs[: len(parts)], refs[len(parts)]
        rest = list(refs[len(parts) + 1 : -1])
        before_ref = rest.pop(0) if before is not None else None
        rows_ref = rest.pop(0) if rows is not None else None
        me, group = lax.axis_index(EXPERT), lax.axis_index("dp")

        def step(first, batch):
            here = pl.ds(offset + first, batch)
            if half is None:
                lefts = [ref[here, :] for ref in part_refs]
            else:
                order = [i ^ 1 for i in range(offset // half, (offset + count) // half)]
                lefts = [
                    jnp.concatenate([ref[i * half : (i + 1) * half, :] for i in order])
                    for ref in part_refs
                ]
            if rows is not None:
                table = rows_ref[here, rows.shape[1] - LANES :].astype(jnp.float32)
                lane = lax.broadcasted_iota(jnp.int32, table.shape, 1)
                mine = (lax.rem(lane, experts) == me) & (lane < 3 * experts)
                scale = jnp.sum(jnp.where(mine, table, 0.0), axis=1, keepdims=True)
            tile = min(2 * TILE, width)
            for i in range(0, width, tile):
                cut = slice(i, i + tile)
                total = 0.0 if before is None else before_ref[here, cut]
                for left, (_, mask, unit) in zip(lefts, parts):
                    start = pl.multiple_of((group ^ mask) * units + unit, LANES)
                    right = down_ref[pl.ds(start, left.shape[1]), cut]
                    total = total + jnp.dot(left, right, preferred_element_type=jnp.float32)
                if rows is not None:
                    total = total.astype(jnp.bfloat16).astype(jnp.float32) * scale
                refs[-1][pl.ds(first, batch), cut] = total.astype(kind)

        row_batches(count, step)

    return pl.pallas_call(
        body,
        out_shape=jax.ShapeDtypeStruct((count, width), kind),
        in_specs=[pl.BlockSpec(memory_space=pltpu.VMEM)] * len(operands),
        out_specs=pl.BlockSpec(memory_space=pltpu.VMEM),
        cost_estimate=pl.CostEstimate(flops=0, bytes_accessed=count * width, transcendentals=0),
        compiler_params=pltpu.CompilerParams(
            vmem_limit_bytes=8 * total_count * width
            + (6 << 20)
            + (0 if rows is None else rows.nbytes)
        ),
        name="contract_hidden",
    )(*operands)


def sum_stage(inputs, plan, shape, dtype):
    def body(*refs):
        sources, targets = refs[: len(inputs)], refs[len(inputs) :]
        for target, blocks in zip(targets, plan):
            for i, block in enumerate(blocks):
                total = 0.0
                for ref in sources:
                    if len(ref.shape) == 2:
                        value = ref[block * shape[0] : (block + 1) * shape[0], :]
                    else:
                        value = ref[block]
                    total = total + value.astype(jnp.float32)
                target[i] = total.astype(target.dtype)

    return pl.pallas_call(
        body,
        out_shape=[
            jax.ShapeDtypeStruct((len(blocks),) + shape, dtype if i else jnp.float32)
            for i, blocks in enumerate(plan)
        ],
        in_specs=[pl.BlockSpec(memory_space=pltpu.VMEM)] * len(inputs),
        out_specs=[pl.BlockSpec(memory_space=pltpu.VMEM)] * len(plan),
        compiler_params=pltpu.CompilerParams(
            vmem_limit_bytes=sum(value.nbytes for value in inputs) * 2 + (6 << 20)
        ),
        name="sum_stage",
    )(*inputs)


def finish(parts, groups, dtype):
    tokens, columns = parts[0][0].shape[1:]

    def body(*refs):
        group = lax.axis_index("dp")
        for i in range(groups):
            mine = [ref[0] for ref, (_, j) in zip(refs, parts) if i == j]
            total = sum(value.astype(jnp.float32) for value in mine)
            start = pl.multiple_of((group ^ i) * columns, LANES)
            refs[-1][:, pl.ds(start, columns)] = total.astype(dtype)

    return pl.pallas_call(
        body,
        out_shape=jax.ShapeDtypeStruct((tokens, groups * columns), dtype),
        in_specs=[pl.BlockSpec(memory_space=pltpu.VMEM)] * len(parts),
        out_specs=pl.BlockSpec(memory_space=pltpu.VMEM),
        compiler_params=pltpu.CompilerParams(vmem_limit_bytes=4 << 20),
        name="finish",
    )(*[value for value, _ in parts])


def local(tokens, expert_ids, gate_probs, w_gate, w_up, w_down):
    token_count, width = tokens.shape
    groups, experts = lax.axis_size("dp"), lax.axis_size(EXPERT)
    wide, high = groups // 2, experts // 4

    block = pack_block(tokens, expert_ids, gate_probs, experts)
    units = w_up.shape[2]
    weights = lax.optimization_barrier((block, w_gate[0], w_up[0], w_down[0]))
    block, gate_weights, up_weights, down_weights = weights
    near = stack_blocks([block] + [swap(block, 0, 4 * i) for i in range(1, high)])
    if wide > 1:
        near = jnp.concatenate([near] + [swap(near, 2 * i, 0) for i in range(1, wide)])
    chip = join_rows([near, swap(near, 0, 2), swap(near, 1, 0), swap(near, 1, 2)])
    rows = jnp.concatenate([chip, swap(chip, 0, 1)])

    chunks = CHUNKS if units % (LANES * CHUNKS) == 0 else 1
    step = units // chunks
    half = rows.shape[0] // 4 if groups == 2 and rows.shape[0] <= BATCH else None

    def from_group(value, mask):
        value = swap(value, mask, 0)
        if half is not None:
            return value
        value = value.reshape(2, 2, 2, wide, high * token_count, step)
        value = jnp.stack([value[:, i ^ (mask & 1)] for i in range(2)], axis=1)
        value = jnp.stack([value[:, :, :, i ^ (mask >> 1)] for i in range(wide)], axis=3)
        return value.reshape(-1, step)

    hidden, others = [], []
    for i in range(chunks):
        if hidden:
            rows, hidden[-1] = lax.optimization_barrier((rows, hidden[-1]))
        hidden.append(expand_rows(rows, gate_weights, up_weights, i * step, step))
        others.append(
            [(from_group(hidden[-1], mask), mask, i * step) for mask in range(1, groups)]
        )
    parts = [(value, 0, i * step) for i, value in enumerate(hidden)]
    total = contract_hidden(parts, down_weights, units)
    for i in range(chunks - 1):
        total = contract_hidden(others[i], down_weights, units, total, half=half)
    last = lambda index, kind: contract_hidden(
        others[-1], down_weights, units, total, rows, half, index, kind
    )
    sent, kept = last(1, jnp.bfloat16), last(0, jnp.float32)

    shape = (token_count, w_down.shape[2])
    rest = [(g, h) for g in range(groups) for h in range(0, high, 2)]
    slot = lambda g, y, h: (((g & 1) * 2 + y) * wide + (g >> 1)) * high + h
    plan = [[slot(g, y, h + z) for g, h in rest] for y, z in ((0, 0), (1, 1), (0, 1), (1, 0))]
    mine, *away = sum_stage([kept, swap(sent, 0, 1)], plan, shape, jnp.bfloat16)
    inputs = [mine] + [swap(value, 0, mask) for value, mask in zip(away, (6, 4, 2))]
    order = sorted(range(1, len(rest)), key=lambda i: (rest[i][1], rest[i][0]), reverse=True)
    mine, *away = sum_stage(inputs, [[i] for i in [0] + order], shape, jnp.bfloat16)
    parts = [
        (swap(value, rest[i][0], 4 * rest[i][1]), rest[i][0]) for value, i in zip(away, order)
    ]
    return finish(parts + [(mine, 0)], groups, tokens.dtype)


def solution(mesh):
    groups, experts = mesh.devices.shape
    split = Mesh(mesh.devices.reshape(groups, experts // 2, 2), ("dp", "far", "core"))
    row, expert = P(("dp", "far", "core"), None), P(EXPERT, None, "dp")
    return jax.shard_map(
        local,
        mesh=split,
        in_specs=(row, row, row, expert, expert, expert),
        out_specs=row,
        check_vma=False,
    )
```

```python
import jax
import jax.numpy as jnp
from jax import lax
from jax.experimental import pallas as pl
from jax.experimental.pallas import tpu as pltpu
from jax.sharding import Mesh
from jax.sharding import PartitionSpec as P

CHUNKS = 2
TILE = 256
BATCH = 128
LANES = 128
EXPERT = ("far", "core")


def permute(value, masks_of):
    groups, experts = lax.axis_size("dp"), lax.axis_size(EXPERT)
    pairs = []
    for g in range(groups):
        for e in range(experts):
            masks = masks_of[e % 2]
            if masks is not None:
                pairs.append((g * experts + e, (g ^ masks[0]) * experts + (e ^ masks[1])))
    return lax.ppermute(value, ("dp",) + EXPERT, pairs)


def swap(value, group_mask, expert_mask):
    return permute(value, ((group_mask, expert_mask),) * 2)


def in_vmem(value):
    return pltpu.with_memory_space_constraint(value, pltpu.VMEM)


def in_hbm(value):
    return pltpu.with_memory_space_constraint(value, pltpu.HBM)


def row_batches(count, step):
    batch = min(BATCH, count)
    if count == batch:
        step(0, batch)
    else:

        @pl.loop(0, count // batch)
        def _(i):
            step(pl.multiple_of(i * batch, batch), batch)


def pack_block(tokens, expert_ids, gate_probs, experts):
    count, width = tokens.shape
    top = expert_ids.shape[1]

    def body(tokens_ref, ids_ref, probs_ref, block_ref):
        block_ref[:, :width] = tokens_ref[...]
        lane = lax.broadcasted_iota(jnp.int32, (count, LANES), 1)
        table = jnp.zeros((count, LANES), jnp.float32)
        for k in range(top):
            hit = ids_ref[:, k : k + 1] == lax.rem(lane, experts)
            table = jnp.where(hit, probs_ref[:, k : k + 1], table)
        packed = jnp.zeros((count, LANES), jnp.float32)
        for i in range(3):
            part = table.astype(jnp.bfloat16).astype(jnp.float32)
            packed = jnp.where(lane // experts == i, part, packed)
            table = table - part
        block_ref[:, width:] = packed.astype(block_ref.dtype)

    return pl.pallas_call(
        body,
        out_shape=jax.ShapeDtypeStruct((count, width + LANES), tokens.dtype),
        in_specs=[pl.BlockSpec(memory_space=pltpu.VMEM)] * 3,
        out_specs=pl.BlockSpec(memory_space=pltpu.VMEM),
        cost_estimate=pl.CostEstimate(flops=60 * 10**9, bytes_accessed=0, transcendentals=0),
        compiler_params=pltpu.CompilerParams(vmem_limit_bytes=1 << 20),
        name="pack_block",
    )(in_hbm(tokens), in_hbm(expert_ids), in_hbm(gate_probs))


def stack_blocks(blocks):
    def body(*refs):
        for i, ref in enumerate(refs[:-1]):
            refs[-1][i] = ref[...]

    return pl.pallas_call(
        body,
        out_shape=jax.ShapeDtypeStruct((len(blocks),) + blocks[0].shape, blocks[0].dtype),
        in_specs=[pl.BlockSpec(memory_space=pltpu.VMEM)] * len(blocks),
        out_specs=pl.BlockSpec(memory_space=pltpu.VMEM),
        compiler_params=pltpu.CompilerParams(vmem_limit_bytes=4 << 20),
        name="stack_blocks",
    )(*blocks)


def join_rows(stacks):
    blocks, tokens, width = stacks[0].shape
    total = len(stacks) * blocks
    batch = max(1, 16 // tokens)

    def body(*refs):
        for i in range(0, total, batch):
            group = [refs[j // blocks][j % blocks] for j in range(i, i + batch)]
            rows = jnp.concatenate([value.astype(jnp.float32) for value in group])
            refs[-1][i * tokens : (i + batch) * tokens, :] = rows.astype(refs[-1].dtype)

    return pl.pallas_call(
        body,
        out_shape=jax.ShapeDtypeStruct((total * tokens, width), stacks[0].dtype),
        in_specs=[pl.BlockSpec(memory_space=pltpu.VMEM)] * len(stacks),
        out_specs=pl.BlockSpec(memory_space=pltpu.VMEM),
        compiler_params=pltpu.CompilerParams(
            vmem_limit_bytes=5 * total * tokens * width + (4 << 20)
        ),
        name="join_rows",
    )(*stacks)


def expand_rows(rows, w_gate, w_up, start, columns):
    count, depth = rows.shape[0], w_gate.shape[0]

    def body(rows_ref, gate_ref, up_ref, hidden_ref):
        def step(first, batch):
            x = rows_ref[pl.ds(first, batch), :depth]
            tile = min(TILE, columns)
            for i in range(0, columns, tile):
                cut = slice(start + i, start + i + tile)
                gate = jnp.dot(x, gate_ref[:, cut], preferred_element_type=jnp.float32)
                up = jnp.dot(x, up_ref[:, cut], preferred_element_type=jnp.float32)
                value = gate / (1.0 + jnp.exp(-gate)) * up
                hidden_ref[pl.ds(first, batch), i : i + tile] = value.astype(hidden_ref.dtype)

        row_batches(count, step)

    return pl.pallas_call(
        body,
        out_shape=jax.ShapeDtypeStruct((count, columns), rows.dtype),
        in_specs=[pl.BlockSpec(memory_space=pltpu.VMEM)] * 3,
        out_specs=pl.BlockSpec(memory_space=pltpu.VMEM),
        cost_estimate=pl.CostEstimate(flops=0, bytes_accessed=count * columns, transcendentals=0),
        compiler_params=pltpu.CompilerParams(vmem_limit_bytes=rows.nbytes + (6 << 20)),
        name="expand_rows",
    )(rows, in_vmem(w_gate), in_vmem(w_up))


def contract_hidden(parts, w_down, units, before=None, rows=None, half=None, split=False):
    count, width = parts[0][0].shape[0], w_down.shape[1]
    experts = lax.axis_size(EXPERT)
    operands = [part for part, _, _ in parts] + [in_vmem(w_down)]
    operands += [value for value in (before, rows) if value is not None]

    def body(*refs):
        part_refs, down_ref = refs[: len(parts)], refs[len(parts)]
        rest = list(refs[len(parts) + 1 : len(operands)])
        outs = refs[len(operands) :]
        before_ref = rest.pop(0) if before is not None else None
        rows_ref = rest.pop(0) if rows is not None else None
        me, group = lax.axis_index(EXPERT), lax.axis_index("dp")

        def step(first, batch):
            here = pl.ds(first, batch)
            if half is None:
                lefts = [ref[here, :] for ref in part_refs]
            else:
                order = [i ^ 1 for i in range(count // half)]
                lefts = [
                    jnp.concatenate([ref[i * half : (i + 1) * half, :] for i in order])
                    for ref in part_refs
                ]
            if rows is not None:
                table = rows_ref[here, rows.shape[1] - LANES :].astype(jnp.float32)
                lane = lax.broadcasted_iota(jnp.int32, table.shape, 1)
                mine = (lax.rem(lane, experts) == me) & (lane < 3 * experts)
                scale = jnp.sum(jnp.where(mine, table, 0.0), axis=1, keepdims=True)
            tile = min(2 * TILE, width)
            for i in range(0, width, tile):
                cut = slice(i, i + tile)
                total = 0.0 if before is None else before_ref[here, cut]
                for left, (_, mask, unit) in zip(lefts, parts):
                    start = pl.multiple_of((group ^ mask) * units + unit, LANES)
                    right = down_ref[pl.ds(start, left.shape[1]), cut]
                    total = total + jnp.dot(left, right, preferred_element_type=jnp.float32)
                if rows is not None:
                    total = total.astype(jnp.bfloat16).astype(jnp.float32) * scale
                if not split:
                    outs[0][here, cut] = total
                    continue
                size, core = count // 8, lax.axis_index("core")
                for j in range(4):
                    near = total[2 * j * size : (2 * j + 1) * size]
                    away = total[(2 * j + 1) * size : (2 * j + 2) * size]
                    kept, sent = slice(j * size, (j + 1) * size), (j ^ 2) * size
                    outs[0][kept, cut] = jnp.where(core == 0, near, away)
                    other = jnp.where(core == 0, away, near).astype(jnp.bfloat16)
                    outs[1][sent : sent + size, cut] = other

        row_batches(count, step)

    shape = jax.ShapeDtypeStruct((count, width), jnp.float32)
    if split:
        kinds = (jnp.float32, jnp.bfloat16)
        shape = [jax.ShapeDtypeStruct((count // 2, width), kind) for kind in kinds]

    return pl.pallas_call(
        body,
        out_shape=shape,
        in_specs=[pl.BlockSpec(memory_space=pltpu.VMEM)] * len(operands),
        out_specs=[pl.BlockSpec(memory_space=pltpu.VMEM)] * 2
        if split
        else pl.BlockSpec(memory_space=pltpu.VMEM),
        cost_estimate=pl.CostEstimate(flops=0, bytes_accessed=count * width, transcendentals=0),
        compiler_params=pltpu.CompilerParams(
            vmem_limit_bytes=8 * count * width
            + (6 << 20)
            + (0 if rows is None else rows.nbytes)
        ),
        name="contract_hidden",
    )(*operands)


def sum_stage(inputs, plan, shape, dtype):
    def body(*refs):
        sources, targets = refs[: len(inputs)], refs[len(inputs) :]
        for target, blocks in zip(targets, plan):
            for i, block in enumerate(blocks):
                total = 0.0
                for ref in sources:
                    if len(ref.shape) == 2:
                        value = ref[block * shape[0] : (block + 1) * shape[0], :]
                    else:
                        value = ref[block]
                    total = total + value.astype(jnp.float32)
                target[i] = total.astype(target.dtype)

    return pl.pallas_call(
        body,
        out_shape=[
            jax.ShapeDtypeStruct((len(blocks),) + shape, dtype if i else jnp.float32)
            for i, blocks in enumerate(plan)
        ],
        in_specs=[pl.BlockSpec(memory_space=pltpu.VMEM)] * len(inputs),
        out_specs=[pl.BlockSpec(memory_space=pltpu.VMEM)] * len(plan),
        compiler_params=pltpu.CompilerParams(
            vmem_limit_bytes=sum(value.nbytes for value in inputs) * 2 + (6 << 20)
        ),
        name="sum_stage",
    )(*inputs)


def add_to_own(own, one, two, shape):
    count = own.shape[0] // 2

    def body(own_ref, one_ref, two_ref, kept_ref, sent_ref):
        core = lax.axis_index("core")

        def block(i):
            mine = jnp.where(core == 0, own_ref[i], two_ref[i].astype(jnp.float32))
            return mine + one_ref[i].astype(jnp.float32)

        for i in range(count):
            kept_ref[i] = block(2 * i + core)
            sent_ref[i ^ (count // 2)] = block(2 * i + 1 - core).astype(sent_ref.dtype)

    return pl.pallas_call(
        body,
        out_shape=[
            jax.ShapeDtypeStruct((count,) + shape, kind) for kind in (jnp.float32, one.dtype)
        ],
        in_specs=[pl.BlockSpec(memory_space=pltpu.VMEM)] * 3,
        out_specs=[pl.BlockSpec(memory_space=pltpu.VMEM)] * 2,
        compiler_params=pltpu.CompilerParams(vmem_limit_bytes=4 * own.nbytes + (4 << 20)),
        name="add_to_own",
    )(own, one, two)


def pick_columns(own, one, two, shape):
    def body(own_ref, one_ref, two_ref, kept_ref, sent_ref):
        core = lax.axis_index("core")
        for i, ref in enumerate((kept_ref, sent_ref)):
            mine = jnp.where(core == 0, own_ref[i], two_ref[i].astype(jnp.float32))
            ref[0] = mine.astype(ref.dtype)
            ref[1] = one_ref[i].astype(ref.dtype)

    return pl.pallas_call(
        body,
        out_shape=[jax.ShapeDtypeStruct((2,) + shape, kind) for kind in (jnp.float32, one.dtype)],
        in_specs=[pl.BlockSpec(memory_space=pltpu.VMEM)] * 3,
        out_specs=[pl.BlockSpec(memory_space=pltpu.VMEM)] * 2,
        compiler_params=pltpu.CompilerParams(vmem_limit_bytes=4 * own.nbytes + (4 << 20)),
        name="pick_columns",
    )(own, one, two)


def finish(kept, received, groups):
    _, tokens, wide_columns = kept.shape
    columns = 2 * wide_columns // groups

    def body(kept_ref, received_ref, out_ref):
        group = lax.axis_index("dp")
        for g in range(groups):
            place = slice((g >> 1) * columns, ((g >> 1) + 1) * columns)
            total = kept_ref[g & 1, :, place] + received_ref[g & 1, :, place].astype(jnp.float32)
            start = pl.multiple_of((group ^ g) * columns, LANES)
            out_ref[:, pl.ds(start, columns)] = total.astype(out_ref.dtype)

    return pl.pallas_call(
        body,
        out_shape=jax.ShapeDtypeStruct((tokens, groups * columns), received.dtype),
        in_specs=[pl.BlockSpec(memory_space=pltpu.VMEM)] * 2,
        out_specs=pl.BlockSpec(memory_space=pltpu.VMEM),
        compiler_params=pltpu.CompilerParams(vmem_limit_bytes=4 << 20),
        name="finish",
    )(kept, received)


def local(tokens, expert_ids, gate_probs, w_gate, w_up, w_down):
    token_count, width = tokens.shape
    groups, experts = lax.axis_size("dp"), lax.axis_size(EXPERT)
    wide, high = groups // 2, experts // 4

    block = pack_block(tokens, expert_ids, gate_probs, experts)
    units = w_up.shape[2]
    weights = lax.optimization_barrier((block, w_gate[0], w_up[0], w_down[0]))
    block, gate_weights, up_weights, down_weights = weights
    near = stack_blocks([block] + [swap(block, 0, 4 * i) for i in range(1, high)])
    if wide > 1:
        near = jnp.concatenate([near] + [swap(near, 2 * i, 0) for i in range(1, wide)])
    chip = join_rows([near, swap(near, 0, 2), swap(near, 1, 0), swap(near, 1, 2)])
    rows = jnp.concatenate([chip, swap(chip, 0, 1)])

    chunks = CHUNKS if units % (LANES * CHUNKS) == 0 else 1
    step = units // chunks
    half = rows.shape[0] // 4 if groups == 2 and rows.shape[0] <= BATCH else None

    def from_group(value, mask):
        value = swap(value, mask, 0)
        if half is not None:
            return value
        value = value.reshape(2, 2, 2, wide, high * token_count, step)
        value = jnp.stack([value[:, i ^ (mask & 1)] for i in range(2)], axis=1)
        value = jnp.stack([value[:, :, :, i ^ (mask >> 1)] for i in range(wide)], axis=3)
        return value.reshape(-1, step)

    hidden, others = [], []
    for i in range(chunks):
        if hidden:
            rows, hidden[-1] = lax.optimization_barrier((rows, hidden[-1]))
        hidden.append(expand_rows(rows, gate_weights, up_weights, i * step, step))
        others.append(
            [(from_group(hidden[-1], mask), mask, i * step) for mask in range(1, groups)]
        )
    parts = [(value, 0, i * step) for i, value in enumerate(hidden)]
    total = contract_hidden(parts, down_weights, units)
    for i in range(chunks - 1):
        total = contract_hidden(others[i], down_weights, units, total, half=half)
    columns = w_down.shape[2]
    if rows.shape[0] <= BATCH:
        kept, sent = contract_hidden(
            others[-1], down_weights, units, total, rows, half, split=True
        )
    else:
        total = contract_hidden(others[-1], down_weights, units, total, rows, half)
        total = total.reshape(2, 2, 2, -1, columns)
        core = lax.axis_index("core")
        kept = lax.dynamic_index_in_dim(total, core, 2, False).reshape(-1, columns)
        sent = lax.dynamic_index_in_dim(total, 1 - core, 2, False)[::-1]
        sent = sent.reshape(-1, columns).astype(jnp.bfloat16)
    inputs = [kept, swap(sent, 0, 1)]
    if wide * high > 4:
        total = kept + inputs[1].astype(jnp.float32)
        total = total.reshape(4, wide, high // 4, 4 * token_count, columns)
        send = lambda value, g, e: swap(value.astype(jnp.bfloat16), g, e).astype(jnp.float32)
        total = total[:, :, 0] + sum(
            send(total[:, :, i], 0, 16 * i) for i in range(1, high // 4)
        )
        total = [total[:, 0]] + [send(total[:, i], 2 * i, 0) for i in range(1, wide)]
        inputs = [jnp.concatenate(total, axis=2).reshape(16, token_count, wide * columns)]
    shape = (token_count, wide * columns)
    low, up = range(0, 16, 2), range(1, 16, 2)
    own, near, away = sum_stage(inputs, [low, low, up], shape, jnp.bfloat16)
    one = permute(away, ((0, 4), (0, 6)))
    two = permute(near, (None, (0, 2)))
    kept, sent = add_to_own(own, one, two, shape)
    inputs = [kept, swap(sent, 0, 1)]
    own, near, away = sum_stage(inputs, [(0, 2), (0, 2), (1, 3)], shape, jnp.bfloat16)
    one = permute(away, ((1, 0), (1, 8)))
    two = permute(near, (None, (0, 8)))
    kept, sent = pick_columns(own, one, two, shape)
    return finish(kept, swap(sent, 0, 1), groups)


def solution(mesh):
    groups, experts = mesh.devices.shape
    split = Mesh(mesh.devices.reshape(groups, experts // 2, 2), ("dp", "far", "core"))
    row, expert = P(("dp", "far", "core"), None), P(EXPERT, None, "dp")
    return jax.shard_map(
        local,
        mesh=split,
        in_specs=(row, row, row, expert, expert, expert),
        out_specs=row,
        check_vma=False,
    )
```

```python
import jax
import jax.numpy as jnp
from jax import lax
from jax.experimental import pallas as pl
from jax.experimental.pallas import tpu as pltpu
from jax.sharding import Mesh
from jax.sharding import PartitionSpec as P

CHUNKS = 2
TILE = 256
BATCH = 128
LANES = 128
EXPERT = ("far", "core")


def swap(value, group_mask, expert_mask):
    groups, experts = lax.axis_size("dp"), lax.axis_size(EXPERT)
    pairs = [
        (g * experts + e, (g ^ group_mask) * experts + (e ^ expert_mask))
        for g in range(groups)
        for e in range(experts)
    ]
    return lax.ppermute(value, ("dp",) + EXPERT, pairs)


def in_vmem(value):
    return pltpu.with_memory_space_constraint(value, pltpu.VMEM)


def in_hbm(value):
    return pltpu.with_memory_space_constraint(value, pltpu.HBM)


def row_batches(count, step):
    batch = min(BATCH, count)
    if count == batch:
        step(0, batch)
    else:

        @pl.loop(0, count // batch)
        def _(i):
            step(pl.multiple_of(i * batch, batch), batch)


def pack_block(tokens, expert_ids, gate_probs, experts):
    count, width = tokens.shape
    top = expert_ids.shape[1]

    def body(tokens_ref, ids_ref, probs_ref, block_ref):
        block_ref[:, :width] = tokens_ref[...]
        lane = lax.broadcasted_iota(jnp.int32, (count, LANES), 1)
        table = jnp.zeros((count, LANES), jnp.float32)
        for k in range(top):
            hit = ids_ref[:, k : k + 1] == lax.rem(lane, experts)
            table = jnp.where(hit, probs_ref[:, k : k + 1], table)
        packed = jnp.zeros((count, LANES), jnp.float32)
        for i in range(3):
            part = table.astype(jnp.bfloat16).astype(jnp.float32)
            packed = jnp.where(lane // experts == i, part, packed)
            table = table - part
        block_ref[:, width:] = packed.astype(block_ref.dtype)

    return pl.pallas_call(
        body,
        out_shape=jax.ShapeDtypeStruct((count, width + LANES), tokens.dtype),
        in_specs=[pl.BlockSpec(memory_space=pltpu.VMEM)] * 3,
        out_specs=pl.BlockSpec(memory_space=pltpu.VMEM),
        cost_estimate=pl.CostEstimate(flops=60 * 10**9, bytes_accessed=0, transcendentals=0),
        compiler_params=pltpu.CompilerParams(vmem_limit_bytes=1 << 20),
        name="pack_block",
    )(in_hbm(tokens), in_hbm(expert_ids), in_hbm(gate_probs))


def stack_blocks(blocks):
    def body(*refs):
        for i, ref in enumerate(refs[:-1]):
            refs[-1][i] = ref[...]

    return pl.pallas_call(
        body,
        out_shape=jax.ShapeDtypeStruct((len(blocks),) + blocks[0].shape, blocks[0].dtype),
        in_specs=[pl.BlockSpec(memory_space=pltpu.VMEM)] * len(blocks),
        out_specs=pl.BlockSpec(memory_space=pltpu.VMEM),
        compiler_params=pltpu.CompilerParams(vmem_limit_bytes=4 << 20),
        name="stack_blocks",
    )(*blocks)


def join_rows(stacks):
    blocks, tokens, width = stacks[0].shape
    total = len(stacks) * blocks
    batch = max(1, 16 // tokens)

    def body(*refs):
        for i in range(0, total, batch):
            group = [refs[j // blocks][j % blocks] for j in range(i, i + batch)]
            rows = jnp.concatenate([value.astype(jnp.float32) for value in group])
            refs[-1][i * tokens : (i + batch) * tokens, :] = rows.astype(refs[-1].dtype)

    return pl.pallas_call(
        body,
        out_shape=jax.ShapeDtypeStruct((total * tokens, width), stacks[0].dtype),
        in_specs=[pl.BlockSpec(memory_space=pltpu.VMEM)] * len(stacks),
        out_specs=pl.BlockSpec(memory_space=pltpu.VMEM),
        compiler_params=pltpu.CompilerParams(
            vmem_limit_bytes=5 * total * tokens * width + (4 << 20)
        ),
        name="join_rows",
    )(*stacks)


def expand_rows(rows, w_gate, w_up, start, columns):
    count, depth = rows.shape[0], w_gate.shape[0]

    def body(rows_ref, gate_ref, up_ref, hidden_ref):
        def step(first, batch):
            x = rows_ref[pl.ds(first, batch), :depth]
            tile = min(TILE, columns)
            for i in range(0, columns, tile):
                cut = slice(start + i, start + i + tile)
                gate = jnp.dot(x, gate_ref[:, cut], preferred_element_type=jnp.float32)
                up = jnp.dot(x, up_ref[:, cut], preferred_element_type=jnp.float32)
                value = gate / (1.0 + jnp.exp(-gate)) * up
                hidden_ref[pl.ds(first, batch), i : i + tile] = value.astype(hidden_ref.dtype)

        row_batches(count, step)

    return pl.pallas_call(
        body,
        out_shape=jax.ShapeDtypeStruct((count, columns), rows.dtype),
        in_specs=[pl.BlockSpec(memory_space=pltpu.VMEM)] * 3,
        out_specs=pl.BlockSpec(memory_space=pltpu.VMEM),
        cost_estimate=pl.CostEstimate(flops=0, bytes_accessed=count * columns, transcendentals=0),
        compiler_params=pltpu.CompilerParams(vmem_limit_bytes=rows.nbytes + (6 << 20)),
        name="expand_rows",
    )(rows, in_vmem(w_gate), in_vmem(w_up))


def contract_hidden(
    parts, w_down, units, before=None, rows=None, half=None, index=None, kind=jnp.float32
):
    total_count, width = parts[0][0].shape[0], w_down.shape[1]
    count = total_count if index is None else total_count // 2
    offset = 0 if index is None else index * count
    experts = lax.axis_size(EXPERT)
    operands = [part for part, _, _ in parts] + [in_vmem(w_down)]
    operands += [value for value in (before, rows) if value is not None]

    def body(*refs):
        part_refs, down_ref = refs[: len(parts)], refs[len(parts)]
        rest = list(refs[len(parts) + 1 : -1])
        before_ref = rest.pop(0) if before is not None else None
        rows_ref = rest.pop(0) if rows is not None else None
        me, group = lax.axis_index(EXPERT), lax.axis_index("dp")

        def step(first, batch):
            here = pl.ds(offset + first, batch)
            if half is None:
                lefts = [ref[here, :] for ref in part_refs]
            else:
                order = [i ^ 1 for i in range(offset // half, (offset + count) // half)]
                lefts = [
                    jnp.concatenate([ref[i * half : (i + 1) * half, :] for i in order])
                    for ref in part_refs
                ]
            if rows is not None:
                table = rows_ref[here, rows.shape[1] - LANES :].astype(jnp.float32)
                lane = lax.broadcasted_iota(jnp.int32, table.shape, 1)
                mine = (lax.rem(lane, experts) == me) & (lane < 3 * experts)
                scale = jnp.sum(jnp.where(mine, table, 0.0), axis=1, keepdims=True)
            tile = min(2 * TILE, width)
            for i in range(0, width, tile):
                cut = slice(i, i + tile)
                total = 0.0 if before is None else before_ref[here, cut]
                for left, (_, mask, unit) in zip(lefts, parts):
                    start = pl.multiple_of((group ^ mask) * units + unit, LANES)
                    right = down_ref[pl.ds(start, left.shape[1]), cut]
                    total = total + jnp.dot(left, right, preferred_element_type=jnp.float32)
                if rows is not None:
                    total = total.astype(jnp.bfloat16).astype(jnp.float32) * scale
                refs[-1][pl.ds(first, batch), cut] = total.astype(kind)

        row_batches(count, step)

    return pl.pallas_call(
        body,
        out_shape=jax.ShapeDtypeStruct((count, width), kind),
        in_specs=[pl.BlockSpec(memory_space=pltpu.VMEM)] * len(operands),
        out_specs=pl.BlockSpec(memory_space=pltpu.VMEM),
        cost_estimate=pl.CostEstimate(flops=0, bytes_accessed=count * width, transcendentals=0),
        compiler_params=pltpu.CompilerParams(
            vmem_limit_bytes=8 * total_count * width
            + (6 << 20)
            + (0 if rows is None else rows.nbytes)
        ),
        name="contract_hidden",
    )(*operands)


def sum_stage(inputs, plan, shape, dtype):
    def body(*refs):
        sources, targets = refs[: len(inputs)], refs[len(inputs) :]
        for target, blocks in zip(targets, plan):
            for i, block in enumerate(blocks):
                total = 0.0
                for ref in sources:
                    if len(ref.shape) == 2:
                        value = ref[block * shape[0] : (block + 1) * shape[0], :]
                    else:
                        value = ref[block]
                    total = total + value.astype(jnp.float32)
                target[i] = total.astype(target.dtype)

    return pl.pallas_call(
        body,
        out_shape=[
            jax.ShapeDtypeStruct((len(blocks),) + shape, dtype if i else jnp.float32)
            for i, blocks in enumerate(plan)
        ],
        in_specs=[pl.BlockSpec(memory_space=pltpu.VMEM)] * len(inputs),
        out_specs=[pl.BlockSpec(memory_space=pltpu.VMEM)] * len(plan),
        compiler_params=pltpu.CompilerParams(
            vmem_limit_bytes=sum(value.nbytes for value in inputs) * 2 + (6 << 20)
        ),
        name="sum_stage",
    )(*inputs)


def finish(parts, groups, dtype):
    tokens, columns = parts[0][0].shape[1:]

    def body(*refs):
        group = lax.axis_index("dp")
        for i in range(groups):
            mine = [ref[0] for ref, (_, j) in zip(refs, parts) if i == j]
            total = sum(value.astype(jnp.float32) for value in mine)
            start = pl.multiple_of((group ^ i) * columns, LANES)
            refs[-1][:, pl.ds(start, columns)] = total.astype(dtype)

    return pl.pallas_call(
        body,
        out_shape=jax.ShapeDtypeStruct((tokens, groups * columns), dtype),
        in_specs=[pl.BlockSpec(memory_space=pltpu.VMEM)] * len(parts),
        out_specs=pl.BlockSpec(memory_space=pltpu.VMEM),
        compiler_params=pltpu.CompilerParams(vmem_limit_bytes=4 << 20),
        name="finish",
    )(*[value for value, _ in parts])


def local(tokens, expert_ids, gate_probs, w_gate, w_up, w_down):
    token_count, width = tokens.shape
    groups, experts = lax.axis_size("dp"), lax.axis_size(EXPERT)
    wide, high = groups // 2, experts // 4

    block = pack_block(tokens, expert_ids, gate_probs, experts)
    units = w_up.shape[2]
    weights = lax.optimization_barrier((block, w_gate[0], w_up[0], w_down[0]))
    block, gate_weights, up_weights, down_weights = weights
    near = stack_blocks([block] + [swap(block, 0, 4 * i) for i in range(1, high)])
    if wide > 1:
        near = jnp.concatenate([near] + [swap(near, 2 * i, 0) for i in range(1, wide)])
    over_y = swap(near, 0, 2)
    first = join_rows([near, swap(near, 1, 0), swap(near, 1, 2)])
    last = join_rows([over_y])
    size = last.shape[0]
    rows = []
    for one, two in ((first, last), (swap(first, 0, 1), swap(last, 0, 1))):
        rows += [one[:size], two, one[size:]]
    rows = jnp.concatenate(rows)

    chunks = CHUNKS if units % (LANES * CHUNKS) == 0 else 1
    step = units // chunks
    half = rows.shape[0] // 4 if groups == 2 and rows.shape[0] <= BATCH else None

    def from_group(value, mask):
        value = swap(value, mask, 0)
        if half is not None:
            return value
        value = value.reshape(2, 2, 2, wide, high * token_count, step)
        value = jnp.stack([value[:, i ^ (mask & 1)] for i in range(2)], axis=1)
        value = jnp.stack([value[:, :, :, i ^ (mask >> 1)] for i in range(wide)], axis=3)
        return value.reshape(-1, step)

    hidden, others = [], []
    for i in range(chunks):
        if hidden:
            rows, hidden[-1] = lax.optimization_barrier((rows, hidden[-1]))
        hidden.append(expand_rows(rows, gate_weights, up_weights, i * step, step))
        others.append(
            [(from_group(hidden[-1], mask), mask, i * step) for mask in range(1, groups)]
        )
    parts = [(value, 0, i * step) for i, value in enumerate(hidden)]
    total = contract_hidden(parts, down_weights, units)
    for i in range(chunks - 1):
        total = contract_hidden(others[i], down_weights, units, total, half=half)
    last = lambda index, kind: contract_hidden(
        others[-1], down_weights, units, total, rows, half, index, kind
    )
    sent, kept = last(1, jnp.bfloat16), last(0, jnp.float32)

    shape = (token_count, w_down.shape[2])
    rest = [(g, h) for g in range(groups) for h in range(0, high, 2)]
    slot = lambda g, y, h: (((g & 1) * 2 + y) * wide + (g >> 1)) * high + h
    plan = [[slot(g, y, h + z) for g, h in rest] for y, z in ((0, 0), (1, 1), (0, 1), (1, 0))]
    mine, *away = sum_stage([kept, swap(sent, 0, 1)], plan, shape, jnp.bfloat16)
    inputs = [mine] + [swap(value, 0, mask) for value, mask in zip(away, (6, 4, 2))]
    order = sorted(range(1, len(rest)), key=lambda i: (rest[i][1], rest[i][0]), reverse=True)
    mine, *away = sum_stage(inputs, [[i] for i in [0] + order], shape, jnp.bfloat16)
    parts = [
        (swap(value, rest[i][0], 4 * rest[i][1]), rest[i][0]) for value, i in zip(away, order)
    ]
    return finish(parts + [(mine, 0)], groups, tokens.dtype)


def solution(mesh):
    groups, experts = mesh.devices.shape
    split = Mesh(mesh.devices.reshape(groups, experts // 2, 2), ("dp", "far", "core"))
    row, expert = P(("dp", "far", "core"), None), P(EXPERT, None, "dp")
    return jax.shard_map(
        local,
        mesh=split,
        in_specs=(row, row, row, expert, expert, expert),
        out_specs=row,
        check_vma=False,
    )
```

```python
import jax
import jax.numpy as jnp
from jax import lax
from jax.experimental import pallas as pl
from jax.experimental.pallas import tpu as pltpu
from jax.sharding import Mesh
from jax.sharding import PartitionSpec as P

CHUNKS = 2
TILE = 256
BATCH = 128
LANES = 128
EXPERT = ("far", "core")


def swap(value, group_mask, expert_mask):
    groups, experts = lax.axis_size("dp"), lax.axis_size(EXPERT)
    pairs = [
        (g * experts + e, (g ^ group_mask) * experts + (e ^ expert_mask))
        for g in range(groups)
        for e in range(experts)
    ]
    return lax.ppermute(value, ("dp",) + EXPERT, pairs)


def in_vmem(value):
    return pltpu.with_memory_space_constraint(value, pltpu.VMEM)


def in_hbm(value):
    return pltpu.with_memory_space_constraint(value, pltpu.HBM)


def row_batches(count, step):
    batch = min(BATCH, count)
    if count == batch:
        step(0, batch)
    else:

        @pl.loop(0, count // batch)
        def _(i):
            step(pl.multiple_of(i * batch, batch), batch)


def pack_block(tokens, expert_ids, gate_probs, experts):
    count, width = tokens.shape
    top = expert_ids.shape[1]

    def body(tokens_ref, ids_ref, probs_ref, block_ref):
        block_ref[:, :width] = tokens_ref[...]
        lane = lax.broadcasted_iota(jnp.int32, (count, LANES), 1)
        table = jnp.zeros((count, LANES), jnp.float32)
        for k in range(top):
            hit = ids_ref[:, k : k + 1] == lax.rem(lane, experts)
            table = jnp.where(hit, probs_ref[:, k : k + 1], table)
        packed = jnp.zeros((count, LANES), jnp.float32)
        for i in range(3):
            part = table.astype(jnp.bfloat16).astype(jnp.float32)
            packed = jnp.where(lane // experts == i, part, packed)
            table = table - part
        block_ref[:, width:] = packed.astype(block_ref.dtype)

    return pl.pallas_call(
        body,
        out_shape=jax.ShapeDtypeStruct((count, width + LANES), tokens.dtype),
        in_specs=[pl.BlockSpec(memory_space=pltpu.VMEM)] * 3,
        out_specs=pl.BlockSpec(memory_space=pltpu.VMEM),
        cost_estimate=pl.CostEstimate(flops=60 * 10**9, bytes_accessed=0, transcendentals=0),
        compiler_params=pltpu.CompilerParams(vmem_limit_bytes=1 << 20),
        name="pack_block",
    )(in_hbm(tokens), in_hbm(expert_ids), in_hbm(gate_probs))


def stack_blocks(blocks):
    def body(*refs):
        for i, ref in enumerate(refs[:-1]):
            refs[-1][i] = ref[...]

    return pl.pallas_call(
        body,
        out_shape=jax.ShapeDtypeStruct((len(blocks),) + blocks[0].shape, blocks[0].dtype),
        in_specs=[pl.BlockSpec(memory_space=pltpu.VMEM)] * len(blocks),
        out_specs=pl.BlockSpec(memory_space=pltpu.VMEM),
        compiler_params=pltpu.CompilerParams(vmem_limit_bytes=4 << 20),
        name="stack_blocks",
    )(*blocks)


def join_rows(stacks):
    blocks, tokens, width = stacks[0].shape
    total = len(stacks) * blocks
    batch = max(1, 16 // tokens)

    def body(*refs):
        for i in range(0, total, batch):
            group = [refs[j // blocks][j % blocks] for j in range(i, i + batch)]
            rows = jnp.concatenate([value.astype(jnp.float32) for value in group])
            refs[-1][i * tokens : (i + batch) * tokens, :] = rows.astype(refs[-1].dtype)

    return pl.pallas_call(
        body,
        out_shape=jax.ShapeDtypeStruct((total * tokens, width), stacks[0].dtype),
        in_specs=[pl.BlockSpec(memory_space=pltpu.VMEM)] * len(stacks),
        out_specs=pl.BlockSpec(memory_space=pltpu.VMEM),
        compiler_params=pltpu.CompilerParams(
            vmem_limit_bytes=5 * total * tokens * width + (4 << 20)
        ),
        name="join_rows",
    )(*stacks)


def expand_rows(rows, w_gate, w_up, start, columns):
    count, depth = rows.shape[0], w_gate.shape[0]

    def body(rows_ref, gate_ref, up_ref, hidden_ref):
        def step(first, batch):
            x = rows_ref[pl.ds(first, batch), :depth]
            tile = min(TILE, columns)
            for i in range(0, columns, tile):
                cut = slice(start + i, start + i + tile)
                gate = jnp.dot(x, gate_ref[:, cut], preferred_element_type=jnp.float32)
                up = jnp.dot(x, up_ref[:, cut], preferred_element_type=jnp.float32)
                value = gate / (1.0 + jnp.exp(-gate)) * up
                hidden_ref[pl.ds(first, batch), i : i + tile] = value.astype(hidden_ref.dtype)

        row_batches(count, step)

    return pl.pallas_call(
        body,
        out_shape=jax.ShapeDtypeStruct((count, columns), rows.dtype),
        in_specs=[pl.BlockSpec(memory_space=pltpu.VMEM)] * 3,
        out_specs=pl.BlockSpec(memory_space=pltpu.VMEM),
        cost_estimate=pl.CostEstimate(flops=0, bytes_accessed=count * columns, transcendentals=0),
        compiler_params=pltpu.CompilerParams(vmem_limit_bytes=rows.nbytes + (6 << 20)),
        name="expand_rows",
    )(rows, in_vmem(w_gate), in_vmem(w_up))


def contract_hidden(
    parts, w_down, units, before=None, rows=None, half=None, index=None, span=None
):
    left_column, right_column = span or (0, w_down.shape[1])
    kind = jnp.float32 if span is None else jnp.bfloat16
    total_count, width = parts[0][0].shape[0], right_column - left_column
    count = total_count if index is None else total_count // 2
    offset = 0 if index is None else index * count
    experts = lax.axis_size(EXPERT)
    operands = [part for part, _, _ in parts] + [in_vmem(w_down)]
    operands += [value for value in (before, rows) if value is not None]

    def body(*refs):
        part_refs, down_ref = refs[: len(parts)], refs[len(parts)]
        rest = list(refs[len(parts) + 1 : -1])
        before_ref = rest.pop(0) if before is not None else None
        rows_ref = rest.pop(0) if rows is not None else None
        me, group = lax.axis_index(EXPERT), lax.axis_index("dp")

        def step(first, batch):
            here = pl.ds(offset + first, batch)
            if half is None:
                lefts = [ref[here, :] for ref in part_refs]
            else:
                order = [i ^ 1 for i in range(offset // half, (offset + count) // half)]
                lefts = [
                    jnp.concatenate([ref[i * half : (i + 1) * half, :] for i in order])
                    for ref in part_refs
                ]
            if rows is not None:
                table = rows_ref[here, rows.shape[1] - LANES :].astype(jnp.float32)
                lane = lax.broadcasted_iota(jnp.int32, table.shape, 1)
                mine = (lax.rem(lane, experts) == me) & (lane < 3 * experts)
                scale = jnp.sum(jnp.where(mine, table, 0.0), axis=1, keepdims=True)
            tile = min(2 * TILE, width)
            for i in range(0, width, tile):
                cut = slice(left_column + i, left_column + i + tile)
                total = 0.0 if before is None else before_ref[here, cut]
                for left, (_, mask, unit) in zip(lefts, parts):
                    start = pl.multiple_of((group ^ mask) * units + unit, LANES)
                    right = down_ref[pl.ds(start, left.shape[1]), cut]
                    total = total + jnp.dot(left, right, preferred_element_type=jnp.float32)
                if rows is not None:
                    total = total.astype(jnp.bfloat16).astype(jnp.float32) * scale
                refs[-1][pl.ds(first, batch), i : i + tile] = total.astype(kind)

        row_batches(count, step)

    return pl.pallas_call(
        body,
        out_shape=jax.ShapeDtypeStruct((count, width), kind),
        in_specs=[pl.BlockSpec(memory_space=pltpu.VMEM)] * len(operands),
        out_specs=pl.BlockSpec(memory_space=pltpu.VMEM),
        cost_estimate=pl.CostEstimate(flops=0, bytes_accessed=count * width, transcendentals=0),
        compiler_params=pltpu.CompilerParams(
            vmem_limit_bytes=8 * total_count * w_down.shape[1]
            + (6 << 20)
            + (0 if rows is None else rows.nbytes)
        ),
        name="contract_hidden",
    )(*operands)


def sum_stage(inputs, plan, shape, dtype):
    inputs = [value if isinstance(value, list) else [value] for value in inputs]
    flat = [piece for value in inputs for piece in value]
    def body(*refs):
        sources, targets = list(refs[: len(flat)]), refs[len(flat) :]
        sources = [[sources.pop(0) for _ in value] for value in inputs]
        for target, blocks in zip(targets, plan):
            for i, block in enumerate(blocks):
                total = 0.0
                for source in sources:
                    here = slice(block * shape[0], (block + 1) * shape[0])
                    pieces = [ref[here, :] if ref.ndim == 2 else ref[block] for ref in source]
                    pieces = [piece.astype(jnp.float32) for piece in pieces]
                    total = total + jnp.concatenate(pieces, axis=1)
                target[i] = total.astype(target.dtype)

    return pl.pallas_call(
        body,
        out_shape=[
            jax.ShapeDtypeStruct((len(blocks),) + shape, dtype if i else jnp.float32)
            for i, blocks in enumerate(plan)
        ],
        in_specs=[pl.BlockSpec(memory_space=pltpu.VMEM)] * len(flat),
        out_specs=[pl.BlockSpec(memory_space=pltpu.VMEM)] * len(plan),
        compiler_params=pltpu.CompilerParams(
            vmem_limit_bytes=sum(value.nbytes for value in flat) * 2 + (6 << 20)
        ),
        name="sum_stage",
    )(*flat)


def finish(parts, groups, dtype):
    tokens, columns = parts[0][0].shape[1:]

    def body(*refs):
        group = lax.axis_index("dp")
        for i in range(groups):
            mine = [ref[0] for ref, (_, j) in zip(refs, parts) if i == j]
            total = sum(value.astype(jnp.float32) for value in mine)
            start = pl.multiple_of((group ^ i) * columns, LANES)
            refs[-1][:, pl.ds(start, columns)] = total.astype(dtype)

    return pl.pallas_call(
        body,
        out_shape=jax.ShapeDtypeStruct((tokens, groups * columns), dtype),
        in_specs=[pl.BlockSpec(memory_space=pltpu.VMEM)] * len(parts),
        out_specs=pl.BlockSpec(memory_space=pltpu.VMEM),
        compiler_params=pltpu.CompilerParams(vmem_limit_bytes=4 << 20),
        name="finish",
    )(*[value for value, _ in parts])


def local(tokens, expert_ids, gate_probs, w_gate, w_up, w_down):
    token_count, width = tokens.shape
    groups, experts = lax.axis_size("dp"), lax.axis_size(EXPERT)
    wide, high = groups // 2, experts // 4

    block = pack_block(tokens, expert_ids, gate_probs, experts)
    units = w_up.shape[2]
    weights = lax.optimization_barrier((block, w_gate[0], w_up[0], w_down[0]))
    block, gate_weights, up_weights, down_weights = weights
    near = stack_blocks([block] + [swap(block, 0, 4 * i) for i in range(1, high)])
    if wide > 1:
        near = jnp.concatenate([near] + [swap(near, 2 * i, 0) for i in range(1, wide)])
    over_x, over_y = swap(near, 1, 0), swap(near, 0, 2)
    first = join_rows([near, swap(near, 1, 2)])
    pieces = [first, join_rows([over_x]), join_rows([over_y])]
    size = pieces[1].shape[0]
    rows = []
    for first, x, y in (pieces, [swap(piece, 0, 1) for piece in pieces]):
        rows += [first[:size], y, x, first[size:]]
    rows = jnp.concatenate(rows)

    chunks = CHUNKS if units % (LANES * CHUNKS) == 0 else 1
    step = units // chunks
    half = rows.shape[0] // 4 if groups == 2 and rows.shape[0] <= BATCH else None

    def from_group(value, mask):
        value = swap(value, mask, 0)
        if half is not None:
            return value
        value = value.reshape(2, 2, 2, wide, high * token_count, step)
        value = jnp.stack([value[:, i ^ (mask & 1)] for i in range(2)], axis=1)
        value = jnp.stack([value[:, :, :, i ^ (mask >> 1)] for i in range(wide)], axis=3)
        return value.reshape(-1, step)

    hidden, others = [], []
    for i in range(chunks):
        if hidden:
            rows, hidden[-1] = lax.optimization_barrier((rows, hidden[-1]))
        hidden.append(expand_rows(rows, gate_weights, up_weights, i * step, step))
        others.append(
            [(from_group(hidden[-1], mask), mask, i * step) for mask in range(1, groups)]
        )
    parts = [(value, 0, i * step) for i, value in enumerate(hidden)]
    total = contract_hidden(parts, down_weights, units)
    for i in range(chunks - 1):
        total = contract_hidden(others[i], down_weights, units, total, half=half)
    columns = w_down.shape[2]
    last = lambda index, span: contract_hidden(
        others[-1], down_weights, units, total, rows, half, index, span
    )
    sent = [last(1, span) for span in ((0, columns // 2), (columns // 2, columns))]
    kept = last(0, None)

    shape = (token_count, columns)
    rest = [(g, h) for g in range(groups) for h in range(0, high, 2)]
    slot = lambda g, y, h: (((g & 1) * 2 + y) * wide + (g >> 1)) * high + h
    plan = [[slot(g, y, h + z) for g, h in rest] for y, z in ((0, 0), (1, 1), (0, 1), (1, 0))]
    mine, *away = sum_stage([kept, [swap(value, 0, 1) for value in sent]], plan, shape, jnp.bfloat16)
    inputs = [mine] + [swap(value, 0, mask) for value, mask in zip(away, (6, 4, 2))]
    order = sorted(range(1, len(rest)), key=lambda i: (rest[i][1], rest[i][0]), reverse=True)
    mine, *away = sum_stage(inputs, [[i] for i in [0] + order], shape, jnp.bfloat16)
    parts = [
        (swap(value, rest[i][0], 4 * rest[i][1]), rest[i][0]) for value, i in zip(away, order)
    ]
    return finish(parts + [(mine, 0)], groups, tokens.dtype)


def solution(mesh):
    groups, experts = mesh.devices.shape
    split = Mesh(mesh.devices.reshape(groups, experts // 2, 2), ("dp", "far", "core"))
    row, expert = P(("dp", "far", "core"), None), P(EXPERT, None, "dp")
    return jax.shard_map(
        local,
        mesh=split,
        in_specs=(row, row, row, expert, expert, expert),
        out_specs=row,
        check_vma=False,
    )
```

```python
import jax
import jax.numpy as jnp
from jax import lax
from jax.experimental import pallas as pl
from jax.experimental.pallas import tpu as pltpu
from jax.sharding import Mesh
from jax.sharding import PartitionSpec as P

CHUNKS = 2
TILE = 256
BATCH = 128
LANES = 128
EXPERT = ("far", "core")


def swap(value, group_mask, expert_mask):
    groups, experts = lax.axis_size("dp"), lax.axis_size(EXPERT)
    pairs = [
        (g * experts + e, (g ^ group_mask) * experts + (e ^ expert_mask))
        for g in range(groups)
        for e in range(experts)
    ]
    return lax.ppermute(value, ("dp",) + EXPERT, pairs)


def in_vmem(value):
    return pltpu.with_memory_space_constraint(value, pltpu.VMEM)


def in_hbm(value):
    return pltpu.with_memory_space_constraint(value, pltpu.HBM)


def row_batches(count, step):
    batch = min(BATCH, count)
    if count == batch:
        step(0, batch)
    else:

        @pl.loop(0, count // batch)
        def _(i):
            step(pl.multiple_of(i * batch, batch), batch)


def pack_block(tokens, expert_ids, gate_probs, experts):
    count, width = tokens.shape
    top = expert_ids.shape[1]

    def body(tokens_ref, ids_ref, probs_ref, block_ref):
        block_ref[:, :width] = tokens_ref[...]
        lane = lax.broadcasted_iota(jnp.int32, (count, LANES), 1)
        table = jnp.zeros((count, LANES), jnp.float32)
        for k in range(top):
            hit = ids_ref[:, k : k + 1] == lax.rem(lane, experts)
            table = jnp.where(hit, probs_ref[:, k : k + 1], table)
        packed = jnp.zeros((count, LANES), jnp.float32)
        for i in range(3):
            part = table.astype(jnp.bfloat16).astype(jnp.float32)
            packed = jnp.where(lane // experts == i, part, packed)
            table = table - part
        block_ref[:, width:] = packed.astype(block_ref.dtype)

    return pl.pallas_call(
        body,
        out_shape=jax.ShapeDtypeStruct((count, width + LANES), tokens.dtype),
        in_specs=[pl.BlockSpec(memory_space=pltpu.VMEM)] * 3,
        out_specs=pl.BlockSpec(memory_space=pltpu.VMEM),
        compiler_params=pltpu.CompilerParams(vmem_limit_bytes=1 << 20),
        name="pack_block",
    )(in_hbm(tokens), in_hbm(expert_ids), in_hbm(gate_probs))


def stack_blocks(blocks):
    def body(*refs):
        for i, ref in enumerate(refs[:-1]):
            refs[-1][i] = ref[...]

    return pl.pallas_call(
        body,
        out_shape=jax.ShapeDtypeStruct((len(blocks),) + blocks[0].shape, blocks[0].dtype),
        in_specs=[pl.BlockSpec(memory_space=pltpu.VMEM)] * len(blocks),
        out_specs=pl.BlockSpec(memory_space=pltpu.VMEM),
        cost_estimate=pl.CostEstimate(flops=60 * 10**9, bytes_accessed=0, transcendentals=0),
        compiler_params=pltpu.CompilerParams(vmem_limit_bytes=4 << 20),
        name="stack_blocks",
    )(*blocks)


def join_rows(stacks):
    blocks, tokens, width = stacks[0].shape
    total = len(stacks) * blocks
    batch = max(1, 16 // tokens)

    def body(*refs):
        for i in range(0, total, batch):
            group = [refs[j // blocks][j % blocks] for j in range(i, i + batch)]
            rows = jnp.concatenate([value.astype(jnp.float32) for value in group])
            refs[-1][i * tokens : (i + batch) * tokens, :] = rows.astype(refs[-1].dtype)

    return pl.pallas_call(
        body,
        out_shape=jax.ShapeDtypeStruct((total * tokens, width), stacks[0].dtype),
        in_specs=[pl.BlockSpec(memory_space=pltpu.VMEM)] * len(stacks),
        out_specs=pl.BlockSpec(memory_space=pltpu.VMEM),
        compiler_params=pltpu.CompilerParams(
            vmem_limit_bytes=5 * total * tokens * width + (4 << 20)
        ),
        name="join_rows",
    )(*stacks)


def expand_rows(rows, w_gate, w_up, start, columns):
    count, depth = rows.shape[0], w_gate.shape[0]

    def body(rows_ref, gate_ref, up_ref, hidden_ref):
        def step(first, batch):
            x = rows_ref[pl.ds(first, batch), :depth]
            tile = min(TILE, columns)
            for i in range(0, columns, tile):
                cut = slice(start + i, start + i + tile)
                gate = jnp.dot(x, gate_ref[:, cut], preferred_element_type=jnp.float32)
                up = jnp.dot(x, up_ref[:, cut], preferred_element_type=jnp.float32)
                value = gate / (1.0 + jnp.exp(-gate)) * up
                hidden_ref[pl.ds(first, batch), i : i + tile] = value.astype(hidden_ref.dtype)

        row_batches(count, step)

    return pl.pallas_call(
        body,
        out_shape=jax.ShapeDtypeStruct((count, columns), rows.dtype),
        in_specs=[pl.BlockSpec(memory_space=pltpu.VMEM)] * 3,
        out_specs=pl.BlockSpec(memory_space=pltpu.VMEM),
        cost_estimate=pl.CostEstimate(flops=0, bytes_accessed=count * columns, transcendentals=0),
        compiler_params=pltpu.CompilerParams(vmem_limit_bytes=rows.nbytes + (6 << 20)),
        name="expand_rows",
    )(rows, in_vmem(w_gate), in_vmem(w_up))


def contract_hidden(
    parts, w_down, units, before=None, rows=None, half=None, index=None, kind=jnp.float32
):
    total_count, width = parts[0][0].shape[0], w_down.shape[1]
    count = total_count if index is None else total_count // 2
    offset = 0 if index is None else index * count
    experts = lax.axis_size(EXPERT)
    operands = [part for part, _, _ in parts] + [in_vmem(w_down)]
    operands += [value for value in (before, rows) if value is not None]

    def body(*refs):
        part_refs, down_ref = refs[: len(parts)], refs[len(parts)]
        rest = list(refs[len(parts) + 1 : -1])
        before_ref = rest.pop(0) if before is not None else None
        rows_ref = rest.pop(0) if rows is not None else None
        me, group = lax.axis_index(EXPERT), lax.axis_index("dp")

        def step(first, batch):
            here = pl.ds(offset + first, batch)
            if half is None:
                lefts = [ref[here, :] for ref in part_refs]
            else:
                order = [i ^ 1 for i in range(offset // half, (offset + count) // half)]
                lefts = [
                    jnp.concatenate([ref[i * half : (i + 1) * half, :] for i in order])
                    for ref in part_refs
                ]
            if rows is not None:
                table = rows_ref[here, rows.shape[1] - LANES :].astype(jnp.float32)
                lane = lax.broadcasted_iota(jnp.int32, table.shape, 1)
                mine = (lax.rem(lane, experts) == me) & (lane < 3 * experts)
                scale = jnp.sum(jnp.where(mine, table, 0.0), axis=1, keepdims=True)
            tile = min(2 * TILE, width)
            for i in range(0, width, tile):
                cut = slice(i, i + tile)
                total = 0.0 if before is None else before_ref[here, cut]
                for left, (_, mask, unit) in zip(lefts, parts):
                    start = pl.multiple_of((group ^ mask) * units + unit, LANES)
                    right = down_ref[pl.ds(start, left.shape[1]), cut]
                    total = total + jnp.dot(left, right, preferred_element_type=jnp.float32)
                if rows is not None:
                    total = total.astype(jnp.bfloat16).astype(jnp.float32) * scale
                refs[-1][pl.ds(first, batch), cut] = total.astype(kind)

        row_batches(count, step)

    return pl.pallas_call(
        body,
        out_shape=jax.ShapeDtypeStruct((count, width), kind),
        in_specs=[pl.BlockSpec(memory_space=pltpu.VMEM)] * len(operands),
        out_specs=pl.BlockSpec(memory_space=pltpu.VMEM),
        cost_estimate=pl.CostEstimate(flops=0, bytes_accessed=count * width, transcendentals=0),
        compiler_params=pltpu.CompilerParams(
            vmem_limit_bytes=8 * total_count * width
            + (6 << 20)
            + (0 if rows is None else rows.nbytes)
        ),
        name="contract_hidden",
    )(*operands)


def sum_stage(inputs, plan, shape, dtype):
    def body(*refs):
        sources, targets = refs[: len(inputs)], refs[len(inputs) :]
        for target, blocks in zip(targets, plan):
            for i, block in enumerate(blocks):
                total = 0.0
                for ref in sources:
                    if len(ref.shape) == 2:
                        value = ref[block * shape[0] : (block + 1) * shape[0], :]
                    else:
                        value = ref[block]
                    total = total + value.astype(jnp.float32)
                target[i] = total.astype(target.dtype)

    return pl.pallas_call(
        body,
        out_shape=[
            jax.ShapeDtypeStruct((len(blocks),) + shape, dtype if i else jnp.float32)
            for i, blocks in enumerate(plan)
        ],
        in_specs=[pl.BlockSpec(memory_space=pltpu.VMEM)] * len(inputs),
        out_specs=[pl.BlockSpec(memory_space=pltpu.VMEM)] * len(plan),
        compiler_params=pltpu.CompilerParams(
            vmem_limit_bytes=sum(value.nbytes for value in inputs) * 2 + (6 << 20)
        ),
        name="sum_stage",
    )(*inputs)


def finish(parts, groups, dtype):
    tokens, columns = parts[0][0].shape[1:]

    def body(*refs):
        group = lax.axis_index("dp")
        for i in range(groups):
            mine = [ref[0] for ref, (_, j) in zip(refs, parts) if i == j]
            total = sum(value.astype(jnp.float32) for value in mine)
            start = pl.multiple_of((group ^ i) * columns, LANES)
            refs[-1][:, pl.ds(start, columns)] = total.astype(dtype)

    return pl.pallas_call(
        body,
        out_shape=jax.ShapeDtypeStruct((tokens, groups * columns), dtype),
        in_specs=[pl.BlockSpec(memory_space=pltpu.VMEM)] * len(parts),
        out_specs=pl.BlockSpec(memory_space=pltpu.VMEM),
        compiler_params=pltpu.CompilerParams(vmem_limit_bytes=4 << 20),
        name="finish",
    )(*[value for value, _ in parts])


def local(tokens, expert_ids, gate_probs, w_gate, w_up, w_down):
    token_count, width = tokens.shape
    groups, experts = lax.axis_size("dp"), lax.axis_size(EXPERT)
    wide, high = groups // 2, experts // 4

    block = pack_block(tokens, expert_ids, gate_probs, experts)
    units = w_up.shape[2]
    weights = lax.optimization_barrier((block, w_gate[0], w_up[0], w_down[0]))
    block, gate_weights, up_weights, down_weights = weights
    near = stack_blocks([block] + [swap(block, 0, 4 * i) for i in range(1, high)])
    if wide > 1:
        near = jnp.concatenate([near] + [swap(near, 2 * i, 0) for i in range(1, wide)])
    over_x, over_y = swap(near, 1, 0), swap(near, 0, 2)
    first = join_rows([near, swap(near, 1, 2)])
    pieces = [first, join_rows([over_x]), join_rows([over_y])]
    size = pieces[1].shape[0]
    rows = []
    for first, x, y in (pieces, [swap(piece, 0, 1) for piece in pieces]):
        rows += [first[:size], y, x, first[size:]]
    rows = jnp.concatenate(rows)

    chunks = CHUNKS if units % (LANES * CHUNKS) == 0 else 1
    step = units // chunks
    half = rows.shape[0] // 4 if groups == 2 and rows.shape[0] <= BATCH else None

    def from_group(value, mask):
        value = swap(value, mask, 0)
        if half is not None:
            return value
        value = value.reshape(2, 2, 2, wide, high * token_count, step)
        value = jnp.stack([value[:, i ^ (mask & 1)] for i in range(2)], axis=1)
        value = jnp.stack([value[:, :, :, i ^ (mask >> 1)] for i in range(wide)], axis=3)
        return value.reshape(-1, step)

    hidden, others = [], []
    for i in range(chunks):
        if hidden:
            rows, hidden[-1] = lax.optimization_barrier((rows, hidden[-1]))
        hidden.append(expand_rows(rows, gate_weights, up_weights, i * step, step))
        others.append(
            [(from_group(hidden[-1], mask), mask, i * step) for mask in range(1, groups)]
        )
    parts = [(value, 0, i * step) for i, value in enumerate(hidden)]
    total = contract_hidden(parts, down_weights, units)
    for i in range(chunks - 1):
        total = contract_hidden(others[i], down_weights, units, total, half=half)
    last = lambda index, kind: contract_hidden(
        others[-1], down_weights, units, total, rows, half, index, kind
    )
    sent, kept = last(1, jnp.bfloat16), last(0, jnp.float32)

    shape = (token_count, w_down.shape[2])
    rest = [(g, h) for g in range(groups) for h in range(0, high, 2)]
    slot = lambda g, y, h: (((g & 1) * 2 + y) * wide + (g >> 1)) * high + h
    plan = [[slot(g, y, h + z) for g, h in rest] for y, z in ((0, 0), (1, 1), (0, 1), (1, 0))]
    mine, *away = sum_stage([kept, swap(sent, 0, 1)], plan, shape, jnp.bfloat16)
    inputs = [mine] + [swap(value, 0, mask) for value, mask in zip(away, (6, 4, 2))]
    order = sorted(range(1, len(rest)), key=lambda i: (rest[i][1], rest[i][0]), reverse=True)
    mine, *away = sum_stage(inputs, [[i] for i in [0] + order], shape, jnp.bfloat16)
    parts = [
        (swap(value, rest[i][0], 4 * rest[i][1]), rest[i][0]) for value, i in zip(away, order)
    ]
    return finish(parts + [(mine, 0)], groups, tokens.dtype)


def solution(mesh):
    groups, experts = mesh.devices.shape
    split = Mesh(mesh.devices.reshape(groups, experts // 2, 2), ("dp", "far", "core"))
    row, expert = P(("dp", "far", "core"), None), P(EXPERT, None, "dp")
    return jax.shard_map(
        local,
        mesh=split,
        in_specs=(row, row, row, expert, expert, expert),
        out_specs=row,
        check_vma=False,
    )
```

```python
import jax
import jax.numpy as jnp
from jax import lax
from jax.experimental import pallas as pl
from jax.experimental.pallas import tpu as pltpu
from jax.sharding import Mesh
from jax.sharding import PartitionSpec as P

TILE = 256
BATCH = 128
LANES = 128
EXPERT = ("far", "core")


def swap(value, group_mask, expert_mask):
    groups, experts = lax.axis_size("dp"), lax.axis_size(EXPERT)
    pairs = [
        (g * experts + e, (g ^ group_mask) * experts + (e ^ expert_mask))
        for g in range(groups)
        for e in range(experts)
    ]
    return lax.ppermute(value, ("dp",) + EXPERT, pairs)


def in_vmem(value):
    return pltpu.with_memory_space_constraint(value, pltpu.VMEM)


def in_hbm(value):
    return pltpu.with_memory_space_constraint(value, pltpu.HBM)


def row_batches(count, step):
    batch = min(BATCH, count)
    if count == batch:
        step(0, batch)
    else:

        @pl.loop(0, count // batch)
        def _(i):
            step(pl.multiple_of(i * batch, batch), batch)


def pack_block(tokens, expert_ids, gate_probs, experts):
    count, width = tokens.shape
    top = expert_ids.shape[1]

    def body(tokens_ref, ids_ref, probs_ref, block_ref):
        block_ref[:, :width] = tokens_ref[...]
        lane = lax.broadcasted_iota(jnp.int32, (count, LANES), 1)
        table = jnp.zeros((count, LANES), jnp.float32)
        for k in range(top):
            hit = ids_ref[:, k : k + 1] == lax.rem(lane, experts)
            table = jnp.where(hit, probs_ref[:, k : k + 1], table)
        packed = jnp.zeros((count, LANES), jnp.float32)
        for i in range(3):
            part = table.astype(jnp.bfloat16).astype(jnp.float32)
            packed = jnp.where(lane // experts == i, part, packed)
            table = table - part
        block_ref[:, width:] = packed.astype(block_ref.dtype)

    return pl.pallas_call(
        body,
        out_shape=jax.ShapeDtypeStruct((count, width + LANES), tokens.dtype),
        in_specs=[pl.BlockSpec(memory_space=pltpu.VMEM)] * 3,
        out_specs=pl.BlockSpec(memory_space=pltpu.VMEM),
        compiler_params=pltpu.CompilerParams(vmem_limit_bytes=1 << 20),
        name="pack_block",
    )(in_hbm(tokens), in_hbm(expert_ids), in_hbm(gate_probs))


def stack_blocks(blocks):
    def body(*refs):
        for i, ref in enumerate(refs[:-1]):
            refs[-1][i] = ref[...]

    return pl.pallas_call(
        body,
        out_shape=jax.ShapeDtypeStruct((len(blocks),) + blocks[0].shape, blocks[0].dtype),
        in_specs=[pl.BlockSpec(memory_space=pltpu.VMEM)] * len(blocks),
        out_specs=pl.BlockSpec(memory_space=pltpu.VMEM),
        cost_estimate=pl.CostEstimate(flops=60 * 10**9, bytes_accessed=0, transcendentals=0),
        compiler_params=pltpu.CompilerParams(vmem_limit_bytes=4 << 20),
        name="stack_blocks",
    )(*blocks)


def join_rows(stacks):
    blocks, tokens, width = stacks[0].shape
    total = len(stacks) * blocks
    batch = max(1, 16 // tokens)

    def body(*refs):
        for i in range(0, total, batch):
            group = [refs[j // blocks][j % blocks] for j in range(i, i + batch)]
            rows = jnp.concatenate([value.astype(jnp.float32) for value in group])
            refs[-1][i * tokens : (i + batch) * tokens, :] = rows.astype(refs[-1].dtype)

    return pl.pallas_call(
        body,
        out_shape=jax.ShapeDtypeStruct((total * tokens, width), stacks[0].dtype),
        in_specs=[pl.BlockSpec(memory_space=pltpu.VMEM)] * len(stacks),
        out_specs=pl.BlockSpec(memory_space=pltpu.VMEM),
        compiler_params=pltpu.CompilerParams(
            vmem_limit_bytes=5 * total * tokens * width + (4 << 20)
        ),
        name="join_rows",
    )(*stacks)


def expand_rows(rows, w_gate, w_up, start, columns):
    count, depth = rows.shape[0], w_gate.shape[0]

    def body(rows_ref, gate_ref, up_ref, hidden_ref):
        def step(first, batch):
            x = rows_ref[pl.ds(first, batch), :depth]
            dot = lambda right: jnp.dot(x, right, preferred_element_type=jnp.float32)
            for i in range(0, columns, TILE):
                tile = min(TILE, columns - i)
                cut = slice(start + i, start + i + tile)
                if 2 * tile <= TILE:
                    both = dot(jnp.concatenate([gate_ref[:, cut], up_ref[:, cut]], axis=1))
                    gate, up = both[:, :tile], both[:, tile:]
                else:
                    gate, up = dot(gate_ref[:, cut]), dot(up_ref[:, cut])
                value = gate / (1.0 + jnp.exp(-gate)) * up
                hidden_ref[pl.ds(first, batch), i : i + tile] = value.astype(hidden_ref.dtype)

        row_batches(count, step)

    return pl.pallas_call(
        body,
        out_shape=jax.ShapeDtypeStruct((count, columns), rows.dtype),
        in_specs=[pl.BlockSpec(memory_space=pltpu.VMEM)] * 3,
        out_specs=pl.BlockSpec(memory_space=pltpu.VMEM),
        cost_estimate=pl.CostEstimate(flops=0, bytes_accessed=count * columns, transcendentals=0),
        compiler_params=pltpu.CompilerParams(vmem_limit_bytes=rows.nbytes + (6 << 20)),
        name="expand_rows",
    )(rows, in_vmem(w_gate), in_vmem(w_up))


def contract_hidden(
    parts, w_down, units, before=None, rows=None, half=None, index=None, kind=jnp.float32
):
    total_count, width = parts[0][0][0].shape[0], w_down.shape[1]
    count = total_count if index is None else total_count // 2
    offset = 0 if index is None else index * count
    experts = lax.axis_size(EXPERT)
    values = [value for part, _, _ in parts for value in part]
    operands = values + [in_vmem(w_down)]
    operands += [value for value in (before, rows) if value is not None]

    def body(*refs):
        part_refs, down_ref = refs[: len(values)], refs[len(values)]
        rest = list(refs[len(values) + 1 : -1])
        before_ref = rest.pop(0) if before is not None else None
        rows_ref = rest.pop(0) if rows is not None else None
        me, group = lax.axis_index(EXPERT), lax.axis_index("dp")

        def step(first, batch):
            here = pl.ds(offset + first, batch)
            if half is None:
                lefts = [ref[here, :] for ref in part_refs]
            else:
                order = [i ^ 1 for i in range(offset // half, (offset + count) // half)]
                lefts = [
                    jnp.concatenate([ref[i * half : (i + 1) * half, :] for i in order])
                    for ref in part_refs
                ]
            lefts = [
                jnp.concatenate([lefts.pop(0) for _ in part], axis=1) for part, _, _ in parts
            ]
            if rows is not None:
                table = rows_ref[here, rows.shape[1] - LANES :].astype(jnp.float32)
                lane = lax.broadcasted_iota(jnp.int32, table.shape, 1)
                mine = (lax.rem(lane, experts) == me) & (lane < 3 * experts)
                scale = jnp.sum(jnp.where(mine, table, 0.0), axis=1, keepdims=True)
            tile = min(2 * TILE, width)
            for i in range(0, width, tile):
                cut = slice(i, i + tile)
                total = 0.0 if before is None else before_ref[here, cut]
                for left, (_, mask, unit) in zip(lefts, parts):
                    start = pl.multiple_of((group ^ mask) * units + unit, LANES)
                    right = down_ref[pl.ds(start, left.shape[1]), cut]
                    total = total + jnp.dot(left, right, preferred_element_type=jnp.float32)
                if rows is not None:
                    total = total.astype(jnp.bfloat16).astype(jnp.float32) * scale
                refs[-1][pl.ds(first, batch), cut] = total.astype(kind)

        row_batches(count, step)

    return pl.pallas_call(
        body,
        out_shape=jax.ShapeDtypeStruct((count, width), kind),
        in_specs=[pl.BlockSpec(memory_space=pltpu.VMEM)] * len(operands),
        out_specs=pl.BlockSpec(memory_space=pltpu.VMEM),
        cost_estimate=pl.CostEstimate(flops=0, bytes_accessed=count * width, transcendentals=0),
        compiler_params=pltpu.CompilerParams(
            vmem_limit_bytes=8 * total_count * width
            + (6 << 20)
            + (0 if rows is None else rows.nbytes)
        ),
        name="contract_hidden",
    )(*operands)


def sum_stage(inputs, plan, shape, dtype):
    def body(*refs):
        sources, targets = refs[: len(inputs)], refs[len(inputs) :]
        for target, blocks in zip(targets, plan):
            for i, block in enumerate(blocks):
                total = 0.0
                for ref in sources:
                    if len(ref.shape) == 2:
                        value = ref[block * shape[0] : (block + 1) * shape[0], :]
                    else:
                        value = ref[block]
                    total = total + value.astype(jnp.float32)
                target[i] = total.astype(target.dtype)

    return pl.pallas_call(
        body,
        out_shape=[
            jax.ShapeDtypeStruct((len(blocks),) + shape, dtype if i else jnp.float32)
            for i, blocks in enumerate(plan)
        ],
        in_specs=[pl.BlockSpec(memory_space=pltpu.VMEM)] * len(inputs),
        out_specs=[pl.BlockSpec(memory_space=pltpu.VMEM)] * len(plan),
        compiler_params=pltpu.CompilerParams(
            vmem_limit_bytes=sum(value.nbytes for value in inputs) * 2 + (6 << 20)
        ),
        name="sum_stage",
    )(*inputs)


def finish(parts, groups, dtype):
    tokens, columns = parts[0][0].shape[1:]

    def body(*refs):
        group = lax.axis_index("dp")
        for i in range(groups):
            mine = [ref[0] for ref, (_, j) in zip(refs, parts) if i == j]
            total = sum(value.astype(jnp.float32) for value in mine)
            start = pl.multiple_of((group ^ i) * columns, LANES)
            refs[-1][:, pl.ds(start, columns)] = total.astype(dtype)

    return pl.pallas_call(
        body,
        out_shape=jax.ShapeDtypeStruct((tokens, groups * columns), dtype),
        in_specs=[pl.BlockSpec(memory_space=pltpu.VMEM)] * len(parts),
        out_specs=pl.BlockSpec(memory_space=pltpu.VMEM),
        compiler_params=pltpu.CompilerParams(vmem_limit_bytes=4 << 20),
        name="finish",
    )(*[value for value, _ in parts])


def local(tokens, expert_ids, gate_probs, w_gate, w_up, w_down):
    token_count, width = tokens.shape
    groups, experts = lax.axis_size("dp"), lax.axis_size(EXPERT)
    wide, high = groups // 2, experts // 4

    block = pack_block(tokens, expert_ids, gate_probs, experts)
    units = w_up.shape[2]
    weights = lax.optimization_barrier((block, w_gate[0], w_up[0], w_down[0]))
    block, gate_weights, up_weights, down_weights = weights
    near = stack_blocks([block] + [swap(block, 0, 4 * i) for i in range(1, high)])
    if wide > 1:
        near = jnp.concatenate([near] + [swap(near, 2 * i, 0) for i in range(1, wide)])
    over_x, over_y = swap(near, 1, 0), swap(near, 0, 2)
    first = join_rows([near, swap(near, 1, 2)])
    pieces = [first, join_rows([over_x]), join_rows([over_y])]
    size = pieces[1].shape[0]
    rows = []
    for first, x, y in (pieces, [swap(piece, 0, 1) for piece in pieces]):
        rows += [first[:size], y, x, first[size:]]
    rows = jnp.concatenate(rows)

    eighth = units // 8
    steps = (3 * eighth, 3 * eighth, 2 * eighth) if eighth % LANES == 0 else (units,)
    starts = [sum(steps[:i]) for i in range(len(steps))]
    half = rows.shape[0] // 4 if groups == 2 and rows.shape[0] <= BATCH else None

    def from_group(value, mask):
        value = swap(value, mask, 0)
        if half is not None:
            return value
        value = value.reshape(2, 2, 2, wide, high * token_count, value.shape[1])
        value = jnp.stack([value[:, i ^ (mask & 1)] for i in range(2)], axis=1)
        value = jnp.stack([value[:, :, :, i ^ (mask >> 1)] for i in range(wide)], axis=3)
        return value.reshape(-1, value.shape[-1])

    hidden, others = [], []
    for start, step in zip(starts, steps):
        if hidden:
            rows, hidden[-1] = lax.optimization_barrier((rows, hidden[-1]))
        hidden.append(expand_rows(rows, gate_weights, up_weights, start, step))
        others.append(
            [([from_group(hidden[-1], mask)], mask, start) for mask in range(1, groups)]
        )
    total = contract_hidden([(hidden, 0, 0)], down_weights, units)
    for parts in others[:-1]:
        total = contract_hidden(parts, down_weights, units, total, half=half)
    last = lambda index, kind: contract_hidden(
        others[-1], down_weights, units, total, rows, half, index, kind
    )
    sent, kept = last(1, jnp.bfloat16), last(0, jnp.float32)

    shape = (token_count, w_down.shape[2])
    rest = [(g, h) for g in range(groups) for h in range(0, high, 2)]
    slot = lambda g, y, h: (((g & 1) * 2 + y) * wide + (g >> 1)) * high + h
    plan = [[slot(g, y, h + z) for g, h in rest] for y, z in ((0, 0), (1, 1), (0, 1), (1, 0))]
    mine, *away = sum_stage([kept, swap(sent, 0, 1)], plan, shape, jnp.bfloat16)
    inputs = [mine] + [swap(value, 0, mask) for value, mask in zip(away, (6, 4, 2))]
    order = sorted(range(1, len(rest)), key=lambda i: (rest[i][1], rest[i][0]), reverse=True)
    mine, *away = sum_stage(inputs, [[i] for i in [0] + order], shape, jnp.bfloat16)
    parts = [
        (swap(value, rest[i][0], 4 * rest[i][1]), rest[i][0]) for value, i in zip(away, order)
    ]
    return finish(parts + [(mine, 0)], groups, tokens.dtype)


def solution(mesh):
    groups, experts = mesh.devices.shape
    split = Mesh(mesh.devices.reshape(groups, experts // 2, 2), ("dp", "far", "core"))
    row, expert = P(("dp", "far", "core"), None), P(EXPERT, None, "dp")
    return jax.shard_map(
        local,
        mesh=split,
        in_specs=(row, row, row, expert, expert, expert),
        out_specs=row,
        check_vma=False,
    )
```

```python
import jax
import jax.numpy as jnp
from jax import lax
from jax.experimental import pallas as pl
from jax.experimental.pallas import tpu as pltpu
from jax.sharding import Mesh
from jax.sharding import PartitionSpec as P

TILE = 256
BATCH = 128
LANES = 128
EXPERT = ("far", "core")


def swap(value, group_mask, expert_mask):
    groups, experts = lax.axis_size("dp"), lax.axis_size(EXPERT)
    pairs = [
        (g * experts + e, (g ^ group_mask) * experts + (e ^ expert_mask))
        for g in range(groups)
        for e in range(experts)
    ]
    return lax.ppermute(value, ("dp",) + EXPERT, pairs)


def in_vmem(value):
    return pltpu.with_memory_space_constraint(value, pltpu.VMEM)


def in_hbm(value):
    return pltpu.with_memory_space_constraint(value, pltpu.HBM)


def row_batches(count, step):
    batch = min(BATCH, count)
    if count == batch:
        step(0, batch)
    else:

        @pl.loop(0, count // batch)
        def _(i):
            step(pl.multiple_of(i * batch, batch), batch)


def pack_block(tokens, expert_ids, gate_probs, experts):
    count, width = tokens.shape
    top = expert_ids.shape[1]

    def body(tokens_ref, ids_ref, probs_ref, block_ref):
        block_ref[:, :width] = tokens_ref[...]
        lane = lax.broadcasted_iota(jnp.int32, (count, LANES), 1)
        table = jnp.zeros((count, LANES), jnp.float32)
        for k in range(top):
            hit = ids_ref[:, k : k + 1] == lax.rem(lane, experts)
            table = jnp.where(hit, probs_ref[:, k : k + 1], table)
        packed = jnp.zeros((count, LANES), jnp.float32)
        for i in range(3):
            part = table.astype(jnp.bfloat16).astype(jnp.float32)
            packed = jnp.where(lane // experts == i, part, packed)
            table = table - part
        block_ref[:, width:] = packed.astype(block_ref.dtype)

    return pl.pallas_call(
        body,
        out_shape=jax.ShapeDtypeStruct((count, width + LANES), tokens.dtype),
        in_specs=[pl.BlockSpec(memory_space=pltpu.VMEM)] * 3,
        out_specs=pl.BlockSpec(memory_space=pltpu.VMEM),
        compiler_params=pltpu.CompilerParams(vmem_limit_bytes=1 << 20),
        name="pack_block",
    )(in_hbm(tokens), in_hbm(expert_ids), in_hbm(gate_probs))


def stack_blocks(blocks):
    def body(*refs):
        for i, ref in enumerate(refs[:-1]):
            refs[-1][i] = ref[...]

    return pl.pallas_call(
        body,
        out_shape=jax.ShapeDtypeStruct((len(blocks),) + blocks[0].shape, blocks[0].dtype),
        in_specs=[pl.BlockSpec(memory_space=pltpu.VMEM)] * len(blocks),
        out_specs=pl.BlockSpec(memory_space=pltpu.VMEM),
        cost_estimate=pl.CostEstimate(flops=60 * 10**9, bytes_accessed=0, transcendentals=0),
        compiler_params=pltpu.CompilerParams(vmem_limit_bytes=4 << 20),
        name="stack_blocks",
    )(*blocks)


def join_rows(stacks):
    blocks, tokens, width = stacks[0].shape
    total = len(stacks) * blocks
    batch = max(1, 16 // tokens)

    def body(*refs):
        for i in range(0, total, batch):
            group = [refs[j // blocks][j % blocks] for j in range(i, i + batch)]
            rows = jnp.concatenate([value.astype(jnp.float32) for value in group])
            refs[-1][i * tokens : (i + batch) * tokens, :] = rows.astype(refs[-1].dtype)

    return pl.pallas_call(
        body,
        out_shape=jax.ShapeDtypeStruct((total * tokens, width), stacks[0].dtype),
        in_specs=[pl.BlockSpec(memory_space=pltpu.VMEM)] * len(stacks),
        out_specs=pl.BlockSpec(memory_space=pltpu.VMEM),
        compiler_params=pltpu.CompilerParams(
            vmem_limit_bytes=5 * total * tokens * width + (4 << 20)
        ),
        name="join_rows",
    )(*stacks)


def expand_rows(rows, w_gate, w_up, start, columns):
    count, depth = rows.shape[0], w_gate.shape[0]

    def body(rows_ref, gate_ref, up_ref, hidden_ref):
        def step(first, batch):
            x = rows_ref[pl.ds(first, batch), :depth]
            dot = lambda right: jnp.dot(x, right, preferred_element_type=jnp.float32)
            for i in range(0, columns, TILE):
                tile = min(TILE, columns - i)
                cut = slice(start + i, start + i + tile)
                if 2 * tile <= TILE:
                    both = dot(jnp.concatenate([gate_ref[:, cut], up_ref[:, cut]], axis=1))
                    gate, up = both[:, :tile], both[:, tile:]
                else:
                    gate, up = dot(gate_ref[:, cut]), dot(up_ref[:, cut])
                value = gate / (1.0 + jnp.exp(-gate)) * up
                hidden_ref[pl.ds(first, batch), i : i + tile] = value.astype(hidden_ref.dtype)

        row_batches(count, step)

    return pl.pallas_call(
        body,
        out_shape=jax.ShapeDtypeStruct((count, columns), rows.dtype),
        in_specs=[pl.BlockSpec(memory_space=pltpu.VMEM)] * 3,
        out_specs=pl.BlockSpec(memory_space=pltpu.VMEM),
        cost_estimate=pl.CostEstimate(flops=0, bytes_accessed=count * columns, transcendentals=0),
        compiler_params=pltpu.CompilerParams(vmem_limit_bytes=rows.nbytes + (6 << 20)),
        name="expand_rows",
    )(rows, in_vmem(w_gate), in_vmem(w_up))


def contract_hidden(
    parts, w_down, units, before=None, rows=None, half=None, index=None, kind=jnp.float32
):
    total_count, width = parts[0][0][0].shape[0], w_down.shape[1]
    count = total_count if index is None else total_count // 2
    offset = 0 if index is None else index * count
    experts = lax.axis_size(EXPERT)
    values = [value for part, _, _ in parts for value in part]
    operands = values + [in_vmem(w_down)]
    operands += [value for value in (before, rows) if value is not None]

    def body(*refs):
        part_refs, down_ref = refs[: len(values)], refs[len(values)]
        rest = list(refs[len(values) + 1 : -1])
        before_ref = rest.pop(0) if before is not None else None
        rows_ref = rest.pop(0) if rows is not None else None
        me, group = lax.axis_index(EXPERT), lax.axis_index("dp")

        def step(first, batch):
            here = pl.ds(offset + first, batch)
            if half is None:
                lefts = [ref[here, :] for ref in part_refs]
            else:
                order = [i ^ 1 for i in range(offset // half, (offset + count) // half)]
                lefts = [
                    jnp.concatenate([ref[i * half : (i + 1) * half, :] for i in order])
                    for ref in part_refs
                ]
            lefts = [
                jnp.concatenate([lefts.pop(0) for _ in part], axis=1) for part, _, _ in parts
            ]
            if rows is not None:
                table = rows_ref[here, rows.shape[1] - LANES :].astype(jnp.float32)
                lane = lax.broadcasted_iota(jnp.int32, table.shape, 1)
                mine = (lax.rem(lane, experts) == me) & (lane < 3 * experts)
                scale = jnp.sum(jnp.where(mine, table, 0.0), axis=1, keepdims=True)
            tile = min(2 * TILE, width)
            for i in range(0, width, tile):
                cut = slice(i, i + tile)
                total = 0.0 if before is None else before_ref[here, cut]
                for left, (_, mask, unit) in zip(lefts, parts):
                    start = pl.multiple_of((group ^ mask) * units + unit, LANES)
                    right = down_ref[pl.ds(start, left.shape[1]), cut]
                    total = total + jnp.dot(left, right, preferred_element_type=jnp.float32)
                if rows is not None:
                    total = total.astype(jnp.bfloat16).astype(jnp.float32) * scale
                refs[-1][pl.ds(first, batch), cut] = total.astype(kind)

        row_batches(count, step)

    return pl.pallas_call(
        body,
        out_shape=jax.ShapeDtypeStruct((count, width), kind),
        in_specs=[pl.BlockSpec(memory_space=pltpu.VMEM)] * len(operands),
        out_specs=pl.BlockSpec(memory_space=pltpu.VMEM),
        cost_estimate=pl.CostEstimate(flops=0, bytes_accessed=count * width, transcendentals=0),
        compiler_params=pltpu.CompilerParams(
            vmem_limit_bytes=8 * total_count * width
            + (6 << 20)
            + (0 if rows is None else rows.nbytes)
        ),
        name="contract_hidden",
    )(*operands)


def sum_stage(inputs, plan, shape, dtype, wide=1):
    def body(*refs):
        sources, targets = refs[: len(inputs)], refs[len(inputs) :]
        for target, blocks in zip(targets, plan):
            for i, block in enumerate(blocks):
                total = 0.0
                for ref in sources:
                    if len(ref.shape) == 2:
                        value = ref[block * shape[0] : (block + 1) * shape[0], :]
                    else:
                        value = ref[block]
                    total = total + value.astype(jnp.float32)
                target[i] = total.astype(target.dtype)

    return pl.pallas_call(
        body,
        out_shape=[
            jax.ShapeDtypeStruct((len(blocks),) + shape, jnp.float32 if i < wide else dtype)
            for i, blocks in enumerate(plan)
        ],
        in_specs=[pl.BlockSpec(memory_space=pltpu.VMEM)] * len(inputs),
        out_specs=[pl.BlockSpec(memory_space=pltpu.VMEM)] * len(plan),
        compiler_params=pltpu.CompilerParams(
            vmem_limit_bytes=sum(value.nbytes for value in inputs) * 2 + (6 << 20)
        ),
        name="sum_stage",
    )(*inputs)


def finish(parts, groups, dtype):
    tokens, columns = parts[0][0].shape[1:]

    def body(*refs):
        group = lax.axis_index("dp")
        for i in range(groups):
            mine = [ref[0] for ref, (_, j) in zip(refs, parts) if i == j]
            total = sum(value.astype(jnp.float32) for value in mine)
            start = pl.multiple_of((group ^ i) * columns, LANES)
            refs[-1][:, pl.ds(start, columns)] = total.astype(dtype)

    return pl.pallas_call(
        body,
        out_shape=jax.ShapeDtypeStruct((tokens, groups * columns), dtype),
        in_specs=[pl.BlockSpec(memory_space=pltpu.VMEM)] * len(parts),
        out_specs=pl.BlockSpec(memory_space=pltpu.VMEM),
        compiler_params=pltpu.CompilerParams(vmem_limit_bytes=4 << 20),
        name="finish",
    )(*[value for value, _ in parts])


def local(tokens, expert_ids, gate_probs, w_gate, w_up, w_down):
    token_count, width = tokens.shape
    groups, experts = lax.axis_size("dp"), lax.axis_size(EXPERT)
    wide, high = groups // 2, experts // 4

    block = pack_block(tokens, expert_ids, gate_probs, experts)
    units = w_up.shape[2]
    weights = lax.optimization_barrier((block, w_gate[0], w_up[0], w_down[0]))
    block, gate_weights, up_weights, down_weights = weights
    near = stack_blocks([block] + [swap(block, 0, 4 * i) for i in range(1, high)])
    if wide > 1:
        near = jnp.concatenate([near] + [swap(near, 2 * i, 0) for i in range(1, wide)])
    over_x, over_y = swap(near, 1, 0), swap(near, 0, 2)
    first = join_rows([near, swap(near, 1, 2)])
    pieces = [first, join_rows([over_x]), join_rows([over_y])]
    size = pieces[1].shape[0]
    rows = []
    for first, x, y in (pieces, [swap(piece, 0, 1) for piece in pieces]):
        rows += [first[:size], y, x, first[size:]]
    rows = jnp.concatenate(rows)

    eighth = units // 8
    steps = (3 * eighth, 3 * eighth, 2 * eighth) if eighth % LANES == 0 else (units,)
    starts = [sum(steps[:i]) for i in range(len(steps))]
    half = rows.shape[0] // 4 if groups == 2 and rows.shape[0] <= BATCH else None

    def from_group(value, mask):
        value = swap(value, mask, 0)
        if half is not None:
            return value
        value = value.reshape(2, 2, 2, wide, high * token_count, value.shape[1])
        value = jnp.stack([value[:, i ^ (mask & 1)] for i in range(2)], axis=1)
        value = jnp.stack([value[:, :, :, i ^ (mask >> 1)] for i in range(wide)], axis=3)
        return value.reshape(-1, value.shape[-1])

    hidden, others = [], []
    for start, step in zip(starts, steps):
        if hidden:
            rows, hidden[-1] = lax.optimization_barrier((rows, hidden[-1]))
        hidden.append(expand_rows(rows, gate_weights, up_weights, start, step))
        others.append(
            [([from_group(hidden[-1], mask)], mask, start) for mask in range(1, groups)]
        )
    total = contract_hidden([(hidden, 0, 0)], down_weights, units)
    for parts in others[:-1]:
        total = contract_hidden(parts, down_weights, units, total, half=half)
    last = lambda index, kind: contract_hidden(
        others[-1], down_weights, units, total, rows, half, index, kind
    )
    sent, kept = last(1, jnp.bfloat16), last(0, jnp.float32)

    shape = (token_count, w_down.shape[2])
    rest = [(g, h) for g in range(groups) for h in range(0, high, 2)]
    slot = lambda g, y, h: (((g & 1) * 2 + y) * wide + (g >> 1)) * high + h
    rest.sort(key=lambda masks: (masks[1], masks[0]), reverse=True)
    sets = ([masks for masks in rest if masks[1]], [masks for masks in rest if not masks[1]])
    near = [[slot(g, 0, h) for g, h in blocks] for blocks in sets]
    away = [
        [slot(g, y, h + z) for g, h in blocks]
        for blocks in sets
        for y, z in ((1, 1), (0, 1), (1, 0))
    ]
    inputs = [kept, swap(sent, 0, 1)]
    sums = sum_stage(inputs, near + away, shape, jnp.bfloat16, 2)
    got = [swap(value, 0, mask) for value, mask in zip(sums[2:], (6, 4, 2) * 2)]
    parts = []
    for i, blocks in enumerate(sets):
        inputs = [sums[i]] + got[3 * i : 3 * i + 3]
        order = range(len(blocks) - 1, -1, -1) if i else range(len(blocks))
        values = sum_stage(inputs, [[j] for j in order], shape, jnp.bfloat16, i)
        for value, (g, h) in zip(values, [blocks[j] for j in order]):
            parts.append((swap(value, g, 4 * h) if g or h else value, g))
    return finish(parts, groups, tokens.dtype)


def solution(mesh):
    groups, experts = mesh.devices.shape
    split = Mesh(mesh.devices.reshape(groups, experts // 2, 2), ("dp", "far", "core"))
    row, expert = P(("dp", "far", "core"), None), P(EXPERT, None, "dp")
    return jax.shard_map(
        local,
        mesh=split,
        in_specs=(row, row, row, expert, expert, expert),
        out_specs=row,
        check_vma=False,
    )
```

```python
import jax
import jax.numpy as jnp
from jax import lax
from jax.experimental import pallas as pl
from jax.experimental.pallas import tpu as pltpu
from jax.sharding import Mesh
from jax.sharding import PartitionSpec as P

TILE = 256
BATCH = 128
LANES = 128
EXPERT = ("far", "core")


def swap(value, group_mask, expert_mask):
    groups, experts = lax.axis_size("dp"), lax.axis_size(EXPERT)
    pairs = [
        (g * experts + e, (g ^ group_mask) * experts + (e ^ expert_mask))
        for g in range(groups)
        for e in range(experts)
    ]
    return lax.ppermute(value, ("dp",) + EXPERT, pairs)


def in_vmem(value):
    return pltpu.with_memory_space_constraint(value, pltpu.VMEM)


def in_hbm(value):
    return pltpu.with_memory_space_constraint(value, pltpu.HBM)


def row_batches(count, step):
    batch = min(BATCH, count)
    if count == batch:
        step(0, batch)
    else:

        @pl.loop(0, count // batch)
        def _(i):
            step(pl.multiple_of(i * batch, batch), batch)


def pack_block(tokens, expert_ids, gate_probs, experts):
    count, width = tokens.shape
    top = expert_ids.shape[1]

    def body(tokens_ref, ids_ref, probs_ref, block_ref):
        block_ref[:, :width] = tokens_ref[...]
        lane = lax.broadcasted_iota(jnp.int32, (count, LANES), 1)
        table = jnp.zeros((count, LANES), jnp.float32)
        for k in range(top):
            hit = ids_ref[:, k : k + 1] == lax.rem(lane, experts)
            table = jnp.where(hit, probs_ref[:, k : k + 1], table)
        packed = jnp.zeros((count, LANES), jnp.float32)
        for i in range(3):
            part = table.astype(jnp.bfloat16).astype(jnp.float32)
            packed = jnp.where(lane // experts == i, part, packed)
            table = table - part
        block_ref[:, width:] = packed.astype(block_ref.dtype)

    return pl.pallas_call(
        body,
        out_shape=jax.ShapeDtypeStruct((count, width + LANES), tokens.dtype),
        in_specs=[pl.BlockSpec(memory_space=pltpu.VMEM)] * 3,
        out_specs=pl.BlockSpec(memory_space=pltpu.VMEM),
        compiler_params=pltpu.CompilerParams(vmem_limit_bytes=1 << 20),
        name="pack_block",
    )(in_hbm(tokens), in_hbm(expert_ids), in_hbm(gate_probs))


def stack_blocks(blocks):
    def body(*refs):
        for i, ref in enumerate(refs[:-1]):
            refs[-1][i] = ref[...]

    return pl.pallas_call(
        body,
        out_shape=jax.ShapeDtypeStruct((len(blocks),) + blocks[0].shape, blocks[0].dtype),
        in_specs=[pl.BlockSpec(memory_space=pltpu.VMEM)] * len(blocks),
        out_specs=pl.BlockSpec(memory_space=pltpu.VMEM),
        cost_estimate=pl.CostEstimate(flops=60 * 10**9, bytes_accessed=0, transcendentals=0),
        compiler_params=pltpu.CompilerParams(vmem_limit_bytes=4 << 20),
        name="stack_blocks",
    )(*blocks)


def join_rows(stacks):
    blocks, tokens, width = stacks[0].shape
    total = len(stacks) * blocks
    batch = min(total, max(1, 16 // tokens))

    def body(*refs):
        for i in range(0, total, batch):
            group = [refs[j // blocks][j % blocks] for j in range(i, i + batch)]
            rows = jnp.concatenate([value.astype(jnp.float32) for value in group])
            refs[-1][i * tokens : (i + batch) * tokens, :] = rows.astype(refs[-1].dtype)

    return pl.pallas_call(
        body,
        out_shape=jax.ShapeDtypeStruct((total * tokens, width), stacks[0].dtype),
        in_specs=[pl.BlockSpec(memory_space=pltpu.VMEM)] * len(stacks),
        out_specs=pl.BlockSpec(memory_space=pltpu.VMEM),
        compiler_params=pltpu.CompilerParams(
            vmem_limit_bytes=5 * total * tokens * width + (4 << 20)
        ),
        name="join_rows",
    )(*stacks)


def expand_rows(rows, w_gate, w_up, start, columns):
    count, depth = rows.shape[0], w_gate.shape[0]

    def body(rows_ref, gate_ref, up_ref, hidden_ref):
        def step(first, batch):
            x = rows_ref[pl.ds(first, batch), :depth]
            dot = lambda right: jnp.dot(x, right, preferred_element_type=jnp.float32)
            for i in range(0, columns, TILE):
                tile = min(TILE, columns - i)
                cut = slice(start + i, start + i + tile)
                if 2 * tile <= TILE:
                    both = dot(jnp.concatenate([gate_ref[:, cut], up_ref[:, cut]], axis=1))
                    gate, up = both[:, :tile], both[:, tile:]
                else:
                    gate, up = dot(gate_ref[:, cut]), dot(up_ref[:, cut])
                value = gate / (1.0 + jnp.exp(-gate)) * up
                hidden_ref[pl.ds(first, batch), i : i + tile] = value.astype(hidden_ref.dtype)

        row_batches(count, step)

    return pl.pallas_call(
        body,
        out_shape=jax.ShapeDtypeStruct((count, columns), rows.dtype),
        in_specs=[pl.BlockSpec(memory_space=pltpu.VMEM)] * 3,
        out_specs=pl.BlockSpec(memory_space=pltpu.VMEM),
        cost_estimate=pl.CostEstimate(flops=0, bytes_accessed=count * columns, transcendentals=0),
        compiler_params=pltpu.CompilerParams(vmem_limit_bytes=rows.nbytes + (6 << 20)),
        name="expand_rows",
    )(rows, in_vmem(w_gate), in_vmem(w_up))


def contract_hidden(
    parts, w_down, units, before=None, rows=None, half=None, index=None, kind=jnp.float32
):
    total_count, width = parts[0][0][0].shape[0], w_down.shape[1]
    count = total_count if index is None else total_count // 2
    offset = 0 if index is None else index * count
    experts = lax.axis_size(EXPERT)
    values = [value for part, _, _ in parts for value in part]
    operands = values + [in_vmem(w_down)]
    operands += [value for value in (before, rows) if value is not None]

    def body(*refs):
        part_refs, down_ref = refs[: len(values)], refs[len(values)]
        rest = list(refs[len(values) + 1 : -1])
        before_ref = rest.pop(0) if before is not None else None
        rows_ref = rest.pop(0) if rows is not None else None
        me, group = lax.axis_index(EXPERT), lax.axis_index("dp")

        def step(first, batch):
            here = pl.ds(offset + first, batch)
            if half is None:
                lefts = [ref[here, :] for ref in part_refs]
            else:
                order = [i ^ 1 for i in range(offset // half, (offset + count) // half)]
                lefts = [
                    jnp.concatenate([ref[i * half : (i + 1) * half, :] for i in order])
                    for ref in part_refs
                ]
            lefts = [
                jnp.concatenate([lefts.pop(0) for _ in part], axis=1) for part, _, _ in parts
            ]
            if rows is not None:
                table = rows_ref[here, rows.shape[1] - LANES :].astype(jnp.float32)
                lane = lax.broadcasted_iota(jnp.int32, table.shape, 1)
                mine = (lax.rem(lane, experts) == me) & (lane < 3 * experts)
                scale = jnp.sum(jnp.where(mine, table, 0.0), axis=1, keepdims=True)
            tile = min(2 * TILE, width)
            for i in range(0, width, tile):
                cut = slice(i, i + tile)
                total = 0.0 if before is None else before_ref[here, cut]
                for left, (_, mask, unit) in zip(lefts, parts):
                    start = pl.multiple_of((group ^ mask) * units + unit, LANES)
                    right = down_ref[pl.ds(start, left.shape[1]), cut]
                    total = total + jnp.dot(left, right, preferred_element_type=jnp.float32)
                if rows is not None:
                    total = total.astype(jnp.bfloat16).astype(jnp.float32) * scale
                refs[-1][pl.ds(first, batch), cut] = total.astype(kind)

        row_batches(count, step)

    return pl.pallas_call(
        body,
        out_shape=jax.ShapeDtypeStruct((count, width), kind),
        in_specs=[pl.BlockSpec(memory_space=pltpu.VMEM)] * len(operands),
        out_specs=pl.BlockSpec(memory_space=pltpu.VMEM),
        cost_estimate=pl.CostEstimate(flops=0, bytes_accessed=count * width, transcendentals=0),
        compiler_params=pltpu.CompilerParams(
            vmem_limit_bytes=8 * total_count * width
            + (6 << 20)
            + (0 if rows is None else rows.nbytes)
        ),
        name="contract_hidden",
    )(*operands)


def sum_stage(inputs, plan, shape, dtype):
    def body(*refs):
        sources, targets = refs[: len(inputs)], refs[len(inputs) :]
        for target, blocks in zip(targets, plan):
            for i, block in enumerate(blocks):
                total = 0.0
                for ref in sources:
                    if len(ref.shape) == 2:
                        value = ref[block * shape[0] : (block + 1) * shape[0], :]
                    else:
                        value = ref[block]
                    total = total + value.astype(jnp.float32)
                target[i] = total.astype(target.dtype)

    return pl.pallas_call(
        body,
        out_shape=[
            jax.ShapeDtypeStruct((len(blocks),) + shape, dtype if i else jnp.float32)
            for i, blocks in enumerate(plan)
        ],
        in_specs=[pl.BlockSpec(memory_space=pltpu.VMEM)] * len(inputs),
        out_specs=[pl.BlockSpec(memory_space=pltpu.VMEM)] * len(plan),
        compiler_params=pltpu.CompilerParams(
            vmem_limit_bytes=sum(value.nbytes for value in inputs) * 2 + (6 << 20)
        ),
        name="sum_stage",
    )(*inputs)


def finish(parts, groups, dtype):
    tokens, columns = parts[0][0].shape[1:]

    def body(*refs):
        group = lax.axis_index("dp")
        for i in range(groups):
            mine = [ref[0] for ref, (_, j) in zip(refs, parts) if i == j]
            total = sum(value.astype(jnp.float32) for value in mine)
            start = pl.multiple_of((group ^ i) * columns, LANES)
            refs[-1][:, pl.ds(start, columns)] = total.astype(dtype)

    return pl.pallas_call(
        body,
        out_shape=jax.ShapeDtypeStruct((tokens, groups * columns), dtype),
        in_specs=[pl.BlockSpec(memory_space=pltpu.VMEM)] * len(parts),
        out_specs=pl.BlockSpec(memory_space=pltpu.VMEM),
        compiler_params=pltpu.CompilerParams(vmem_limit_bytes=4 << 20),
        name="finish",
    )(*[value for value, _ in parts])


def local(tokens, expert_ids, gate_probs, w_gate, w_up, w_down):
    token_count, width = tokens.shape
    groups, experts = lax.axis_size("dp"), lax.axis_size(EXPERT)
    wide, high = groups // 2, experts // 4

    block = pack_block(tokens, expert_ids, gate_probs, experts)
    units = w_up.shape[2]
    weights = lax.optimization_barrier((block, w_gate[0], w_up[0], w_down[0]))
    block, gate_weights, up_weights, down_weights = weights
    order = [0] + list(range(high - 1, 0, -1))
    blocks = [swap(block, 0, 4 * i) if i else block for i in order]
    units = w_up.shape[2]
    weights = lax.optimization_barrier((block, w_gate[0], w_up[0], w_down[0]))
    block, gate_weights, up_weights, down_weights = weights
    near = stack_blocks([block] + [swap(block, 0, 4 * i) for i in range(1, high)])
    sets = []
    for part in (blocks[: high // 2], blocks[high // 2 :]):
        near = stack_blocks(part)
        if wide > 1:
            near = jnp.concatenate([near] + [swap(near, 2 * i, 0) for i in range(1, wide)])
        sets.append((near, swap(near, 0, 2), swap(near, 1, 0), swap(near, 1, 2)))
    near, over_y, over_x, corner = sets[1]
    pieces = [join_rows(sets[0]), join_rows([near, corner]), join_rows([over_y, over_x])]
    size = pieces[0].shape[0] // 4
    rows = []
    for first, outer, inner in (pieces, [swap(piece, 0, 1) for piece in pieces]):
        rows += [first, outer[:size], inner, outer[size:]]
    rows = jnp.concatenate(rows)

    eighth = units // 8
    steps = (3 * eighth, 3 * eighth, 2 * eighth) if eighth % LANES == 0 else (units,)
    starts = [sum(steps[:i]) for i in range(len(steps))]
    half = rows.shape[0] // 8 if groups == 2 and rows.shape[0] <= BATCH else None

    def from_group(value, mask):
        value = swap(value, mask, 0)
        if half is not None:
            return value
        value = value.reshape(4, 2, 2, wide, -1, value.shape[1])
        value = jnp.stack([value[:, i ^ (mask & 1)] for i in range(2)], axis=1)
        value = jnp.stack([value[:, :, :, i ^ (mask >> 1)] for i in range(wide)], axis=3)
        return value.reshape(-1, value.shape[-1])

    hidden, others = [], []
    for start, step in zip(starts, steps):
        if hidden:
            rows, hidden[-1] = lax.optimization_barrier((rows, hidden[-1]))
        hidden.append(expand_rows(rows, gate_weights, up_weights, start, step))
        others.append(
            [([from_group(hidden[-1], mask)], mask, start) for mask in range(1, groups)]
        )
    total = contract_hidden([(hidden, 0, 0)], down_weights, units)
    for parts in others[:-1]:
        total = contract_hidden(parts, down_weights, units, total, half=half)
    last = lambda index, kind: contract_hidden(
        others[-1], down_weights, units, total, rows, half, index, kind
    )
    sent, kept = last(1, jnp.bfloat16), last(0, jnp.float32)

    shape = (token_count, w_down.shape[2])
    rest = [(g, h) for g in range(groups) for h in range(0, high, 2)]

    def slot(g, y, h):
        which, place = divmod(order.index(h), high // 2)
        return (((which * 2 + (g & 1)) * 2 + y) * wide + (g >> 1)) * (high // 2) + place

    plan = [[slot(g, y, h + z) for g, h in rest] for y, z in ((0, 0), (1, 1), (0, 1), (1, 0))]
    mine, *away = sum_stage([kept, swap(sent, 0, 1)], plan, shape, jnp.bfloat16)
    inputs = [mine] + [swap(value, 0, mask) for value, mask in zip(away, (6, 4, 2))]
    last = sorted(range(1, len(rest)), key=lambda i: (rest[i][1], rest[i][0]), reverse=True)
    mine, *away = sum_stage(inputs, [[i] for i in [0] + last], shape, jnp.bfloat16)
    parts = [(swap(value, rest[i][0], 4 * rest[i][1]), rest[i][0]) for value, i in zip(away, last)]
    return finish(parts + [(mine, 0)], groups, tokens.dtype)


def solution(mesh):
    groups, experts = mesh.devices.shape
    split = Mesh(mesh.devices.reshape(groups, experts // 2, 2), ("dp", "far", "core"))
    row, expert = P(("dp", "far", "core"), None), P(EXPERT, None, "dp")
    return jax.shard_map(
        local,
        mesh=split,
        in_specs=(row, row, row, expert, expert, expert),
        out_specs=row,
        check_vma=False,
    )
```

```python
import jax
import jax.numpy as jnp
from jax import lax
from jax.experimental import pallas as pl
from jax.experimental.pallas import tpu as pltpu
from jax.sharding import Mesh
from jax.sharding import PartitionSpec as P

TILE = 256
BATCH = 128
LANES = 128
EXPERT = ("far", "core")


def swap(value, group_mask, expert_mask):
    groups, experts = lax.axis_size("dp"), lax.axis_size(EXPERT)
    pairs = [
        (g * experts + e, (g ^ group_mask) * experts + (e ^ expert_mask))
        for g in range(groups)
        for e in range(experts)
    ]
    return lax.ppermute(value, ("dp",) + EXPERT, pairs)


def in_vmem(value):
    return pltpu.with_memory_space_constraint(value, pltpu.VMEM)


def in_hbm(value):
    return pltpu.with_memory_space_constraint(value, pltpu.HBM)


def row_batches(count, step):
    batch = min(BATCH, count)
    if count == batch:
        step(0, batch)
    else:

        @pl.loop(0, count // batch)
        def _(i):
            step(pl.multiple_of(i * batch, batch), batch)


def pack_block(tokens, expert_ids, gate_probs, experts):
    count, width = tokens.shape
    top = expert_ids.shape[1]

    def body(tokens_ref, ids_ref, probs_ref, block_ref):
        block_ref[:, :width] = tokens_ref[...]
        lane = lax.broadcasted_iota(jnp.int32, (count, LANES), 1)
        table = jnp.zeros((count, LANES), jnp.float32)
        for k in range(top):
            hit = ids_ref[:, k : k + 1] == lax.rem(lane, experts)
            table = jnp.where(hit, probs_ref[:, k : k + 1], table)
        packed = jnp.zeros((count, LANES), jnp.float32)
        for i in range(3):
            part = table.astype(jnp.bfloat16).astype(jnp.float32)
            packed = jnp.where(lane // experts == i, part, packed)
            table = table - part
        block_ref[:, width:] = packed.astype(block_ref.dtype)

    return pl.pallas_call(
        body,
        out_shape=jax.ShapeDtypeStruct((count, width + LANES), tokens.dtype),
        in_specs=[pl.BlockSpec(memory_space=pltpu.VMEM)] * 3,
        out_specs=pl.BlockSpec(memory_space=pltpu.VMEM),
        compiler_params=pltpu.CompilerParams(vmem_limit_bytes=1 << 20),
        name="pack_block",
    )(in_hbm(tokens), in_hbm(expert_ids), in_hbm(gate_probs))


def stack_blocks(blocks):
    def body(*refs):
        for i, ref in enumerate(refs[:-1]):
            refs[-1][i] = ref[...]

    return pl.pallas_call(
        body,
        out_shape=jax.ShapeDtypeStruct((len(blocks),) + blocks[0].shape, blocks[0].dtype),
        in_specs=[pl.BlockSpec(memory_space=pltpu.VMEM)] * len(blocks),
        out_specs=pl.BlockSpec(memory_space=pltpu.VMEM),
        cost_estimate=pl.CostEstimate(flops=60 * 10**9, bytes_accessed=0, transcendentals=0),
        compiler_params=pltpu.CompilerParams(vmem_limit_bytes=4 << 20),
        name="stack_blocks",
    )(*blocks)


def join_rows(stacks):
    blocks, tokens, width = stacks[0].shape
    total = len(stacks) * blocks
    batch = min(total, max(1, 16 // tokens))

    def body(*refs):
        for i in range(0, total, batch):
            group = [refs[j // blocks][j % blocks] for j in range(i, i + batch)]
            rows = jnp.concatenate([value.astype(jnp.float32) for value in group])
            refs[-1][i * tokens : (i + batch) * tokens, :] = rows.astype(refs[-1].dtype)

    return pl.pallas_call(
        body,
        out_shape=jax.ShapeDtypeStruct((total * tokens, width), stacks[0].dtype),
        in_specs=[pl.BlockSpec(memory_space=pltpu.VMEM)] * len(stacks),
        out_specs=pl.BlockSpec(memory_space=pltpu.VMEM),
        compiler_params=pltpu.CompilerParams(
            vmem_limit_bytes=5 * total * tokens * width + (4 << 20)
        ),
        name="join_rows",
    )(*stacks)


def expand_rows(rows, w_gate, w_up, start, columns):
    count, depth = rows.shape[0], w_gate.shape[0]

    def body(rows_ref, gate_ref, up_ref, hidden_ref):
        def step(first, batch):
            x = rows_ref[pl.ds(first, batch), :depth]
            dot = lambda right: jnp.dot(x, right, preferred_element_type=jnp.float32)
            for i in range(0, columns, TILE):
                tile = min(TILE, columns - i)
                cut = slice(start + i, start + i + tile)
                if 2 * tile <= TILE:
                    both = dot(jnp.concatenate([gate_ref[:, cut], up_ref[:, cut]], axis=1))
                    gate, up = both[:, :tile], both[:, tile:]
                else:
                    gate, up = dot(gate_ref[:, cut]), dot(up_ref[:, cut])
                value = gate / (1.0 + jnp.exp(-gate)) * up
                hidden_ref[pl.ds(first, batch), i : i + tile] = value.astype(hidden_ref.dtype)

        row_batches(count, step)

    return pl.pallas_call(
        body,
        out_shape=jax.ShapeDtypeStruct((count, columns), rows.dtype),
        in_specs=[pl.BlockSpec(memory_space=pltpu.VMEM)] * 3,
        out_specs=pl.BlockSpec(memory_space=pltpu.VMEM),
        cost_estimate=pl.CostEstimate(flops=0, bytes_accessed=count * columns, transcendentals=0),
        compiler_params=pltpu.CompilerParams(vmem_limit_bytes=rows.nbytes + (6 << 20)),
        name="expand_rows",
    )(rows, in_vmem(w_gate), in_vmem(w_up))


def contract_hidden(
    parts, w_down, units, before=None, rows=None, half=None, index=None, kind=jnp.float32
):
    total_count, width = parts[0][0][0].shape[0], w_down.shape[1]
    count = total_count if index is None else total_count // 2
    offset = 0 if index is None else index * count
    experts = lax.axis_size(EXPERT)
    values = [value for part, _, _ in parts for value in part]
    operands = values + [in_vmem(w_down)]
    operands += [value for value in (before, rows) if value is not None]

    def body(*refs):
        part_refs, down_ref = refs[: len(values)], refs[len(values)]
        rest = list(refs[len(values) + 1 : -1])
        before_ref = rest.pop(0) if before is not None else None
        rows_ref = rest.pop(0) if rows is not None else None
        me, group = lax.axis_index(EXPERT), lax.axis_index("dp")

        def step(first, batch):
            here = pl.ds(offset + first, batch)
            if half is None:
                lefts = [ref[here, :] for ref in part_refs]
            else:
                order = [i ^ 1 for i in range(offset // half, (offset + count) // half)]
                lefts = [
                    jnp.concatenate([ref[i * half : (i + 1) * half, :] for i in order])
                    for ref in part_refs
                ]
            lefts = [
                jnp.concatenate([lefts.pop(0) for _ in part], axis=1) for part, _, _ in parts
            ]
            if rows is not None:
                table = rows_ref[here, rows.shape[1] - LANES :].astype(jnp.float32)
                lane = lax.broadcasted_iota(jnp.int32, table.shape, 1)
                mine = (lax.rem(lane, experts) == me) & (lane < 3 * experts)
                scale = jnp.sum(jnp.where(mine, table, 0.0), axis=1, keepdims=True)
            tile = min(2 * TILE, width)
            for i in range(0, width, tile):
                cut = slice(i, i + tile)
                total = 0.0 if before is None else before_ref[here, cut]
                for left, (_, mask, unit) in zip(lefts, parts):
                    start = pl.multiple_of((group ^ mask) * units + unit, LANES)
                    right = down_ref[pl.ds(start, left.shape[1]), cut]
                    total = total + jnp.dot(left, right, preferred_element_type=jnp.float32)
                if rows is not None:
                    total = total.astype(jnp.bfloat16).astype(jnp.float32) * scale
                refs[-1][pl.ds(first, batch), cut] = total.astype(kind)

        row_batches(count, step)

    return pl.pallas_call(
        body,
        out_shape=jax.ShapeDtypeStruct((count, width), kind),
        in_specs=[pl.BlockSpec(memory_space=pltpu.VMEM)] * len(operands),
        out_specs=pl.BlockSpec(memory_space=pltpu.VMEM),
        cost_estimate=pl.CostEstimate(flops=0, bytes_accessed=count * width, transcendentals=0),
        compiler_params=pltpu.CompilerParams(
            vmem_limit_bytes=8 * total_count * width
            + (6 << 20)
            + (0 if rows is None else rows.nbytes)
        ),
        name="contract_hidden",
    )(*operands)


def sum_stage(inputs, plan, shape, dtype):
    def body(*refs):
        sources, targets = refs[: len(inputs)], refs[len(inputs) :]
        for target, blocks in zip(targets, plan):
            for i, block in enumerate(blocks):
                total = 0.0
                for ref in sources:
                    if len(ref.shape) == 2:
                        value = ref[block * shape[0] : (block + 1) * shape[0], :]
                    else:
                        value = ref[block]
                    total = total + value.astype(jnp.float32)
                target[i] = total.astype(target.dtype)

    return pl.pallas_call(
        body,
        out_shape=[
            jax.ShapeDtypeStruct((len(blocks),) + shape, dtype if i else jnp.float32)
            for i, blocks in enumerate(plan)
        ],
        in_specs=[pl.BlockSpec(memory_space=pltpu.VMEM)] * len(inputs),
        out_specs=[pl.BlockSpec(memory_space=pltpu.VMEM)] * len(plan),
        compiler_params=pltpu.CompilerParams(
            vmem_limit_bytes=sum(value.nbytes for value in inputs) * 2 + (6 << 20)
        ),
        name="sum_stage",
    )(*inputs)


def finish(parts, groups, dtype):
    tokens, columns = parts[0][0].shape[1:]

    def body(*refs):
        group = lax.axis_index("dp")
        for i in range(groups):
            mine = [ref[0] for ref, (_, j) in zip(refs, parts) if i == j]
            total = sum(value.astype(jnp.float32) for value in mine)
            start = pl.multiple_of((group ^ i) * columns, LANES)
            refs[-1][:, pl.ds(start, columns)] = total.astype(dtype)

    return pl.pallas_call(
        body,
        out_shape=jax.ShapeDtypeStruct((tokens, groups * columns), dtype),
        in_specs=[pl.BlockSpec(memory_space=pltpu.VMEM)] * len(parts),
        out_specs=pl.BlockSpec(memory_space=pltpu.VMEM),
        compiler_params=pltpu.CompilerParams(vmem_limit_bytes=4 << 20),
        name="finish",
    )(*[value for value, _ in parts])


def local(tokens, expert_ids, gate_probs, w_gate, w_up, w_down):
    token_count, width = tokens.shape
    groups, experts = lax.axis_size("dp"), lax.axis_size(EXPERT)
    wide, high = groups // 2, experts // 4

    block = pack_block(tokens, expert_ids, gate_probs, experts)
    units = w_up.shape[2]
    weights = lax.optimization_barrier((block, w_gate[0], w_up[0], w_down[0]))
    block, gate_weights, up_weights, down_weights = weights
    order = [0] + list(range(high - 1, 0, -1))
    blocks = [swap(block, 0, 4 * i) if i else block for i in order]
    units = w_up.shape[2]
    weights = lax.optimization_barrier((block, w_gate[0], w_up[0], w_down[0]))
    block, gate_weights, up_weights, down_weights = weights
    near = stack_blocks([block] + [swap(block, 0, 4 * i) for i in range(1, high)])
    sets = []
    for part in (blocks[: high // 2], blocks[high // 2 :]):
        if sets:
            part[0], sets[0][0] = lax.optimization_barrier((part[0], sets[0][0]))
        near = stack_blocks(part)
        if wide > 1:
            near = jnp.concatenate([near] + [swap(near, 2 * i, 0) for i in range(1, wide)])
        sets.append([near, swap(near, 0, 2), swap(near, 1, 0), swap(near, 1, 2)])
    pieces = [join_rows(blocks) for blocks in sets]
    rows = jnp.concatenate(pieces + [swap(piece, 0, 1) for piece in pieces])

    eighth = units // 8
    steps = (3 * eighth, 3 * eighth, 2 * eighth) if eighth % LANES == 0 else (units,)
    starts = [sum(steps[:i]) for i in range(len(steps))]
    half = rows.shape[0] // 8 if groups == 2 and rows.shape[0] <= BATCH else None

    def from_group(value, mask):
        value = swap(value, mask, 0)
        if half is not None:
            return value
        value = value.reshape(4, 2, 2, wide, -1, value.shape[1])
        value = jnp.stack([value[:, i ^ (mask & 1)] for i in range(2)], axis=1)
        value = jnp.stack([value[:, :, :, i ^ (mask >> 1)] for i in range(wide)], axis=3)
        return value.reshape(-1, value.shape[-1])

    hidden, others = [], []
    for start, step in zip(starts, steps):
        if hidden:
            rows, hidden[-1] = lax.optimization_barrier((rows, hidden[-1]))
        hidden.append(expand_rows(rows, gate_weights, up_weights, start, step))
        others.append(
            [([from_group(hidden[-1], mask)], mask, start) for mask in range(1, groups)]
        )
    total = contract_hidden([(hidden, 0, 0)], down_weights, units)
    for parts in others[:-1]:
        total = contract_hidden(parts, down_weights, units, total, half=half)
    last = lambda index, kind: contract_hidden(
        others[-1], down_weights, units, total, rows, half, index, kind
    )
    sent, kept = last(1, jnp.bfloat16), last(0, jnp.float32)

    shape = (token_count, w_down.shape[2])
    rest = [(g, h) for g in range(groups) for h in range(0, high, 2)]

    def slot(g, y, h):
        which, place = divmod(order.index(h), high // 2)
        return (((which * 2 + (g & 1)) * 2 + y) * wide + (g >> 1)) * (high // 2) + place

    plan = [[slot(g, y, h + z) for g, h in rest] for y, z in ((0, 0), (1, 1), (0, 1), (1, 0))]
    mine, *away = sum_stage([kept, swap(sent, 0, 1)], plan, shape, jnp.bfloat16)
    inputs = [mine] + [swap(value, 0, mask) for value, mask in zip(away, (6, 4, 2))]
    last = sorted(range(1, len(rest)), key=lambda i: (rest[i][1], rest[i][0]), reverse=True)
    mine, *away = sum_stage(inputs, [[i] for i in [0] + last], shape, jnp.bfloat16)
    parts = [(swap(value, rest[i][0], 4 * rest[i][1]), rest[i][0]) for value, i in zip(away, last)]
    return finish(parts + [(mine, 0)], groups, tokens.dtype)


def solution(mesh):
    groups, experts = mesh.devices.shape
    split = Mesh(mesh.devices.reshape(groups, experts // 2, 2), ("dp", "far", "core"))
    row, expert = P(("dp", "far", "core"), None), P(EXPERT, None, "dp")
    return jax.shard_map(
        local,
        mesh=split,
        in_specs=(row, row, row, expert, expert, expert),
        out_specs=row,
        check_vma=False,
    )
```

```python
import jax
import jax.numpy as jnp
from jax import lax
from jax.experimental import pallas as pl
from jax.experimental.pallas import tpu as pltpu
from jax.sharding import Mesh
from jax.sharding import PartitionSpec as P

TILE = 256
BATCH = 128
LANES = 128
EXPERT = ("far", "core")


def swap(value, group_mask, expert_mask):
    groups, experts = lax.axis_size("dp"), lax.axis_size(EXPERT)
    pairs = [
        (g * experts + e, (g ^ group_mask) * experts + (e ^ expert_mask))
        for g in range(groups)
        for e in range(experts)
    ]
    return lax.ppermute(value, ("dp",) + EXPERT, pairs)


def in_vmem(value):
    return pltpu.with_memory_space_constraint(value, pltpu.VMEM)


def in_hbm(value):
    return pltpu.with_memory_space_constraint(value, pltpu.HBM)


def row_batches(count, step):
    batch = min(BATCH, count)
    if count == batch:
        step(0, batch)
    else:

        @pl.loop(0, count // batch)
        def _(i):
            step(pl.multiple_of(i * batch, batch), batch)


def pack_block(tokens, expert_ids, gate_probs, experts):
    count, width = tokens.shape
    top = expert_ids.shape[1]

    def body(tokens_ref, ids_ref, probs_ref, block_ref):
        block_ref[:, :width] = tokens_ref[...]
        lane = lax.broadcasted_iota(jnp.int32, (count, LANES), 1)
        table = jnp.zeros((count, LANES), jnp.float32)
        for k in range(top):
            hit = ids_ref[:, k : k + 1] == lax.rem(lane, experts)
            table = jnp.where(hit, probs_ref[:, k : k + 1], table)
        packed = jnp.zeros((count, LANES), jnp.float32)
        for i in range(3):
            part = table.astype(jnp.bfloat16).astype(jnp.float32)
            packed = jnp.where(lane // experts == i, part, packed)
            table = table - part
        block_ref[:, width:] = packed.astype(block_ref.dtype)

    return pl.pallas_call(
        body,
        out_shape=jax.ShapeDtypeStruct((count, width + LANES), tokens.dtype),
        in_specs=[pl.BlockSpec(memory_space=pltpu.VMEM)] * 3,
        out_specs=pl.BlockSpec(memory_space=pltpu.VMEM),
        compiler_params=pltpu.CompilerParams(vmem_limit_bytes=1 << 20),
        name="pack_block",
    )(in_hbm(tokens), in_hbm(expert_ids), in_hbm(gate_probs))


def stack_blocks(blocks):
    def body(*refs):
        for i, ref in enumerate(refs[:-1]):
            refs[-1][i] = ref[...]

    return pl.pallas_call(
        body,
        out_shape=jax.ShapeDtypeStruct((len(blocks),) + blocks[0].shape, blocks[0].dtype),
        in_specs=[pl.BlockSpec(memory_space=pltpu.VMEM)] * len(blocks),
        out_specs=pl.BlockSpec(memory_space=pltpu.VMEM),
        cost_estimate=pl.CostEstimate(flops=60 * 10**9, bytes_accessed=0, transcendentals=0),
        compiler_params=pltpu.CompilerParams(vmem_limit_bytes=4 << 20),
        name="stack_blocks",
    )(*blocks)


def join_rows(stacks):
    blocks, tokens, width = stacks[0].shape
    total = len(stacks) * blocks
    batch = max(1, 16 // tokens)

    def body(*refs):
        for i in range(0, total, batch):
            group = [refs[j // blocks][j % blocks] for j in range(i, i + batch)]
            rows = jnp.concatenate([value.astype(jnp.float32) for value in group])
            refs[-1][i * tokens : (i + batch) * tokens, :] = rows.astype(refs[-1].dtype)

    return pl.pallas_call(
        body,
        out_shape=jax.ShapeDtypeStruct((total * tokens, width), stacks[0].dtype),
        in_specs=[pl.BlockSpec(memory_space=pltpu.VMEM)] * len(stacks),
        out_specs=pl.BlockSpec(memory_space=pltpu.VMEM),
        compiler_params=pltpu.CompilerParams(
            vmem_limit_bytes=5 * total * tokens * width + (4 << 20)
        ),
        name="join_rows",
    )(*stacks)


def expand_rows(rows, w_gate, w_up, start, columns):
    count, depth = rows.shape[0], w_gate.shape[0]

    def body(rows_ref, gate_ref, up_ref, hidden_ref):
        def step(first, batch):
            x = rows_ref[pl.ds(first, batch), :depth]
            dot = lambda right: jnp.dot(x, right, preferred_element_type=jnp.float32)
            for i in range(0, columns, TILE):
                tile = min(TILE, columns - i)
                cut = slice(start + i, start + i + tile)
                if 2 * tile <= TILE:
                    both = dot(jnp.concatenate([gate_ref[:, cut], up_ref[:, cut]], axis=1))
                    gate, up = both[:, :tile], both[:, tile:]
                else:
                    gate, up = dot(gate_ref[:, cut]), dot(up_ref[:, cut])
                value = gate / (1.0 + jnp.exp(-gate)) * up
                hidden_ref[pl.ds(first, batch), i : i + tile] = value.astype(hidden_ref.dtype)

        row_batches(count, step)

    return pl.pallas_call(
        body,
        out_shape=jax.ShapeDtypeStruct((count, columns), rows.dtype),
        in_specs=[pl.BlockSpec(memory_space=pltpu.VMEM)] * 3,
        out_specs=pl.BlockSpec(memory_space=pltpu.VMEM),
        cost_estimate=pl.CostEstimate(flops=0, bytes_accessed=count * columns, transcendentals=0),
        compiler_params=pltpu.CompilerParams(vmem_limit_bytes=rows.nbytes + (6 << 20)),
        name="expand_rows",
    )(rows, in_vmem(w_gate), in_vmem(w_up))


def contract_hidden(
    parts, w_down, units, before=None, rows=None, half=None, index=None, kind=jnp.float32
):
    total_count, width = parts[0][0][0].shape[0], w_down.shape[1]
    count = total_count if index is None else total_count // 2
    offset = 0 if index is None else index * count
    experts = lax.axis_size(EXPERT)
    values = [value for part, _, _ in parts for value in part]
    operands = values + [in_vmem(w_down)]
    operands += [value for value in (before, rows) if value is not None]

    def body(*refs):
        part_refs, down_ref = refs[: len(values)], refs[len(values)]
        rest = list(refs[len(values) + 1 : -1])
        before_ref = rest.pop(0) if before is not None else None
        rows_ref = rest.pop(0) if rows is not None else None
        me, group = lax.axis_index(EXPERT), lax.axis_index("dp")

        def step(first, batch):
            here = pl.ds(offset + first, batch)
            if half is None:
                lefts = [ref[here, :] for ref in part_refs]
            else:
                order = [i ^ 1 for i in range(offset // half, (offset + count) // half)]
                lefts = [
                    jnp.concatenate([ref[i * half : (i + 1) * half, :] for i in order])
                    for ref in part_refs
                ]
            lefts = [
                jnp.concatenate([lefts.pop(0) for _ in part], axis=1) for part, _, _ in parts
            ]
            if rows is not None:
                table = rows_ref[here, rows.shape[1] - LANES :].astype(jnp.float32)
                lane = lax.broadcasted_iota(jnp.int32, table.shape, 1)
                mine = (lax.rem(lane, experts) == me) & (lane < 3 * experts)
                scale = jnp.sum(jnp.where(mine, table, 0.0), axis=1, keepdims=True)
            tile = min(2 * TILE, width)
            for i in range(0, width, tile):
                cut = slice(i, i + tile)
                total = 0.0 if before is None else before_ref[here, cut]
                for left, (_, mask, unit) in zip(lefts, parts):
                    start = pl.multiple_of((group ^ mask) * units + unit, LANES)
                    right = down_ref[pl.ds(start, left.shape[1]), cut]
                    total = total + jnp.dot(left, right, preferred_element_type=jnp.float32)
                if rows is not None:
                    total = total.astype(jnp.bfloat16).astype(jnp.float32) * scale
                refs[-1][pl.ds(first, batch), cut] = total.astype(kind)

        row_batches(count, step)

    return pl.pallas_call(
        body,
        out_shape=jax.ShapeDtypeStruct((count, width), kind),
        in_specs=[pl.BlockSpec(memory_space=pltpu.VMEM)] * len(operands),
        out_specs=pl.BlockSpec(memory_space=pltpu.VMEM),
        cost_estimate=pl.CostEstimate(flops=0, bytes_accessed=count * width, transcendentals=0),
        compiler_params=pltpu.CompilerParams(
            vmem_limit_bytes=8 * total_count * width
            + (6 << 20)
            + (0 if rows is None else rows.nbytes)
        ),
        name="contract_hidden",
    )(*operands)


def sum_stage(inputs, plan, shape, dtype):
    def body(*refs):
        sources, targets = refs[: len(inputs)], refs[len(inputs) :]
        for target, blocks in zip(targets, plan):
            for i, block in enumerate(blocks):
                total = 0.0
                for ref in sources:
                    if len(ref.shape) == 2:
                        value = ref[block * shape[0] : (block + 1) * shape[0], :]
                    else:
                        value = ref[block]
                    total = total + value.astype(jnp.float32)
                target[i] = total.astype(target.dtype)

    return pl.pallas_call(
        body,
        out_shape=[
            jax.ShapeDtypeStruct((len(blocks),) + shape, dtype if i else jnp.float32)
            for i, blocks in enumerate(plan)
        ],
        in_specs=[pl.BlockSpec(memory_space=pltpu.VMEM)] * len(inputs),
        out_specs=[pl.BlockSpec(memory_space=pltpu.VMEM)] * len(plan),
        compiler_params=pltpu.CompilerParams(
            vmem_limit_bytes=sum(value.nbytes for value in inputs) * 2 + (6 << 20)
        ),
        name="sum_stage",
    )(*inputs)


def finish(parts, groups, dtype):
    tokens, columns = parts[0][0].shape[1:]

    def body(*refs):
        group = lax.axis_index("dp")
        for i in range(groups):
            mine = [ref[0] for ref, (_, j) in zip(refs, parts) if i == j]
            total = sum(value.astype(jnp.float32) for value in mine)
            start = pl.multiple_of((group ^ i) * columns, LANES)
            refs[-1][:, pl.ds(start, columns)] = total.astype(dtype)

    return pl.pallas_call(
        body,
        out_shape=jax.ShapeDtypeStruct((tokens, groups * columns), dtype),
        in_specs=[pl.BlockSpec(memory_space=pltpu.VMEM)] * len(parts),
        out_specs=pl.BlockSpec(memory_space=pltpu.VMEM),
        compiler_params=pltpu.CompilerParams(vmem_limit_bytes=4 << 20),
        name="finish",
    )(*[value for value, _ in parts])


def local(tokens, expert_ids, gate_probs, w_gate, w_up, w_down):
    token_count, width = tokens.shape
    groups, experts = lax.axis_size("dp"), lax.axis_size(EXPERT)
    wide, high = groups // 2, experts // 4

    block = pack_block(tokens, expert_ids, gate_probs, experts)
    units = w_up.shape[2]
    weights = lax.optimization_barrier((block, w_gate[0], w_up[0], w_down[0]))
    block, gate_weights, up_weights, down_weights = weights
    near = stack_blocks([block] + [swap(block, 0, 4 * i) for i in range(1, high)])
    if wide > 1:
        near = jnp.concatenate([near] + [swap(near, 2 * i, 0) for i in range(1, wide)])
    over_x, over_y = swap(near, 1, 0), swap(near, 0, 2)
    first = join_rows([near, swap(near, 1, 2)])
    pieces = [first, join_rows([over_x]), join_rows([over_y])]
    size = pieces[1].shape[0]
    rows = []
    for first, x, y in (pieces, [swap(piece, 0, 1) for piece in pieces]):
        rows += [first[:size], y, x, first[size:]]
    rows = jnp.concatenate(rows)

    eighth = units // 8
    steps = (3 * eighth, 3 * eighth, eighth, eighth) if eighth % LANES == 0 else (units,)
    starts = [sum(steps[:i]) for i in range(len(steps))]
    half = rows.shape[0] // 4 if groups == 2 and rows.shape[0] <= BATCH else None

    def from_group(value, mask):
        value = swap(value, mask, 0)
        if half is not None:
            return value
        value = value.reshape(2, 2, 2, wide, high * token_count, value.shape[1])
        value = jnp.stack([value[:, i ^ (mask & 1)] for i in range(2)], axis=1)
        value = jnp.stack([value[:, :, :, i ^ (mask >> 1)] for i in range(wide)], axis=3)
        return value.reshape(-1, value.shape[-1])

    hidden, others = [], []
    for start, step in zip(starts, steps):
        if hidden:
            rows, hidden[-1] = lax.optimization_barrier((rows, hidden[-1]))
        hidden.append(expand_rows(rows, gate_weights, up_weights, start, step))
        others.append(
            [([from_group(hidden[-1], mask)], mask, start) for mask in range(1, groups)]
        )
    total = contract_hidden([(hidden, 0, 0)], down_weights, units)
    for parts in others[:-1]:
        total = contract_hidden(parts, down_weights, units, total, half=half)
    last = lambda index, kind: contract_hidden(
        others[-1], down_weights, units, total, rows, half, index, kind
    )
    sent, kept = last(1, jnp.bfloat16), last(0, jnp.float32)

    shape = (token_count, w_down.shape[2])
    rest = [(g, h) for g in range(groups) for h in range(0, high, 2)]
    slot = lambda g, y, h: (((g & 1) * 2 + y) * wide + (g >> 1)) * high + h
    plan = [[slot(g, y, h + z) for g, h in rest] for y, z in ((0, 0), (1, 1), (0, 1), (1, 0))]
    mine, *away = sum_stage([kept, swap(sent, 0, 1)], plan, shape, jnp.bfloat16)
    inputs = [mine] + [swap(value, 0, mask) for value, mask in zip(away, (6, 4, 2))]
    order = sorted(range(1, len(rest)), key=lambda i: (rest[i][1], rest[i][0]), reverse=True)
    mine, *away = sum_stage(inputs, [[i] for i in [0] + order], shape, jnp.bfloat16)
    parts = [
        (swap(value, rest[i][0], 4 * rest[i][1]), rest[i][0]) for value, i in zip(away, order)
    ]
    return finish(parts + [(mine, 0)], groups, tokens.dtype)


def solution(mesh):
    groups, experts = mesh.devices.shape
    split = Mesh(mesh.devices.reshape(groups, experts // 2, 2), ("dp", "far", "core"))
    row, expert = P(("dp", "far", "core"), None), P(EXPERT, None, "dp")
    return jax.shard_map(
        local,
        mesh=split,
        in_specs=(row, row, row, expert, expert, expert),
        out_specs=row,
        check_vma=False,
    )
```

```python
import jax
import jax.numpy as jnp
from jax import lax
from jax.experimental import pallas as pl
from jax.experimental.pallas import tpu as pltpu
from jax.sharding import Mesh
from jax.sharding import PartitionSpec as P

TILE = 256
BATCH = 128
LANES = 128
EXPERT = ("far", "core")


def swap(value, group_mask, expert_mask):
    groups, experts = lax.axis_size("dp"), lax.axis_size(EXPERT)
    pairs = [
        (g * experts + e, (g ^ group_mask) * experts + (e ^ expert_mask))
        for g in range(groups)
        for e in range(experts)
    ]
    return lax.ppermute(value, ("dp",) + EXPERT, pairs)


def in_vmem(value):
    return pltpu.with_memory_space_constraint(value, pltpu.VMEM)


def in_hbm(value):
    return pltpu.with_memory_space_constraint(value, pltpu.HBM)


def row_batches(count, step):
    batch = min(BATCH, count)
    if count == batch:
        step(0, batch)
    else:

        @pl.loop(0, count // batch)
        def _(i):
            step(pl.multiple_of(i * batch, batch), batch)


def pack_block(tokens, expert_ids, gate_probs, experts):
    count, width = tokens.shape
    top = expert_ids.shape[1]

    def body(tokens_ref, ids_ref, probs_ref, block_ref):
        block_ref[:, :width] = tokens_ref[...]
        lane = lax.broadcasted_iota(jnp.int32, (count, LANES), 1)
        table = jnp.zeros((count, LANES), jnp.float32)
        for k in range(top):
            hit = ids_ref[:, k : k + 1] == lax.rem(lane, experts)
            table = jnp.where(hit, probs_ref[:, k : k + 1], table)
        packed = jnp.zeros((count, LANES), jnp.float32)
        for i in range(3):
            part = table.astype(jnp.bfloat16).astype(jnp.float32)
            packed = jnp.where(lane // experts == i, part, packed)
            table = table - part
        block_ref[:, width:] = packed.astype(block_ref.dtype)

    return pl.pallas_call(
        body,
        out_shape=jax.ShapeDtypeStruct((count, width + LANES), tokens.dtype),
        in_specs=[pl.BlockSpec(memory_space=pltpu.VMEM)] * 3,
        out_specs=pl.BlockSpec(memory_space=pltpu.VMEM),
        compiler_params=pltpu.CompilerParams(vmem_limit_bytes=1 << 20),
        name="pack_block",
    )(in_hbm(tokens), in_hbm(expert_ids), in_hbm(gate_probs))


def stack_blocks(blocks):
    def body(*refs):
        for i, ref in enumerate(refs[:-1]):
            refs[-1][i] = ref[...]

    return pl.pallas_call(
        body,
        out_shape=jax.ShapeDtypeStruct((len(blocks),) + blocks[0].shape, blocks[0].dtype),
        in_specs=[pl.BlockSpec(memory_space=pltpu.VMEM)] * len(blocks),
        out_specs=pl.BlockSpec(memory_space=pltpu.VMEM),
        cost_estimate=pl.CostEstimate(flops=60 * 10**9, bytes_accessed=0, transcendentals=0),
        compiler_params=pltpu.CompilerParams(vmem_limit_bytes=4 << 20),
        name="stack_blocks",
    )(*blocks)


def join_rows(stacks):
    blocks, tokens, width = stacks[0].shape
    total = len(stacks) * blocks
    batch = max(1, 16 // tokens)

    def body(*refs):
        for i in range(0, total, batch):
            group = [refs[j // blocks][j % blocks] for j in range(i, i + batch)]
            rows = jnp.concatenate([value.astype(jnp.float32) for value in group])
            refs[-1][i * tokens : (i + batch) * tokens, :] = rows.astype(refs[-1].dtype)

    return pl.pallas_call(
        body,
        out_shape=jax.ShapeDtypeStruct((total * tokens, width), stacks[0].dtype),
        in_specs=[pl.BlockSpec(memory_space=pltpu.VMEM)] * len(stacks),
        out_specs=pl.BlockSpec(memory_space=pltpu.VMEM),
        compiler_params=pltpu.CompilerParams(
            vmem_limit_bytes=5 * total * tokens * width + (4 << 20)
        ),
        name="join_rows",
    )(*stacks)


def expand_rows(rows, w_gate, w_up, start, columns):
    count, depth = rows.shape[0], w_gate.shape[0]

    def body(rows_ref, gate_ref, up_ref, hidden_ref):
        def step(first, batch):
            x = rows_ref[pl.ds(first, batch), :depth]
            dot = lambda right: jnp.dot(x, right, preferred_element_type=jnp.float32)
            for i in range(0, columns, TILE):
                tile = min(TILE, columns - i)
                cut = slice(start + i, start + i + tile)
                if 2 * tile <= TILE:
                    both = dot(jnp.concatenate([gate_ref[:, cut], up_ref[:, cut]], axis=1))
                    gate, up = both[:, :tile], both[:, tile:]
                else:
                    gate, up = dot(gate_ref[:, cut]), dot(up_ref[:, cut])
                value = gate / (1.0 + jnp.exp(-gate)) * up
                hidden_ref[pl.ds(first, batch), i : i + tile] = value.astype(hidden_ref.dtype)

        row_batches(count, step)

    return pl.pallas_call(
        body,
        out_shape=jax.ShapeDtypeStruct((count, columns), rows.dtype),
        in_specs=[pl.BlockSpec(memory_space=pltpu.VMEM)] * 3,
        out_specs=pl.BlockSpec(memory_space=pltpu.VMEM),
        cost_estimate=pl.CostEstimate(flops=0, bytes_accessed=count * columns, transcendentals=0),
        compiler_params=pltpu.CompilerParams(vmem_limit_bytes=rows.nbytes + (6 << 20)),
        name="expand_rows",
    )(rows, in_vmem(w_gate), in_vmem(w_up))


def contract_hidden(
    parts, w_down, units, before=None, rows=None, half=None, index=None, kind=jnp.float32
):
    total_count, width = parts[0][0][0].shape[0], w_down.shape[1]
    count = total_count if index is None else total_count // 2
    offset = 0 if index is None else index * count
    experts = lax.axis_size(EXPERT)
    values = [value for part, _, _ in parts for value in part]
    operands = values + [in_vmem(w_down)]
    operands += [value for value in (before, rows) if value is not None]

    def body(*refs):
        part_refs, down_ref = refs[: len(values)], refs[len(values)]
        rest = list(refs[len(values) + 1 : -1])
        before_ref = rest.pop(0) if before is not None else None
        rows_ref = rest.pop(0) if rows is not None else None
        me, group = lax.axis_index(EXPERT), lax.axis_index("dp")

        def step(first, batch):
            here = pl.ds(offset + first, batch)
            if half is None:
                lefts = [ref[here, :] for ref in part_refs]
            else:
                order = [i ^ 1 for i in range(offset // half, (offset + count) // half)]
                lefts = [
                    jnp.concatenate([ref[i * half : (i + 1) * half, :] for i in order])
                    for ref in part_refs
                ]
            lefts = [
                jnp.concatenate([lefts.pop(0) for _ in part], axis=1) for part, _, _ in parts
            ]
            if rows is not None:
                table = rows_ref[here, rows.shape[1] - LANES :].astype(jnp.float32)
                lane = lax.broadcasted_iota(jnp.int32, table.shape, 1)
                mine = (lax.rem(lane, experts) == me) & (lane < 3 * experts)
                scale = jnp.sum(jnp.where(mine, table, 0.0), axis=1, keepdims=True)
            tile = min(2 * TILE, width)
            for i in range(0, width, tile):
                cut = slice(i, i + tile)
                total = 0.0 if before is None else before_ref[here, cut]
                for left, (_, mask, unit) in zip(lefts, parts):
                    start = pl.multiple_of((group ^ mask) * units + unit, LANES)
                    right = down_ref[pl.ds(start, left.shape[1]), cut]
                    total = total + jnp.dot(left, right, preferred_element_type=jnp.float32)
                if rows is not None:
                    total = total.astype(jnp.bfloat16).astype(jnp.float32) * scale
                refs[-1][pl.ds(first, batch), cut] = total.astype(kind)

        row_batches(count, step)

    return pl.pallas_call(
        body,
        out_shape=jax.ShapeDtypeStruct((count, width), kind),
        in_specs=[pl.BlockSpec(memory_space=pltpu.VMEM)] * len(operands),
        out_specs=pl.BlockSpec(memory_space=pltpu.VMEM),
        cost_estimate=pl.CostEstimate(flops=0, bytes_accessed=count * width, transcendentals=0),
        compiler_params=pltpu.CompilerParams(
            vmem_limit_bytes=8 * total_count * width
            + (6 << 20)
            + (0 if rows is None else rows.nbytes)
        ),
        name="contract_hidden",
    )(*operands)


def sum_stage(inputs, plan, shape, dtype):
    def body(*refs):
        sources, targets = refs[: len(inputs)], refs[len(inputs) :]
        for target, blocks in zip(targets, plan):
            for i, block in enumerate(blocks):
                total = 0.0
                for ref in sources:
                    if len(ref.shape) == 2:
                        value = ref[block * shape[0] : (block + 1) * shape[0], :]
                    else:
                        value = ref[block]
                    total = total + value.astype(jnp.float32)
                target[i] = total.astype(target.dtype)

    return pl.pallas_call(
        body,
        out_shape=[
            jax.ShapeDtypeStruct((len(blocks),) + shape, dtype if i else jnp.float32)
            for i, blocks in enumerate(plan)
        ],
        in_specs=[pl.BlockSpec(memory_space=pltpu.VMEM)] * len(inputs),
        out_specs=[pl.BlockSpec(memory_space=pltpu.VMEM)] * len(plan),
        compiler_params=pltpu.CompilerParams(
            vmem_limit_bytes=sum(value.nbytes for value in inputs) * 2 + (6 << 20)
        ),
        name="sum_stage",
    )(*inputs)


def finish(parts, groups, dtype):
    tokens, columns = parts[0][0].shape[1:]

    def body(*refs):
        group = lax.axis_index("dp")
        for i in range(groups):
            mine = [ref[0] for ref, (_, j) in zip(refs, parts) if i == j]
            total = sum(value.astype(jnp.float32) for value in mine)
            start = pl.multiple_of((group ^ i) * columns, LANES)
            refs[-1][:, pl.ds(start, columns)] = total.astype(dtype)

    return pl.pallas_call(
        body,
        out_shape=jax.ShapeDtypeStruct((tokens, groups * columns), dtype),
        in_specs=[pl.BlockSpec(memory_space=pltpu.VMEM)] * len(parts),
        out_specs=pl.BlockSpec(memory_space=pltpu.VMEM),
        compiler_params=pltpu.CompilerParams(vmem_limit_bytes=4 << 20),
        name="finish",
    )(*[value for value, _ in parts])


def local(tokens, expert_ids, gate_probs, w_gate, w_up, w_down):
    token_count, width = tokens.shape
    groups, experts = lax.axis_size("dp"), lax.axis_size(EXPERT)
    wide, high = groups // 2, experts // 4

    block = pack_block(tokens, expert_ids, gate_probs, experts)
    units = w_up.shape[2]
    weights = lax.optimization_barrier((block, w_gate[0], w_up[0], w_down[0]))
    block, gate_weights, up_weights, down_weights = weights
    near = stack_blocks([block] + [swap(block, 0, 4 * i) for i in range(1, high)])
    if wide > 1:
        near = jnp.concatenate([near] + [swap(near, 2 * i, 0) for i in range(1, wide)])
    over_x, over_y = swap(near, 1, 1), swap(near, 0, 3)
    first = join_rows([near, swap(near, 1, 3)])
    pieces = [first, join_rows([over_x]), join_rows([over_y])]
    size = pieces[1].shape[0]
    here, there = pieces, [swap(piece, 0, 1) for piece in pieces]
    rows = []
    for near, (first, x, y) in ((here[0], there), (there[0], here)):
        rows += [near[:size], y, x, first[size:]]
    rows = jnp.concatenate(rows)

    eighth = units // 8
    steps = (3 * eighth, 3 * eighth, 2 * eighth) if eighth % LANES == 0 else (units,)
    starts = [sum(steps[:i]) for i in range(len(steps))]
    half = rows.shape[0] // 4 if groups == 2 and rows.shape[0] <= BATCH else None

    def from_group(value, mask):
        value = swap(value, mask, 0)
        if half is not None:
            return value
        value = value.reshape(2, 2, 2, wide, high * token_count, value.shape[1])
        value = jnp.stack([value[:, i ^ (mask & 1)] for i in range(2)], axis=1)
        value = jnp.stack([value[:, :, :, i ^ (mask >> 1)] for i in range(wide)], axis=3)
        return value.reshape(-1, value.shape[-1])

    hidden, others = [], []
    for start, step in zip(starts, steps):
        if hidden:
            rows, hidden[-1] = lax.optimization_barrier((rows, hidden[-1]))
        hidden.append(expand_rows(rows, gate_weights, up_weights, start, step))
        others.append(
            [([from_group(hidden[-1], mask)], mask, start) for mask in range(1, groups)]
        )
    total = contract_hidden([(hidden, 0, 0)], down_weights, units)
    for parts in others[:-1]:
        total = contract_hidden(parts, down_weights, units, total, half=half)
    last = lambda index, kind: contract_hidden(
        others[-1], down_weights, units, total, rows, half, index, kind
    )
    sent, kept = last(1, jnp.bfloat16), last(0, jnp.float32)

    shape = (token_count, w_down.shape[2])
    rest = [(g, h) for g in range(groups) for h in range(0, high, 2)]
    slot = lambda g, y, h: (((g & 1) * 2 + y) * wide + (g >> 1)) * high + h
    plan = [[slot(g, y, h + z) for g, h in rest] for y, z in ((0, 0), (1, 1), (0, 1), (1, 0))]
    mine, *away = sum_stage([kept, swap(sent, 0, 1)], plan, shape, jnp.bfloat16)
    inputs = [mine] + [swap(value, 0, mask) for value, mask in zip(away, (6, 4, 2))]
    order = sorted(range(1, len(rest)), key=lambda i: (rest[i][1], rest[i][0]), reverse=True)
    mine, *away = sum_stage(inputs, [[i] for i in [0] + order], shape, jnp.bfloat16)
    parts = [
        (swap(value, rest[i][0], 4 * rest[i][1]), rest[i][0]) for value, i in zip(away, order)
    ]
    return finish(parts + [(mine, 0)], groups, tokens.dtype)


def solution(mesh):
    groups, experts = mesh.devices.shape
    split = Mesh(mesh.devices.reshape(groups, experts // 2, 2), ("dp", "far", "core"))
    row, expert = P(("dp", "far", "core"), None), P(EXPERT, None, "dp")
    return jax.shard_map(
        local,
        mesh=split,
        in_specs=(row, row, row, expert, expert, expert),
        out_specs=row,
        check_vma=False,
    )
```

```python
import jax
import jax.numpy as jnp
from jax import lax
from jax.experimental import pallas as pl
from jax.experimental.pallas import tpu as pltpu
from jax.sharding import Mesh
from jax.sharding import PartitionSpec as P

TILE = 256
BATCH = 128
LANES = 128
EXPERT = ("far", "core")


def swap(value, group_mask, expert_mask):
    groups, experts = lax.axis_size("dp"), lax.axis_size(EXPERT)
    pairs = [
        (g * experts + e, (g ^ group_mask) * experts + (e ^ expert_mask))
        for g in range(groups)
        for e in range(experts)
    ]
    return lax.ppermute(value, ("dp",) + EXPERT, pairs)


def in_vmem(value):
    return pltpu.with_memory_space_constraint(value, pltpu.VMEM)


def in_hbm(value):
    return pltpu.with_memory_space_constraint(value, pltpu.HBM)


def row_batches(count, step):
    batch = min(BATCH, count)
    if count == batch:
        step(0, batch)
    else:

        @pl.loop(0, count // batch)
        def _(i):
            step(pl.multiple_of(i * batch, batch), batch)


def pack_block(tokens, expert_ids, gate_probs, experts):
    count, width = tokens.shape
    top = expert_ids.shape[1]

    def body(tokens_ref, ids_ref, probs_ref, block_ref):
        block_ref[:, :width] = tokens_ref[...]
        lane = lax.broadcasted_iota(jnp.int32, (count, LANES), 1)
        table = jnp.zeros((count, LANES), jnp.float32)
        for k in range(top):
            hit = ids_ref[:, k : k + 1] == lax.rem(lane, experts)
            table = jnp.where(hit, probs_ref[:, k : k + 1], table)
        packed = jnp.zeros((count, LANES), jnp.float32)
        for i in range(3):
            part = table.astype(jnp.bfloat16).astype(jnp.float32)
            packed = jnp.where(lane // experts == i, part, packed)
            table = table - part
        block_ref[:, width:] = packed.astype(block_ref.dtype)

    return pl.pallas_call(
        body,
        out_shape=jax.ShapeDtypeStruct((count, width + LANES), tokens.dtype),
        in_specs=[pl.BlockSpec(memory_space=pltpu.VMEM)] * 3,
        out_specs=pl.BlockSpec(memory_space=pltpu.VMEM),
        compiler_params=pltpu.CompilerParams(vmem_limit_bytes=1 << 20),
        name="pack_block",
    )(in_hbm(tokens), in_hbm(expert_ids), in_hbm(gate_probs))


def stack_blocks(blocks, places):
    def body(*refs):
        for i, ref in zip(places, refs):
            refs[-1][i] = ref[...]

    return pl.pallas_call(
        body,
        out_shape=jax.ShapeDtypeStruct((len(blocks),) + blocks[0].shape, blocks[0].dtype),
        in_specs=[pl.BlockSpec(memory_space=pltpu.VMEM)] * len(blocks),
        out_specs=pl.BlockSpec(memory_space=pltpu.VMEM),
        cost_estimate=pl.CostEstimate(flops=60 * 10**9, bytes_accessed=0, transcendentals=0),
        compiler_params=pltpu.CompilerParams(vmem_limit_bytes=4 << 20),
        name="stack_blocks",
    )(*blocks)


def join_rows(stacks):
    blocks, tokens, width = stacks[0].shape
    total = len(stacks) * blocks
    batch = max(1, 16 // tokens)

    def body(*refs):
        for i in range(0, total, batch):
            group = [refs[j // blocks][j % blocks] for j in range(i, i + batch)]
            rows = jnp.concatenate([value.astype(jnp.float32) for value in group])
            refs[-1][i * tokens : (i + batch) * tokens, :] = rows.astype(refs[-1].dtype)

    return pl.pallas_call(
        body,
        out_shape=jax.ShapeDtypeStruct((total * tokens, width), stacks[0].dtype),
        in_specs=[pl.BlockSpec(memory_space=pltpu.VMEM)] * len(stacks),
        out_specs=pl.BlockSpec(memory_space=pltpu.VMEM),
        compiler_params=pltpu.CompilerParams(
            vmem_limit_bytes=5 * total * tokens * width + (4 << 20)
        ),
        name="join_rows",
    )(*stacks)


def expand_rows(rows, w_gate, w_up, start, columns):
    count, depth = rows.shape[0], w_gate.shape[0]

    def body(rows_ref, gate_ref, up_ref, hidden_ref):
        def step(first, batch):
            x = rows_ref[pl.ds(first, batch), :depth]
            dot = lambda right: jnp.dot(x, right, preferred_element_type=jnp.float32)
            for i in range(0, columns, TILE):
                tile = min(TILE, columns - i)
                cut = slice(start + i, start + i + tile)
                if 2 * tile <= TILE:
                    both = dot(jnp.concatenate([gate_ref[:, cut], up_ref[:, cut]], axis=1))
                    gate, up = both[:, :tile], both[:, tile:]
                else:
                    gate, up = dot(gate_ref[:, cut]), dot(up_ref[:, cut])
                value = gate / (1.0 + jnp.exp(-gate)) * up
                hidden_ref[pl.ds(first, batch), i : i + tile] = value.astype(hidden_ref.dtype)

        row_batches(count, step)

    return pl.pallas_call(
        body,
        out_shape=jax.ShapeDtypeStruct((count, columns), rows.dtype),
        in_specs=[pl.BlockSpec(memory_space=pltpu.VMEM)] * 3,
        out_specs=pl.BlockSpec(memory_space=pltpu.VMEM),
        cost_estimate=pl.CostEstimate(flops=0, bytes_accessed=count * columns, transcendentals=0),
        compiler_params=pltpu.CompilerParams(vmem_limit_bytes=rows.nbytes + (6 << 20)),
        name="expand_rows",
    )(rows, in_vmem(w_gate), in_vmem(w_up))


def contract_hidden(
    parts, w_down, units, before=None, rows=None, half=None, index=None, kind=jnp.float32
):
    total_count, width = parts[0][0][0].shape[0], w_down.shape[1]
    count = total_count if index is None else total_count // 2
    offset = 0 if index is None else index * count
    experts = lax.axis_size(EXPERT)
    values = [value for part, _, _ in parts for value in part]
    operands = values + [in_vmem(w_down)]
    operands += [value for value in (before, rows) if value is not None]

    def body(*refs):
        part_refs, down_ref = refs[: len(values)], refs[len(values)]
        rest = list(refs[len(values) + 1 : -1])
        before_ref = rest.pop(0) if before is not None else None
        rows_ref = rest.pop(0) if rows is not None else None
        me, group = lax.axis_index(EXPERT), lax.axis_index("dp")

        def step(first, batch):
            here = pl.ds(offset + first, batch)
            if half is None:
                lefts = [ref[here, :] for ref in part_refs]
            else:
                order = [i ^ 1 for i in range(offset // half, (offset + count) // half)]
                lefts = [
                    jnp.concatenate([ref[i * half : (i + 1) * half, :] for i in order])
                    for ref in part_refs
                ]
            lefts = [
                jnp.concatenate([lefts.pop(0) for _ in part], axis=1) for part, _, _ in parts
            ]
            if rows is not None:
                table = rows_ref[here, rows.shape[1] - LANES :].astype(jnp.float32)
                lane = lax.broadcasted_iota(jnp.int32, table.shape, 1)
                mine = (lax.rem(lane, experts) == me) & (lane < 3 * experts)
                scale = jnp.sum(jnp.where(mine, table, 0.0), axis=1, keepdims=True)
            tile = min(2 * TILE, width)
            for i in range(0, width, tile):
                cut = slice(i, i + tile)
                total = 0.0 if before is None else before_ref[here, cut]
                for left, (_, mask, unit) in zip(lefts, parts):
                    start = pl.multiple_of((group ^ mask) * units + unit, LANES)
                    right = down_ref[pl.ds(start, left.shape[1]), cut]
                    total = total + jnp.dot(left, right, preferred_element_type=jnp.float32)
                if rows is not None:
                    total = total.astype(jnp.bfloat16).astype(jnp.float32) * scale
                refs[-1][pl.ds(first, batch), cut] = total.astype(kind)

        row_batches(count, step)

    return pl.pallas_call(
        body,
        out_shape=jax.ShapeDtypeStruct((count, width), kind),
        in_specs=[pl.BlockSpec(memory_space=pltpu.VMEM)] * len(operands),
        out_specs=pl.BlockSpec(memory_space=pltpu.VMEM),
        cost_estimate=pl.CostEstimate(flops=0, bytes_accessed=count * width, transcendentals=0),
        compiler_params=pltpu.CompilerParams(
            vmem_limit_bytes=8 * total_count * width
            + (6 << 20)
            + (0 if rows is None else rows.nbytes)
        ),
        name="contract_hidden",
    )(*operands)


def sum_stage(inputs, plan, shape, dtype):
    def body(*refs):
        sources, targets = refs[: len(inputs)], refs[len(inputs) :]
        for target, blocks in zip(targets, plan):
            for i, block in enumerate(blocks):
                total = 0.0
                for ref in sources:
                    if len(ref.shape) == 2:
                        value = ref[block * shape[0] : (block + 1) * shape[0], :]
                    else:
                        value = ref[block]
                    total = total + value.astype(jnp.float32)
                target[i] = total.astype(target.dtype)

    return pl.pallas_call(
        body,
        out_shape=[
            jax.ShapeDtypeStruct((len(blocks),) + shape, dtype if i else jnp.float32)
            for i, blocks in enumerate(plan)
        ],
        in_specs=[pl.BlockSpec(memory_space=pltpu.VMEM)] * len(inputs),
        out_specs=[pl.BlockSpec(memory_space=pltpu.VMEM)] * len(plan),
        compiler_params=pltpu.CompilerParams(
            vmem_limit_bytes=sum(value.nbytes for value in inputs) * 2 + (6 << 20)
        ),
        name="sum_stage",
    )(*inputs)


def finish(parts, groups, dtype):
    tokens, columns = parts[0][0].shape[1:]

    def body(*refs):
        group = lax.axis_index("dp")
        for i in range(groups):
            mine = [ref[0] for ref, (_, j) in zip(refs, parts) if i == j]
            total = sum(value.astype(jnp.float32) for value in mine)
            start = pl.multiple_of((group ^ i) * columns, LANES)
            refs[-1][:, pl.ds(start, columns)] = total.astype(dtype)

    return pl.pallas_call(
        body,
        out_shape=jax.ShapeDtypeStruct((tokens, groups * columns), dtype),
        in_specs=[pl.BlockSpec(memory_space=pltpu.VMEM)] * len(parts),
        out_specs=pl.BlockSpec(memory_space=pltpu.VMEM),
        compiler_params=pltpu.CompilerParams(vmem_limit_bytes=4 << 20),
        name="finish",
    )(*[value for value, _ in parts])


def local(tokens, expert_ids, gate_probs, w_gate, w_up, w_down):
    token_count, width = tokens.shape
    groups, experts = lax.axis_size("dp"), lax.axis_size(EXPERT)
    wide, high = groups // 2, experts // 4

    block = pack_block(tokens, expert_ids, gate_probs, experts)
    units = w_up.shape[2]
    weights = lax.optimization_barrier((block, w_gate[0], w_up[0], w_down[0]))
    block, gate_weights, up_weights, down_weights = weights
    places = [0] + [i for i in range(1, high) if i != 2] + [2]
    near = stack_blocks([block] + [swap(block, 0, 4 * i) for i in places[1:]], places)
    if wide > 1:
        near = jnp.concatenate([near] + [swap(near, 2 * i, 0) for i in range(1, wide)])
    over_x, over_y = swap(near, 1, 0), swap(near, 0, 2)
    first = join_rows([near, swap(near, 1, 2)])
    pieces = [first, join_rows([over_x]), join_rows([over_y])]
    size = pieces[1].shape[0]
    rows = []
    for first, x, y in (pieces, [swap(piece, 0, 1) for piece in pieces]):
        rows += [first[:size], y, x, first[size:]]
    rows = jnp.concatenate(rows)

    eighth = units // 8
    steps = (3 * eighth, 3 * eighth, 2 * eighth) if eighth % LANES == 0 else (units,)
    starts = [sum(steps[:i]) for i in range(len(steps))]
    half = rows.shape[0] // 4 if groups == 2 and rows.shape[0] <= BATCH else None

    def from_group(value, mask):
        value = swap(value, mask, 0)
        if half is not None:
            return value
        value = value.reshape(2, 2, 2, wide, high * token_count, value.shape[1])
        value = jnp.stack([value[:, i ^ (mask & 1)] for i in range(2)], axis=1)
        value = jnp.stack([value[:, :, :, i ^ (mask >> 1)] for i in range(wide)], axis=3)
        return value.reshape(-1, value.shape[-1])

    hidden, others = [], []
    for start, step in zip(starts, steps):
        if hidden:
            rows, hidden[-1] = lax.optimization_barrier((rows, hidden[-1]))
        hidden.append(expand_rows(rows, gate_weights, up_weights, start, step))
        others.append(
            [([from_group(hidden[-1], mask)], mask, start) for mask in range(1, groups)]
        )
    total = contract_hidden([(hidden, 0, 0)], down_weights, units)
    for parts in others[:-1]:
        total = contract_hidden(parts, down_weights, units, total, half=half)
    last = lambda index, kind: contract_hidden(
        others[-1], down_weights, units, total, rows, half, index, kind
    )
    sent, kept = last(1, jnp.bfloat16), last(0, jnp.float32)

    shape = (token_count, w_down.shape[2])
    rest = [(g, h) for g in range(groups) for h in range(0, high, 2)]
    slot = lambda g, y, h: (((g & 1) * 2 + y) * wide + (g >> 1)) * high + h
    plan = [[slot(g, y, h + z) for g, h in rest] for y, z in ((0, 0), (1, 1), (0, 1), (1, 0))]
    mine, *away = sum_stage([kept, swap(sent, 0, 1)], plan, shape, jnp.bfloat16)
    inputs = [mine] + [swap(value, 0, mask) for value, mask in zip(away, (6, 4, 2))]
    order = sorted(range(1, len(rest)), key=lambda i: (rest[i][1], rest[i][0]), reverse=True)
    mine, *away = sum_stage(inputs, [[i] for i in [0] + order], shape, jnp.bfloat16)
    parts = [
        (swap(value, rest[i][0], 4 * rest[i][1]), rest[i][0]) for value, i in zip(away, order)
    ]
    return finish(parts + [(mine, 0)], groups, tokens.dtype)


def solution(mesh):
    groups, experts = mesh.devices.shape
    split = Mesh(mesh.devices.reshape(groups, experts // 2, 2), ("dp", "far", "core"))
    row, expert = P(("dp", "far", "core"), None), P(EXPERT, None, "dp")
    return jax.shard_map(
        local,
        mesh=split,
        in_specs=(row, row, row, expert, expert, expert),
        out_specs=row,
        check_vma=False,
    )
```
